128 devices in a mesh: blocks: 32 (over z, x, core), sub: 4 (over y).
Axes of the slice: x: 4, y: 4, z: 4, core: 2. Of those that a mesh axis runs over, the one named last changes fastest.
Arguments:
- features: bfloat16 [512, 16, 16, 512], P(('blocks', 'sub')), may hold values from -6 to 6
- coords: int32 [512, 3], P(('blocks', 'sub')), may hold values from -1 to 255, as said below
- neighbours: int32 [512, 6], P(('blocks', 'sub')), may hold values from -1 to 511, as said below
- fine_weight: bfloat16 [3, 3, 3072], replicated, may hold values from -0.21875 to 0.21875
- coarse_weight: bfloat16 [3, 3, 6144], replicated, may hold values from -0.21875 to 0.21875
- cotangent: bfloat16 [128, 16, 16, 1024], P(('blocks', 'sub')), may hold values from -0.01953125 to 0.01953125
Outputs:
- coarse_out: bfloat16 [128, 16, 16, 1024], P(('blocks', 'sub'))
- fine_grad: float32 [3, 3, 3072], replicated
- coarse_grad: float32 [3, 3, 6144], replicated
- cell_grad: float32 [512, 16, 16, 512], P(('blocks', 'sub'))
The draws below stay inside these ranges and needn't reach their ends.
Inputs may be any that keep to these rules, and one draw needn't show every extreme that they name: `coords`: device d (index blocks * 4 + sub, slots d * 4 on) holds 2 to 4 occupied blocks in its first slots, in Morton order, all with x from 2 * d to 2 * d + 1 and y, z in 0..1; among them are the blocks (2 * d, 0, 0) and (2 * d + 1, 0, 0); its other slots hold -1; the last device and some other holds 4, and the last device holds the blocks at x = 255, y = 1. `neighbours`: column f names the slot of the occupied block across face f (order -x, +x, -y, +y, -z, +z) of the slot's block, -1 for none and for empty slots.
All inputs are finite; a program needn't handle non-finite values.
Results may differ from the reference program's by a relative error of at most 0.015.
Values may be sent and summed in bfloat16 or wider, within the bound.
A program may use at most 256 MiB of HBM per device.

```python
import jax
import jax.numpy as jnp
from jax import lax

BE = 16
C1 = 32
C2 = 64
PAR = 1
NB = 512
NCB = 128
N_BLOCKS = 32
N_SUB = 4


def layout_tables(key):
    positions = 8 * PAR
    slot_count = 4 * PAR
    devices = N_BLOCKS * N_SUB
    count_key, order_key, fullest_key = jax.random.split(key, 3)
    counts = jax.random.randint(count_key, (devices,), 2, slot_count + 1)
    fullest = jax.random.randint(fullest_key, (), 0, devices)
    device_ids = jnp.arange(devices)
    counts = jnp.where((device_ids == fullest) | (device_ids == devices - 1), slot_count, counts)
    spots = jnp.arange(positions)[None, :]
    scores = jax.random.randint(order_key, (devices, positions), 0, 1 << 20) * positions + spots
    scores = jnp.where(spots == 0, -4, scores)
    scores = jnp.where(spots == positions - 4, -3, scores)
    last_row = device_ids[:, None] == devices - 1
    scores = jnp.where(last_row & (spots == positions - 1), -2, scores)
    scores = jnp.where(last_row & (spots == positions - 2), -1, scores)
    ranks = jnp.argsort(jnp.argsort(scores, axis=1), axis=1)
    listed = jnp.sort(jnp.where(ranks < counts[:, None], spots, positions), axis=1)[:, :slot_count]
    valid = listed < positions
    owner = device_ids[:, None]
    coord_x = 2 * (owner * PAR + listed // 8) + listed % 8 // 4
    coord_y = listed % 4 // 2
    coord_z = listed % 2
    table = jnp.stack([coord_x, coord_y, coord_z], axis=-1)
    table = jnp.where(valid[:, :, None], table, -1)
    return table.reshape(devices * slot_count, 3).astype(jnp.int32)


def draw_coords(key, part):
    table = layout_tables(key)
    return table


def draw_neighbours(key, part):
    table = layout_tables(key)
    total = table.shape[0]
    length_x = 2 * PAR * N_BLOCKS * N_SUB
    valid = table[:, 0] >= 0
    labels = jnp.arange(total, dtype=jnp.int32)
    placing = jnp.where(valid, table[:, 0], length_x)
    lookup = jnp.full((length_x, 2, 2), -1, jnp.int32)
    lookup = lookup.at[placing, jnp.clip(table[:, 1], 0, 1), jnp.clip(table[:, 2], 0, 1)].set(labels, mode='drop')
    offsets = [(-1, 0, 0), (1, 0, 0), (0, -1, 0), (0, 1, 0), (0, 0, -1), (0, 0, 1)]
    columns = []
    for step_x, step_y, step_z in offsets:
        near_x = table[:, 0] + step_x
        near_y = table[:, 1] + step_y
        near_z = table[:, 2] + step_z
        inside = valid & (near_x >= 0) & (near_x < length_x) & (near_y >= 0) & (near_y < 2) & (near_z >= 0) & (near_z < 2)
        found = lookup[jnp.clip(near_x, 0, length_x - 1), jnp.clip(near_y, 0, 1), jnp.clip(near_z, 0, 1)]
        columns.append(jnp.where(inside, found, -1))
    return jnp.stack(columns, axis=1).astype(jnp.int32)


def shard_levels(own_key, dims, shards, low, high):
    factor_of, own = 1.0, jax.random.fold_in(own_key, 6)
    for axis_at, shards_of in shards:
        steps = jnp.exp(jax.random.uniform(jax.random.fold_in(own, axis_at), (shards_of,), jnp.float32, low / len(shards), high / len(shards)))
        factor_of = factor_of * jnp.repeat(steps, dims[axis_at] // shards_of).reshape([-1 if axis == axis_at else 1 for axis in range(len(dims))])
    return factor_of


def normal_values(rng, shape, scale, limit, cuts=(), held_as=jnp.bfloat16):
    result = scale * jax.random.normal(rng, shape, jnp.float32)
    if cuts:
        result = result * shard_levels(rng, shape, cuts, -0.22, 0.18)
    return jnp.clip(result, -limit, limit).astype(held_as)


def setup_inputs(seed: int = 0) -> dict:
    arg_keys = jax.random.split(jax.random.key(seed), 7)
    features = normal_values(arg_keys[0], (NB, BE, BE, BE * C1), 1.0, 6.0, ((0, 128),))
    coords = draw_coords(jax.random.fold_in(arg_keys[6], 71), 0)
    neighbours = draw_neighbours(jax.random.fold_in(arg_keys[6], 71), 0)
    fine_weight = normal_values(arg_keys[3], (3, 3, 3 * C1 * C1), (27 * C1) ** -0.5, 0.21875)
    coarse_weight = normal_values(arg_keys[4], (3, 3, 3 * C1 * C2), (27 * C1) ** -0.5, 0.21875)
    cotangent = normal_values(arg_keys[5], (NCB, BE, BE, BE * C2), (1.0 / (NCB * BE ** 3) ** 0.5), 0.01953125, ((0, 128),))
    return dict(features=features, coords=coords, neighbours=neighbours, fine_weight=fine_weight, coarse_weight=coarse_weight, cotangent=cotangent)


def convolve(padded, kernel):
    return lax.conv_general_dilated(padded, kernel, (1, 1, 1), 'VALID', dimension_numbers=('NDHWC', 'DHWIO', 'NDHWC'), precision=lax.Precision.HIGHEST)

def reference(features, coords, neighbours, fine_weight, coarse_weight, cotangent):
    half_edge = BE // 2
    occupied = coords[:, 0] >= 0
    live = occupied.astype(jnp.float32)[:, None, None, None, None]
    cells = features.astype(jnp.float32).reshape(NB, BE, BE, BE, C1) * live

    def across(column, slabs):
        target = neighbours[:, column]
        chosen = slabs[jnp.clip(target, 0, NB - 1)]
        return chosen * (target >= 0).astype(jnp.float32)[:, None, None, None]
    padded = jnp.pad(cells, ((0, 0), (1, 1), (1, 1), (1, 1), (0, 0)))
    padded = padded.at[:, 0, 1:-1, 1:-1].set(across(0, cells[:, BE - 1]))
    padded = padded.at[:, BE + 1, 1:-1, 1:-1].set(across(1, cells[:, 0]))
    padded = padded.at[:, 1:-1, 0, 1:-1].set(across(2, cells[:, :, BE - 1]))
    padded = padded.at[:, 1:-1, BE + 1, 1:-1].set(across(3, cells[:, :, 0]))
    padded = padded.at[:, 1:-1, 1:-1, 0].set(across(4, cells[:, :, :, BE - 1]))
    padded = padded.at[:, 1:-1, 1:-1, BE + 1].set(across(5, cells[:, :, :, 0]))
    fine_kernel = fine_weight.astype(jnp.float32).reshape(3, 3, 3, C1, C1)
    act, fine_pull = jax.vjp(lambda kernel: convolve(padded, kernel), fine_kernel)
    sigma = jax.nn.sigmoid(act)
    hidden = (live * (cells + act * sigma)).astype(jnp.bfloat16)
    pooled = hidden.astype(jnp.float32).reshape(NB, half_edge, 2, half_edge, 2, half_edge, 2, C1).mean(axis=(2, 4, 6))
    parent = jnp.where(occupied, coords[:, 0] // 2, NCB).astype(jnp.int32)
    octant_x = jnp.where(occupied, coords[:, 0] % 2, 0).astype(jnp.int32)
    octant_y = jnp.clip(coords[:, 1], 0, 1).astype(jnp.int32)
    octant_z = jnp.clip(coords[:, 2], 0, 1).astype(jnp.int32)
    layout = jnp.zeros((NCB, 2, 2, 2, half_edge, half_edge, half_edge, C1), jnp.float32)
    layout = layout.at[parent, octant_x, octant_y, octant_z].add(pooled, mode='drop')
    chain = layout.transpose(0, 1, 4, 2, 5, 3, 6, 7).reshape(NCB * BE, BE, BE, C1).astype(jnp.bfloat16)
    grid = jnp.pad(chain.astype(jnp.float32)[None], ((0, 0), (1, 1), (1, 1), (1, 1), (0, 0)))
    coarse_kernel = coarse_weight.astype(jnp.float32).reshape(3, 3, 3, C1, C2)
    coarse_full, coarse_pull = jax.vjp(convolve, grid, coarse_kernel)
    coarse_out = coarse_full[0].astype(jnp.bfloat16).reshape(NCB, BE, BE, BE * C2)
    cot_chain = cotangent.astype(jnp.float32).reshape(1, NCB * BE, BE, BE, C2)
    grid_grad, coarse_grad = coarse_pull(cot_chain)
    pooled_grad = grid_grad[0, 1:-1, 1:-1, 1:-1]
    by_octant = pooled_grad.reshape(NCB, 2, half_edge, 2, half_edge, 2, half_edge, C1).transpose(0, 1, 3, 5, 2, 4, 6, 7)
    slot_grad = by_octant[jnp.clip(parent, 0, NCB - 1), octant_x, octant_y, octant_z] * live
    expanded = jnp.broadcast_to(slot_grad[:, :, None, :, None, :, None, :], (NB, half_edge, 2, half_edge, 2, half_edge, 2, C1))
    expanded = expanded.reshape(NB, BE, BE, BE, C1) / 8.0
    act_grad = (expanded * live * (sigma * (1.0 + act * (1.0 - sigma)))).astype(jnp.bfloat16)
    cell_grad = act_grad.astype(jnp.float32).reshape(NB, BE, BE, BE * C1) * (NCB * BE ** 3) ** 0.5
    fine_grad, = fine_pull(act_grad.astype(jnp.float32))
    return (coarse_out, fine_grad.reshape(3, 3, 3 * C1 * C1), coarse_grad.reshape(3, 3, 3 * C1 * C2), cell_grad)
```

```python
import functools

import jax
import jax.numpy as jnp
from jax import lax
from jax.experimental import pallas as pl
from jax.experimental.pallas import tpu as pltpu
from jax.sharding import PartitionSpec as P

BE = 16
C1 = 32
C2 = 64
SLOTS = 4
ROWS = BE * BE
MESH = pl.DeviceIdType.MESH
F32 = jnp.float32
BF16 = jnp.bfloat16


def iota(shape, dim):
    return lax.broadcasted_iota(jnp.int32, shape, dim)


def dot(a, b):
    return jnp.dot(a, b, preferred_element_type=F32)


def dot_t(a, b):
    return lax.dot_general(a, b, (((1,), (1,)), ((), ())), preferred_element_type=F32)


def shifted(cells, row, k):
    if k == 1:
        return cells
    sub = iota(cells.shape, 0)
    if k == 0:
        return jnp.where(sub == 0, row, pltpu.roll(cells, 1, 0))
    return jnp.where(sub == BE - 1, row, pltpu.roll(cells, BE - 1, 0))


def tiled_weight(row, width):
    per_tile = 128 // width
    groups = []
    sub = iota((8, 128), 0)
    lane = iota((8, 128), 1)
    for g in range(C1 // 8):
        first = g * 8 // per_tile
        picked = row[:, first * 128 : (first + 1) * 128]
        picked = jnp.broadcast_to(picked, (8, 128))
        for t in range(1, 8 // per_tile):
            tile = row[:, (first + t) * 128 : (first + t + 1) * 128]
            picked = jnp.where(sub // per_tile == t, tile, picked)
        groups.append(jnp.where(lane // width == sub % per_tile, picked, 0.0))
    tiled = jnp.concatenate(groups, axis=0)
    step = 64
    while step >= width:
        tiled = tiled + pltpu.roll(tiled, step, 1)
        step //= 2
    return tiled


def fold_taps(block, edge_low, edge_high, width):
    quarter = iota((width, 128), 1) // C1
    total = None
    for cls in range(4):
        part = None
        for z_out in (cls, cls + 4):
            rows = block[z_out * width : (z_out + 1) * width]
            tiles = [rows[:, :128], rows[:, 128:]]
            if z_out == 0:
                picked = jnp.where(quarter == 3, edge_low, tiles[0])
            elif z_out == 7:
                picked = jnp.where(quarter == 0, edge_high, tiles[1])
            elif z_out == 3:
                picked = jnp.where(quarter == 0, tiles[1], tiles[0])
            elif z_out == 4:
                picked = jnp.where(quarter == 3, tiles[0], tiles[1])
            else:
                picked = tiles[z_out // 4]
            part = picked if part is None else part + picked
        shift = (1 - cls) % 4 * C1
        if shift:
            part = pltpu.roll(part, shift, 1)
        total = part if total is None else total + part
    return jnp.where(quarter < 3, total, 0.0)


def body(
    nb, ns, nq, shard_rows,
    coords, neigh, feat, fw, cw, cot,
    out_coarse, out_act, out_red,
    hx, hc, hp, ps_ends, xp, ex, wf, wc, wce, wct, cp, ec, pg, up, gt, ct, ps, pool, pp, ep,
    red, rs1, rs2,
    halo_send, halo_recv, s1, r1, s2, r2, s3, r3,
):
    i0 = lax.axis_index("blocks")
    i1 = lax.axis_index("sub")
    count = nb * ns
    me = i0 * ns + i1
    nxt = lax.rem(me + 1, count)
    prv = lax.rem(me + count - 1, count)
    prev_id = (prv // ns, lax.rem(prv, ns))
    next_id = (nxt // ns, lax.rem(nxt, ns))
    na = count // nq
    q = lax.rem(i0, nq)
    a = (i0 // nq) * ns + i1

    def a_peer(j):
        other = lax.rem(a + j, na)
        return other, ((other // ns) * nq + q, lax.rem(other, ns))

    def q_peer(j):
        other = lax.rem(q + j, nq)
        return other, (i0 - q + other, i1)

    barrier = pltpu.get_barrier_semaphore()

    def greet(device):
        pl.semaphore_signal(barrier, inc=1, device_id=device, device_id_type=MESH)

    greet(prev_id)
    greet(next_id)
    for j in range(1, na):
        greet(a_peer(j)[1])
    for j in range(1, nq):
        greet(q_peer(j)[1])
    pl.semaphore_wait(barrier, na + nq)

    def remote(src, dst, send, recv, device):
        copy = pltpu.make_async_remote_copy(
            src_ref=src, dst_ref=dst, send_sem=send, recv_sem=recv, device_id=device, device_id_type=MESH
        )
        copy.start()
        return copy

    halos = [
        remote(feat.at[:, BE - 1], hx.at[0], halo_send.at[0], halo_recv.at[0], next_id),
        remote(feat.at[:, 0], hx.at[1], halo_send.at[1], halo_recv.at[1], prev_id),
        remote(cot.at[0, BE - 1], hc.at[0], halo_send.at[2], halo_recv.at[2], next_id),
        remote(cot.at[0, 0], hc.at[1], halo_send.at[3], halo_recv.at[3], prev_id),
    ]

    quarter8 = iota((C1, 256), 1) // C1
    half8 = iota((C1, 512), 1) // C2
    half4 = iota((C1, 256), 1) // C2
    half2 = iota((C1, 128), 1) // C2
    zeros = jnp.zeros((2 * C1, 256), BF16)
    for dx in range(3):
        for dy in range(3):
            tap = dx * 3 + dy
            row_f = fw[dx, dy : dy + 1, :].astype(F32)
            tiles = []
            for dz in range(3):
                t = tiled_weight(row_f[:, dz * C1 * C1 : (dz + 1) * C1 * C1], C1)
                tiles.append(jnp.concatenate([t, t], axis=1))
            for z_in in range(8):
                line = jnp.where(quarter8 == z_in, tiles[1], 0.0)
                line = jnp.where(quarter8 == z_in + 1, tiles[0], line)
                line = jnp.where(quarter8 == z_in - 1, tiles[2], line)
                wf[tap * 256 + z_in * C1 : tap * 256 + (z_in + 1) * C1, :] = line.astype(BF16)
            base = 2304 + dx * 384 + dy * 128
            wf[base : base + 32, :] = jnp.where(quarter8 == 7, tiles[2], 0.0).astype(BF16)
            wf[base + 32 : base + 96, :] = zeros
            wf[base + 96 : base + 128, :] = jnp.where(quarter8 == 0, tiles[0], 0.0).astype(BF16)

            row_c = cw[dx, dy : dy + 1, :].astype(F32)
            narrow = [
                tiled_weight(row_c[:, dz * C1 * C2 : (dz + 1) * C1 * C2], C2) for dz in range(3)
            ]
            wide = [jnp.concatenate([t] * 4, axis=1) for t in narrow]
            for z_in in range(8):
                line = jnp.where(half8 == z_in, wide[1], 0.0)
                line = jnp.where(half8 == z_in + 1, wide[0], line)
                line = jnp.where(half8 == z_in - 1, wide[2], line)
                wc[tap, z_in * C1 : (z_in + 1) * C1, :] = line.astype(BF16)
            base = dx * 384 + dy * 128
            pair = [jnp.concatenate([t] * 2, axis=1) for t in narrow]
            wce[base : base + 32, :] = jnp.where(half4 == 1, pair[2], 0.0).astype(BF16)
            wce[base + 32 : base + 96, :] = zeros
            wce[base + 96 : base + 128, :] = jnp.where(half4 == 2, pair[0], 0.0).astype(BF16)
            base = (2 - dx) * 384 + (2 - dy) * 128
            wct[0:96, base : base + 128] = jnp.zeros((96, 128), BF16)
            wct[96:128, base : base + 128] = jnp.where(half2 == 0, narrow[0], 0.0).astype(BF16)
            wct[128:160, base : base + 128] = jnp.where(half2 == 1, narrow[2], 0.0).astype(BF16)
            wct[160:256, base : base + 128] = jnp.zeros((96, 128), BF16)

    first = me * SLOTS
    eye = (iota((256, 256), 0) == iota((256, 256), 1)).astype(BF16)

    flat_cot = cot[0].reshape(ROWS, BE * C2)
    for j in range(4):
        ct[j * 256 : (j + 1) * 256, :] = dot_t(eye, flat_cot[:, j * 256 : (j + 1) * 256]).astype(BF16)

    def put_cot(layer, cells):
        lane = iota((BE, 128), 1)
        zero = jnp.zeros((1, BE * C2), F32)
        for k in range(3):
            plane = shifted(cells, zero, k)
            cp[k, layer] = plane.astype(BF16)
            ec[layer, :, k * 128 : (k + 1) * 128] = jnp.where(
                lane < C2, plane[:, 512:640], plane[:, 384:512]
            ).astype(BF16)

    def cot_layer(x, _):
        put_cot(x + 1, cot[0, x].astype(F32))
        return 0

    lax.fori_loop(0, BE, cot_layer, 0, unroll=2)

    def put_cells(s, layer, cells, row_low, row_high, z_low, z_high):
        lane = iota((BE, 128), 1)
        zero = jnp.zeros((1, 128), F32)
        for k in range(3):
            plane = shifted(cells, (row_low, None, row_high)[k], k)
            xp[k, s, layer] = plane.astype(BF16)
            low = 0.0 if z_low is None else shifted(z_low, zero, k)
            high = 0.0 if z_high is None else shifted(z_high, zero, k)
            ex[0, s, layer, :, k * 128 : (k + 1) * 128] = jnp.where(
                lane < C1, plane[:, 256:384], low
            ).astype(BF16)
            ex[1, s, layer, :, k * 128 : (k + 1) * 128] = jnp.where(
                lane < C1, high, plane[:, 128:256]
            ).astype(BF16)

    def across(s, column):
        target = neigh[s, column]
        local = target - first
        return jnp.clip(local, 0, SLOTS - 1), local, (target >= 0).astype(F32)

    for s in range(SLOTS):
        ylow, _, ylow_on = across(s, 2)
        yhigh, _, yhigh_on = across(s, 3)
        zlow, _, zlow_on = across(s, 4)
        zhigh, _, zhigh_on = across(s, 5)

        def cell_layer(x, _):
            put_cells(
                s,
                x + 1,
                feat[s, x].astype(F32),
                feat[ylow, x].astype(F32)[BE - 1 : BE] * ylow_on,
                feat[yhigh, x].astype(F32)[0:1] * yhigh_on,
                feat[zlow, x, :, 384:512].astype(F32) * zlow_on,
                feat[zhigh, x, :, 0:128].astype(F32) * zhigh_on,
            )
            return 0

        lax.fori_loop(0, BE, cell_layer, 0, unroll=2)

    for copy in halos:
        copy.wait()

    is_first = (me > 0).astype(F32)
    is_last = (me < count - 1).astype(F32)
    put_cot(0, hc[0].astype(F32) * is_first)
    put_cot(BE + 1, hc[1].astype(F32) * is_last)
    for s in range(SLOTS):
        zero = jnp.zeros((1, BE * C1), F32)
        near, local, on = across(s, 0)
        inside = (local >= 0).astype(F32) * on
        outside = (local < 0).astype(F32) * on
        far = jnp.clip(local + SLOTS, 0, SLOTS - 1)
        plane = feat[near, BE - 1].astype(F32) * inside + hx[0, far].astype(F32) * outside
        put_cells(s, 0, plane, zero, zero, None, None)
        near, local, on = across(s, 1)
        inside = (local < SLOTS).astype(F32) * on
        outside = (local >= SLOTS).astype(F32) * on
        far = jnp.clip(local - SLOTS, 0, SLOTS - 1)
        plane = feat[near, 0].astype(F32) * inside + hx[1, far].astype(F32) * outside
        put_cells(s, BE + 1, plane, zero, zero, None, None)

    edge = jnp.concatenate([ec[k : k + BE].reshape(ROWS, 384) for k in range(3)], axis=1)
    from_edge = dot_t(edge, wct[...])
    for h in range(2):
        total = None
        for dx in range(3):
            for dy in range(3):
                window = cp[2 - dy, 2 - dx : 2 - dx + BE, :, h * 512 : (h + 1) * 512]
                term = dot_t(window.reshape(ROWS, 512), wc[dx * 3 + dy])
                total = term if total is None else total + term
        parts = [total[:, :128], total[:, 128:]]
        parts[1 - h] = parts[1 - h] + from_edge[:, h * 128 : (h + 1) * 128]
        for t in range(2):
            part = parts[t].reshape(2, 8, 2, 8, 128)
            for ox in range(2):
                for oy in range(2):
                    pg[ox * 4 + oy * 2 + h, :, :, t * 128 : (t + 1) * 128] = part[ox, :, oy]

    r = iota((256, 512), 0)
    l = iota((256, 512), 1)
    spread_z = ((l // 64 == r // 32) & (l % 32 == r % 32)).astype(BF16)
    r = iota((128, 64), 0)
    l = iota((128, 64), 1)
    spread_y = (r // 2 == l).astype(BF16)
    r = iota((64, 256), 0)
    l = iota((64, 256), 1)
    sum_xy = ((l // 32 == r // 8) & (l % 16 // 2 == r % 8)).astype(BF16)
    r = iota((256, 128), 0)
    l = iota((256, 128), 1)
    sum_z = ((r // 64 == l // 32) & (r % 32 == l % 32)).astype(F32)
    sum_z = (sum_z * 0.125).astype(BF16)

    def fine_slot(s, _):
        live = (coords[s, 0] >= 0).astype(F32)
        octant = lax.rem(coords[s, 0], 2) * 4 + coords[s, 1] * 2 + coords[s, 2]
        octant = jnp.clip(octant, 0, 7)
        grad = pg[octant].reshape(64, 256) * (live * 0.125)
        grad = dot(grad.astype(BF16), spread_z).astype(BF16)
        up[...] = dot(spread_y, grad).reshape(8, 1, BE, 512)
        for h in range(2):
            lanes = slice(h * 256, (h + 1) * 256)
            pieces = [
                xp[dy, s, dx : dx + BE, :, lanes].reshape(ROWS, 256)
                for dx in range(3)
                for dy in range(3)
            ]
            pieces += [ex[h, s, dx : dx + BE].reshape(ROWS, 384) for dx in range(3)]
            act = dot(jnp.concatenate(pieces, axis=1), wf[...])
            sigma = 0.5 * jnp.tanh(0.5 * act) + 0.5
            cells = feat[s, :, :, lanes].reshape(ROWS, 256).astype(F32)
            hidden = (cells + act * sigma).astype(BF16)
            slope = sigma * (1.0 + act * (1.0 - sigma))
            upward = jnp.broadcast_to(up[:, :, :, lanes], (8, 2, BE, 256)).reshape(ROWS, 256)
            act_grad = (upward * slope).astype(BF16)
            out_act[s, :, :, lanes] = act_grad.reshape(BE, BE, 256)
            gt[s * 2 + h] = dot_t(eye, act_grad).astype(BF16)
            sums = dot(sum_xy, hidden)
            top = sums.astype(BF16)
            rest = (sums - top.astype(F32)).astype(BF16)
            ps[s, :, :, h * 128 : (h + 1) * 128] = (dot(top, sum_z) + dot(rest, sum_z)).reshape(8, 8, 128)
        return 0

    lax.fori_loop(0, SLOTS, fine_slot, 0)

    for t in range(8):
        slot = jnp.int32(0)
        on = jnp.int32(0)
        for s in range(SLOTS):
            octant = lax.rem(coords[s, 0], 2) * 4 + coords[s, 1] * 2 + coords[s, 2]
            here = ((coords[s, 0] >= 0) & (octant == t)).astype(jnp.int32)
            slot = slot + here * s
            on = on + here
        block = ps[jnp.clip(slot, 0, SLOTS - 1)] * on.astype(F32)
        ox, oy, oz = t // 4, t // 2 % 2, t % 2
        pool[ox * 8 : (ox + 1) * 8, oy * 8 : (oy + 1) * 8, oz * 256 : (oz + 1) * 256] = block
    ps_ends[0] = pool[0].astype(BF16)
    ps_ends[1] = pool[BE - 1].astype(BF16)
    ends = [
        remote(ps_ends.at[1], hp.at[0], halo_send.at[4], halo_recv.at[4], next_id),
        remote(ps_ends.at[0], hp.at[1], halo_send.at[5], halo_recv.at[5], prev_id),
    ]

    def put_pool(layer, cells):
        lane = iota((BE, 128), 1)
        zero = jnp.zeros((1, BE * C1), F32)
        for k in range(3):
            plane = shifted(cells, zero, k)
            pp[k, layer] = plane.astype(BF16)
            ep[layer, :, k * 128 : (k + 1) * 128] = jnp.where(
                lane < C1, plane[:, 256:384], plane[:, 128:256]
            ).astype(BF16)

    def pool_layer(x, _):
        put_pool(x + 1, pool[x])
        return 0

    lax.fori_loop(0, BE, pool_layer, 0, unroll=2)

    def fine_dx(dx, _):
        left = jnp.concatenate([gt[i] for i in range(8)], axis=1)
        low = jnp.concatenate([gt[i, 0:32, :] for i in range(8)], axis=1)
        high = jnp.concatenate([gt[i, 224:256, :] for i in range(8)], axis=1)
        edges = jnp.concatenate(
            [ex[i % 2, i // 2, pl.ds(dx, BE)].reshape(ROWS, 384) for i in range(8)], axis=0
        )
        edge_low = dot(low, edges)
        edge_high = dot(high, edges)
        for dy in range(3):
            right = jnp.concatenate(
                [
                    xp[dy, i // 2, pl.ds(dx, BE), :, i % 2 * 256 : i % 2 * 256 + 256].reshape(ROWS, 256)
                    for i in range(8)
                ],
                axis=0,
            )
            lanes = slice(dy * 128, (dy + 1) * 128)
            folded = fold_taps(dot(left, right), edge_low[:, lanes], edge_high[:, lanes], C1)
            red[pl.ds(pl.multiple_of((dx * 3 + dy) * C1, C1), C1), :] = folded.astype(BF16)
        return 0

    lax.fori_loop(0, 3, fine_dx, 0)

    for copy in ends:
        copy.wait()
    put_pool(0, hp[0].astype(F32) * is_first)
    put_pool(BE + 1, hp[1].astype(F32) * is_last)

    def coarse_dx(dx, _):
        left = jnp.concatenate([ct[0:512, :], ct[512:1024, :]], axis=1)
        edges = ep[pl.ds(dx, BE)].reshape(ROWS, 384)
        edge_high = dot(ct[448:512, :], edges)
        edge_low = dot(ct[512:576, :], edges)
        for dy in range(3):
            window = pp[dy, pl.ds(dx, BE)].reshape(ROWS, 512)
            right = jnp.concatenate([window[:, :256], window[:, 256:]], axis=0)
            lanes = slice(dy * 128, (dy + 1) * 128)
            folded = fold_taps(dot(left, right), edge_low[:, lanes], edge_high[:, lanes], C2)
            base = 9 * C1 + (dx * 3 + dy) * C2
            red[pl.ds(pl.multiple_of(base, C1), C2), :] = folded.astype(BF16)
        return 0

    lax.fori_loop(0, 3, coarse_dx, 0)
    used = 9 * (C1 + C2)
    spare = na * shard_rows - used
    if spare:
        red[used:, :] = jnp.zeros((spare, 128), BF16)

    def shard(i):
        return pl.ds(pl.multiple_of(i * shard_rows, shard_rows), shard_rows)

    first_copies = []
    for j in range(1, na):
        other, device = a_peer(j)
        first_copies.append(remote(red.at[shard(other)], rs1.at[a], s1.at[j], r1.at[j], device))

    edge = jnp.concatenate([ep[k : k + BE].reshape(ROWS, 384) for k in range(3)], axis=1)
    from_edge = dot(edge, wce[...])
    for h in range(2):
        pieces = [
            pp[dy, dx : dx + BE, :, h * 256 : (h + 1) * 256].reshape(ROWS, 256)
            for dx in range(3)
            for dy in range(3)
        ]
        total = dot(jnp.concatenate(pieces, axis=1), wc[...].reshape(9 * 256, 512))
        parts = [total[:, t * 128 : (t + 1) * 128] for t in range(4)]
        parts[3 if h == 0 else 0] += from_edge[:, h * 128 : (h + 1) * 128]
        for t in range(4):
            base = h * 512 + t * 128
            out_coarse[0, :, :, base : base + 128] = parts[t].astype(BF16).reshape(BE, BE, 128)

    total = red[shard(a), :].astype(F32)
    for j in range(1, na):
        first_copies[j - 1].wait_recv()
        total = total + rs1[lax.rem(a + na - j, na)].astype(F32)
    rs2[q] = total.astype(BF16)
    second_copies = []
    for j in range(1, nq):
        _, device = q_peer(j)
        second_copies.append(remote(rs2.at[q], rs2.at[q], s2.at[j], r2.at[j], device))
    for copy in second_copies:
        copy.wait_recv()
    total = rs2[0].astype(F32)
    for j in range(1, nq):
        total = total + rs2[j].astype(F32)
    out_red[shard(a), :] = total.astype(BF16)
    third_copies = []
    for j in range(1, na):
        _, device = a_peer(j)
        third_copies.append(
            remote(out_red.at[shard(a)], out_red.at[shard(a)], s3.at[j], r3.at[j], device)
        )
    for copy in third_copies:
        copy.wait_recv()
    for copy in first_copies + second_copies + third_copies:
        copy.wait_send()


def on_device(nb, ns, features, coords, neighbours, fine_weight, coarse_weight, cotangent):
    nq = 8 if nb % 16 == 0 else 2
    na = nb * ns // nq
    shard_rows = -(-9 * (C1 + C2) // (na * 16)) * 16
    vmem = pl.BlockSpec(memory_space=pltpu.VMEM)
    smem = pl.BlockSpec(memory_space=pltpu.SMEM)
    dma = pltpu.SemaphoreType.DMA
    coarse_out, act_grad, sums = pl.pallas_call(
        functools.partial(body, nb, ns, nq, shard_rows),
        out_shape=(
            jax.ShapeDtypeStruct((1, BE, BE, BE * C2), BF16),
            jax.ShapeDtypeStruct((SLOTS, BE, BE, BE * C1), BF16),
            jax.ShapeDtypeStruct((na * shard_rows, 128), BF16),
        ),
        in_specs=[smem, smem, vmem, vmem, vmem, vmem],
        out_specs=(vmem, vmem, vmem),
        scratch_shapes=[
            pltpu.VMEM((2, SLOTS, BE, BE * C1), BF16),
            pltpu.VMEM((2, BE, BE * C2), BF16),
            pltpu.VMEM((2, BE, BE * C1), BF16),
            pltpu.VMEM((2, BE, BE * C1), BF16),
            pltpu.VMEM((3, SLOTS, BE + 2, BE, BE * C1), BF16),
            pltpu.VMEM((2, SLOTS, BE + 2, BE, 384), BF16),
            pltpu.VMEM((9 * 256 + 9 * 128, 256), BF16),
            pltpu.VMEM((9, 256, 512), BF16),
            pltpu.VMEM((9 * 128, 256), BF16),
            pltpu.VMEM((256, 9 * 128), BF16),
            pltpu.VMEM((3, BE + 2, BE, BE * C2), BF16),
            pltpu.VMEM((BE + 2, BE, 384), BF16),
            pltpu.VMEM((8, 8, 8, 256), F32),
            pltpu.VMEM((8, 1, BE, 512), F32),
            pltpu.VMEM((2 * SLOTS, 256, 256), BF16),
            pltpu.VMEM((BE * C2, ROWS), BF16),
            pltpu.VMEM((SLOTS, 8, 8, 256), F32),
            pltpu.VMEM((BE, BE, BE * C1), F32),
            pltpu.VMEM((3, BE + 2, BE, BE * C1), BF16),
            pltpu.VMEM((BE + 2, BE, 384), BF16),
            pltpu.VMEM((na * shard_rows, 128), BF16),
            pltpu.VMEM((na, shard_rows, 128), BF16),
            pltpu.VMEM((nq, shard_rows, 128), BF16),
            dma((6,)), dma((6,)), dma((na,)), dma((na,)), dma((nq,)), dma((nq,)), dma((na,)), dma((na,)),
        ],
        compiler_params=pltpu.CompilerParams(
            collective_id=0, has_side_effects=True, vmem_limit_bytes=56 * 1024 * 1024
        ),
        name="unet_level",
    )(coords, neighbours, features, fine_weight, coarse_weight, cotangent)
    cell_grad = act_grad.astype(F32) * float(nb * ns * BE**3) ** 0.5

    def weight_grad(rows, width):
        grid = rows.reshape(9, width, 128)[:, :, : 3 * C1].astype(F32)
        return grid.transpose(0, 2, 1).reshape(3, 3, 3 * C1 * width)

    fine_grad = weight_grad(sums[: 9 * C1], C1)
    coarse_grad = weight_grad(sums[9 * C1 : 9 * (C1 + C2)], C2)
    return coarse_out, fine_grad, coarse_grad, cell_grad


def solution(mesh):
    nb, ns = mesh.shape["blocks"], mesh.shape["sub"]
    split = P(("blocks", "sub"), None, None, None)
    return jax.shard_map(
        functools.partial(on_device, nb, ns),
        mesh=mesh,
        in_specs=(split, P(("blocks", "sub"), None), P(("blocks", "sub"), None), P(), P(), split),
        out_specs=(split, P(), P(), split),
        check_vma=False,
    )
```

```python
import functools

import jax
import jax.numpy as jnp
from jax import lax
from jax.experimental import pallas as pl
from jax.experimental.pallas import tpu as pltpu
from jax.sharding import PartitionSpec as P

BE = 16
C1 = 32
C2 = 64
SLOTS = 4
ROWS = BE * BE
MESH = pl.DeviceIdType.MESH
F32 = jnp.float32
BF16 = jnp.bfloat16


def iota(shape, dim):
    return lax.broadcasted_iota(jnp.int32, shape, dim)


def eye_matrix(size):
    return (iota((size, size), 0) == iota((size, size), 1)).astype(BF16)


def dot(a, b):
    return jnp.dot(a, b, preferred_element_type=F32)


def dot_t(a, b):
    return lax.dot_general(a, b, (((1,), (1,)), ((), ())), preferred_element_type=F32)


def shifted(cells, row, k):
    if k == 1:
        return cells
    sub = iota(cells.shape, 0)
    if k == 0:
        return jnp.where(sub == 0, row, pltpu.roll(cells, 1, 0))
    return jnp.where(sub == BE - 1, row, pltpu.roll(cells, BE - 1, 0))


def tiled_weight(row, width):
    per_tile = 128 // width
    groups = []
    sub = iota((8, 128), 0)
    lane = iota((8, 128), 1)
    for g in range(C1 // 8):
        first = g * 8 // per_tile
        picked = row[:, first * 128 : (first + 1) * 128]
        picked = jnp.broadcast_to(picked, (8, 128))
        for t in range(1, 8 // per_tile):
            tile = row[:, (first + t) * 128 : (first + t + 1) * 128]
            picked = jnp.where(sub // per_tile == t, tile, picked)
        groups.append(jnp.where(lane // width == sub % per_tile, picked, 0.0))
    tiled = jnp.concatenate(groups, axis=0)
    step = 64
    while step >= width:
        tiled = tiled + pltpu.roll(tiled, step, 1)
        step //= 2
    return tiled


def fold_taps(block, edge_low, edge_high, width):
    quarter = iota((width, 128), 1) // C1
    total = None
    for cls in range(4):
        part = None
        for z_out in (cls, cls + 4):
            rows = block[z_out * width : (z_out + 1) * width]
            tiles = [rows[:, :128], rows[:, 128:]]
            if z_out == 0:
                picked = jnp.where(quarter == 3, edge_low, tiles[0])
            elif z_out == 7:
                picked = jnp.where(quarter == 0, edge_high, tiles[1])
            elif z_out == 3:
                picked = jnp.where(quarter == 0, tiles[1], tiles[0])
            elif z_out == 4:
                picked = jnp.where(quarter == 3, tiles[0], tiles[1])
            else:
                picked = tiles[z_out // 4]
            part = picked if part is None else part + picked
        shift = (1 - cls) % 4 * C1
        if shift:
            part = pltpu.roll(part, shift, 1)
        total = part if total is None else total + part
    return jnp.where(quarter < 3, total, 0.0)


def body(
    nb, ns, nq, fine_rows, coarse_rows,
    coords, neigh, feat, fw, cw, cot,
    out_coarse, out_fine_grad, out_coarse_grad, out_act,
    hx, hc, hp, ps_ends, xp, ex, wf, wc, wce, wct, cp, ec, pg, up, acts, hid, gt, ct, ps, pool, pp, ep,
    folds, turned, lines, red_f, red_c, got_f, got_c, mid_f, mid_c, all_f, all_c,
    halo_send, halo_recv, send_f, recv_f, send_c, recv_c,
):
    i0 = lax.axis_index("blocks")
    i1 = lax.axis_index("sub")
    count = nb * ns
    me = i0 * ns + i1
    nxt = lax.rem(me + 1, count)
    prv = lax.rem(me + count - 1, count)
    prev_id = (prv // ns, lax.rem(prv, ns))
    next_id = (nxt // ns, lax.rem(nxt, ns))
    na = count // nq
    q = lax.rem(i0, nq)
    a = (i0 // nq) * ns + i1

    def a_peer(j):
        other = lax.rem(a + j, na)
        return other, ((other // ns) * nq + q, lax.rem(other, ns))

    def q_peer(j):
        other = lax.rem(q + j, nq)
        return other, (i0 - q + other, i1)

    barrier = pltpu.get_barrier_semaphore()

    def greet(device):
        pl.semaphore_signal(barrier, inc=1, device_id=device, device_id_type=MESH)

    greet(prev_id)
    greet(next_id)
    for j in range(1, na):
        greet(a_peer(j)[1])
    for j in range(1, nq):
        greet(q_peer(j)[1])

    def remote(src, dst, send, recv, device):
        copy = pltpu.make_async_remote_copy(
            src_ref=src, dst_ref=dst, send_sem=send, recv_sem=recv, device_id=device, device_id_type=MESH
        )
        copy.start()
        return copy

    first = me * SLOTS
    quarter8 = iota((C1, 256), 1) // C1
    half8 = iota((C1, 512), 1) // C2
    half4 = iota((C1, 256), 1) // C2
    half2 = iota((C1, 128), 1) // C2
    zeros = jnp.zeros((2 * C1, 256), BF16)
    for dx in range(3):
        for dy in range(3):
            tap = dx * 3 + dy
            row_f = fw[dx, dy : dy + 1, :].astype(F32)
            tiles = []
            for dz in range(3):
                t = tiled_weight(row_f[:, dz * C1 * C1 : (dz + 1) * C1 * C1], C1)
                tiles.append(jnp.concatenate([t, t], axis=1))
            for z_in in range(8):
                line = jnp.where(quarter8 == z_in, tiles[1], 0.0)
                line = jnp.where(quarter8 == z_in + 1, tiles[0], line)
                line = jnp.where(quarter8 == z_in - 1, tiles[2], line)
                wf[tap * 256 + z_in * C1 : tap * 256 + (z_in + 1) * C1, :] = line.astype(BF16)
            base = 2304 + dx * 384 + dy * 128
            wf[base : base + 32, :] = jnp.where(quarter8 == 7, tiles[2], 0.0).astype(BF16)
            wf[base + 32 : base + 96, :] = zeros
            wf[base + 96 : base + 128, :] = jnp.where(quarter8 == 0, tiles[0], 0.0).astype(BF16)

            row_c = cw[dx, dy : dy + 1, :].astype(F32)
            narrow = [
                tiled_weight(row_c[:, dz * C1 * C2 : (dz + 1) * C1 * C2], C2) for dz in range(3)
            ]
            wide = [jnp.concatenate([t] * 4, axis=1) for t in narrow]
            for z_in in range(8):
                line = jnp.where(half8 == z_in, wide[1], 0.0)
                line = jnp.where(half8 == z_in + 1, wide[0], line)
                line = jnp.where(half8 == z_in - 1, wide[2], line)
                wc[tap, z_in * C1 : (z_in + 1) * C1, :] = line.astype(BF16)
            base = dx * 384 + dy * 128
            pair = [jnp.concatenate([t] * 2, axis=1) for t in narrow]
            wce[base : base + 32, :] = jnp.where(half4 == 1, pair[2], 0.0).astype(BF16)
            wce[base + 32 : base + 96, :] = zeros
            wce[base + 96 : base + 128, :] = jnp.where(half4 == 2, pair[0], 0.0).astype(BF16)
            base = (2 - dx) * 384 + (2 - dy) * 128
            wct[0:96, base : base + 128] = jnp.zeros((96, 128), BF16)
            wct[96:128, base : base + 128] = jnp.where(half2 == 0, narrow[0], 0.0).astype(BF16)
            wct[128:160, base : base + 128] = jnp.where(half2 == 1, narrow[2], 0.0).astype(BF16)
            wct[160:256, base : base + 128] = jnp.zeros((96, 128), BF16)

    eye = eye_matrix(256)

    flat_cot = cot[0].reshape(ROWS, BE * C2)
    for j in range(4):
        ct[j * 256 : (j + 1) * 256, :] = dot_t(eye, flat_cot[:, j * 256 : (j + 1) * 256]).astype(BF16)

    def put_cot(layer, cells):
        lane = iota((BE, 128), 1)
        zero = jnp.zeros((1, BE * C2), F32)
        for k in range(3):
            plane = shifted(cells, zero, k)
            cp[k, layer] = plane.astype(BF16)
            ec[layer, :, k * 128 : (k + 1) * 128] = jnp.where(
                lane < C2, plane[:, 512:640], plane[:, 384:512]
            ).astype(BF16)

    def cot_layer(x, _):
        put_cot(x + 1, cot[0, x].astype(F32))
        return 0

    lax.fori_loop(0, BE, cot_layer, 0, unroll=2)

    pl.semaphore_wait(barrier, na + nq)
    halos = [
        remote(feat.at[:, BE - 1], hx.at[0], halo_send.at[0], halo_recv.at[0], next_id),
        remote(feat.at[:, 0], hx.at[1], halo_send.at[1], halo_recv.at[1], prev_id),
        remote(cot.at[0, BE - 1], hc.at[0], halo_send.at[2], halo_recv.at[2], next_id),
        remote(cot.at[0, 0], hc.at[1], halo_send.at[3], halo_recv.at[3], prev_id),
    ]

    def put_cells(s, layer, cells, row_low, row_high, z_low, z_high):
        lane = iota((BE, 128), 1)
        zero = jnp.zeros((1, 128), F32)
        for k in range(3):
            plane = shifted(cells, (row_low, None, row_high)[k], k)
            xp[k, s, layer] = plane.astype(BF16)
            low = 0.0 if z_low is None else shifted(z_low, zero, k)
            high = 0.0 if z_high is None else shifted(z_high, zero, k)
            ex[0, s, layer, :, k * 128 : (k + 1) * 128] = jnp.where(
                lane < C1, plane[:, 256:384], low
            ).astype(BF16)
            ex[1, s, layer, :, k * 128 : (k + 1) * 128] = jnp.where(
                lane < C1, high, plane[:, 128:256]
            ).astype(BF16)

    def across(s, column):
        target = neigh[s, column]
        local = target - first
        return jnp.clip(local, 0, SLOTS - 1), local, (target >= 0).astype(F32)

    for s in range(SLOTS):
        ylow, _, ylow_on = across(s, 2)
        yhigh, _, yhigh_on = across(s, 3)
        zlow, _, zlow_on = across(s, 4)
        zhigh, _, zhigh_on = across(s, 5)

        def cell_layer(x, _):
            put_cells(
                s,
                x + 1,
                feat[s, x].astype(F32),
                feat[ylow, x].astype(F32)[BE - 1 : BE] * ylow_on,
                feat[yhigh, x].astype(F32)[0:1] * yhigh_on,
                feat[zlow, x, :, 384:512].astype(F32) * zlow_on,
                feat[zhigh, x, :, 0:128].astype(F32) * zhigh_on,
            )
            return 0

        lax.fori_loop(0, BE, cell_layer, 0, unroll=2)

    for copy in halos:
        copy.wait()

    is_first = (me > 0).astype(F32)
    is_last = (me < count - 1).astype(F32)
    put_cot(0, hc[0].astype(F32) * is_first)
    put_cot(BE + 1, hc[1].astype(F32) * is_last)
    for s in range(SLOTS):
        zero = jnp.zeros((1, BE * C1), F32)
        near, local, on = across(s, 0)
        inside = (local >= 0).astype(F32) * on
        outside = (local < 0).astype(F32) * on
        far = jnp.clip(local + SLOTS, 0, SLOTS - 1)
        plane = feat[near, BE - 1].astype(F32) * inside + hx[0, far].astype(F32) * outside
        put_cells(s, 0, plane, zero, zero, None, None)
        near, local, on = across(s, 1)
        inside = (local < SLOTS).astype(F32) * on
        outside = (local >= SLOTS).astype(F32) * on
        far = jnp.clip(local - SLOTS, 0, SLOTS - 1)
        plane = feat[near, 0].astype(F32) * inside + hx[1, far].astype(F32) * outside
        put_cells(s, BE + 1, plane, zero, zero, None, None)

    edge = jnp.concatenate([ec[k : k + BE].reshape(ROWS, 384) for k in range(3)], axis=1)
    from_edge = dot_t(edge, wct[...])
    for h in range(2):
        total = None
        for dx in range(3):
            for dy in range(3):
                window = cp[2 - dy, 2 - dx : 2 - dx + BE, :, h * 512 : (h + 1) * 512]
                term = dot_t(window.reshape(ROWS, 512), wc[dx * 3 + dy])
                total = term if total is None else total + term
        parts = [total[:, :128], total[:, 128:]]
        parts[1 - h] = parts[1 - h] + from_edge[:, h * 128 : (h + 1) * 128]
        for t in range(2):
            part = parts[t].reshape(2, 8, 2, 8, 128)
            for ox in range(2):
                for oy in range(2):
                    pg[ox * 4 + oy * 2 + h, :, :, t * 128 : (t + 1) * 128] = part[ox, :, oy]

    r = iota((256, 512), 0)
    l = iota((256, 512), 1)
    spread_z = ((l // 64 == r // 32) & (l % 32 == r % 32)).astype(BF16)
    r = iota((128, 64), 0)
    l = iota((128, 64), 1)
    spread_y = (r // 2 == l).astype(BF16)
    r = iota((64, 256), 0)
    l = iota((64, 256), 1)
    sum_xy = ((l // 32 == r // 8) & (l % 16 // 2 == r % 8)).astype(BF16)
    r = iota((256, 128), 0)
    l = iota((256, 128), 1)
    sum_z = ((r // 64 == l // 32) & (r % 32 == l % 32)).astype(F32)
    sum_z = (sum_z * 0.125).astype(BF16)

    grads = []
    for s in range(SLOTS):
        live = (coords[s, 0] >= 0).astype(F32)
        octant = lax.rem(coords[s, 0], 2) * 4 + coords[s, 1] * 2 + coords[s, 2]
        grads.append(pg[jnp.clip(octant, 0, 7)].reshape(64, 256) * (live * 0.125))
    grads = dot(jnp.concatenate(grads, axis=0).astype(BF16), spread_z).astype(BF16)
    for s in range(SLOTS):
        up[s] = dot(spread_y, grads[s * 64 : (s + 1) * 64]).reshape(8, BE, 512)

    def fine_act(s, _):
        for h in range(2):
            lanes = slice(h * 256, (h + 1) * 256)
            pieces = [
                xp[dy, s, dx : dx + BE, :, lanes].reshape(ROWS, 256)
                for dx in range(3)
                for dy in range(3)
            ]
            pieces += [ex[h, s, dx : dx + BE].reshape(ROWS, 384) for dx in range(3)]
            act = dot(jnp.concatenate(pieces, axis=1), wf[...])
            acts[s, :, :, lanes] = act.reshape(BE, BE, 256)
        return 0

    def fine_layer(i, _):
        s = i // BE
        x = lax.rem(i, BE)
        act = acts[s, x]
        sigma = 0.5 * jnp.tanh(0.5 * act) + 0.5
        gated = act * sigma
        hid[s, x] = (feat[s, x].astype(F32) + gated).astype(BF16)
        slope = sigma + gated * (1.0 - sigma)
        out_act[s, x] = (up[s, x // 2] * slope).astype(BF16)
        return 0

    lax.fori_loop(0, SLOTS, fine_act, 0)
    lax.fori_loop(0, SLOTS * BE, fine_layer, 0, unroll=4)

    sums = jnp.concatenate([dot(sum_xy, hid[s].reshape(ROWS, 512)) for s in range(SLOTS)], axis=0)
    top = sums.astype(BF16)
    rest = (sums - top.astype(F32)).astype(BF16)
    for h in range(2):
        lanes = slice(h * 256, (h + 1) * 256)
        both = jnp.concatenate([top[:, lanes], rest[:, lanes]], axis=1)
        small = dot(both, jnp.concatenate([sum_z, sum_z], axis=0))
        ps[:, :, :, h * 128 : (h + 1) * 128] = small.reshape(SLOTS, 8, 8, 128)

    for t in range(8):
        slot = jnp.int32(0)
        on = jnp.int32(0)
        for s in range(SLOTS):
            octant = lax.rem(coords[s, 0], 2) * 4 + coords[s, 1] * 2 + coords[s, 2]
            here = ((coords[s, 0] >= 0) & (octant == t)).astype(jnp.int32)
            slot = slot + here * s
            on = on + here
        block = ps[jnp.clip(slot, 0, SLOTS - 1)] * on.astype(F32)
        ox, oy, oz = t // 4, t // 2 % 2, t % 2
        pool[ox * 8 : (ox + 1) * 8, oy * 8 : (oy + 1) * 8, oz * 256 : (oz + 1) * 256] = block
    ps_ends[0] = pool[0].astype(BF16)
    ps_ends[1] = pool[BE - 1].astype(BF16)
    ends = [
        remote(ps_ends.at[1], hp.at[0], halo_send.at[4], halo_recv.at[4], next_id),
        remote(ps_ends.at[0], hp.at[1], halo_send.at[5], halo_recv.at[5], prev_id),
    ]

    def put_pool(layer, cells):
        lane = iota((BE, 128), 1)
        zero = jnp.zeros((1, BE * C1), F32)
        for k in range(3):
            plane = shifted(cells, zero, k)
            pp[k, layer] = plane.astype(BF16)
            ep[layer, :, k * 128 : (k + 1) * 128] = jnp.where(
                lane < C1, plane[:, 256:384], plane[:, 128:256]
            ).astype(BF16)

    def pool_layer(x, _):
        put_pool(x + 1, pool[x])
        return 0

    lax.fori_loop(0, BE, pool_layer, 0, unroll=2)

    eye = eye_matrix(256)
    for i in range(2 * SLOTS):
        lanes = slice(i % 2 * 256, i % 2 * 256 + 256)
        gt[i] = dot_t(eye, out_act[i // 2, :, :, lanes].reshape(ROWS, 256)).astype(BF16)
    eye = eye_matrix(128)

    def turn(rows, width):
        copies = 128 // width
        rows = rows.astype(BF16)
        turned[...] = dot_t(eye, jnp.concatenate([rows] * copies, axis=0))
        lane = iota((3 * C1 // copies, 128), 1) // width
        picked = turned[pl.ds(0, 3 * C1 // copies, stride=copies), :]
        for t in range(1, copies):
            picked = jnp.where(lane == t, turned[pl.ds(t, 3 * C1 // copies, stride=copies), :], picked)
        return picked

    def fine_taps(dx):
        left = jnp.concatenate([gt[i] for i in range(8)], axis=1)
        border = jnp.concatenate(
            [jnp.concatenate([gt[i, 0:32, :], gt[i, 224:256, :]], axis=0) for i in range(8)], axis=1
        )
        edges = jnp.concatenate(
            [ex[i % 2, i // 2, dx : dx + BE].reshape(ROWS, 384) for i in range(8)], axis=0
        )
        edge = dot(border, edges)
        for dy in range(3):
            right = jnp.concatenate(
                [
                    xp[dy, i // 2, dx : dx + BE, :, i % 2 * 256 : i % 2 * 256 + 256].reshape(ROWS, 256)
                    for i in range(8)
                ],
                axis=0,
            )
            lanes = slice(dy * 128, (dy + 1) * 128)
            folded = fold_taps(dot(left, right), edge[:32, lanes], edge[32:, lanes], C1)
            tap = dx * 3 + dy
            lines[tap * 24 : (tap + 1) * 24, :] = turn(folded, C1)

    def coarse_taps(dx):
        left = jnp.concatenate([ct[0:512, :], ct[512:1024, :]], axis=1)
        edge = dot(ct[448:576, :], ep[dx : dx + BE].reshape(ROWS, 384))
        for dy in range(3):
            window = pp[dy, dx : dx + BE].reshape(ROWS, 512)
            right = jnp.concatenate([window[:, :256], window[:, 256:]], axis=0)
            lanes = slice(dy * 128, (dy + 1) * 128)
            folded = fold_taps(dot(left, right), edge[64:, lanes], edge[:64, lanes], C2)
            tap = dx * 3 + dy
            red_c[tap * 48 : (tap + 1) * 48, :] = turn(folded, C2).astype(BF16)

    def spread(red, got, rows, send, recv):
        copies = []
        for j in range(1, na):
            other, device = a_peer(j)
            part = pl.ds(pl.multiple_of(other * rows, rows), rows)
            copies.append(remote(red.at[part], got.at[a], send.at[0, j], recv.at[0, j], device))
        return copies

    def exchange(copies, red, got, mid, rows, send, recv):
        total = red[pl.ds(pl.multiple_of(a * rows, rows), rows), :].astype(F32)
        for j in range(1, na):
            copies[j - 1].wait_recv()
            total = total + got[lax.rem(a + na - j, na)].astype(F32)
        mid[q] = total.astype(BF16)
        return [
            remote(mid.at[q], mid.at[q], send.at[1, j], recv.at[1, j], q_peer(j)[1]) for j in range(1, nq)
        ]

    def gather(copies, mid, full, rows, send, recv):
        for copy in copies:
            copy.wait_recv()
        total = mid[0].astype(F32)
        for j in range(1, nq):
            total = total + mid[j].astype(F32)
        part = pl.ds(pl.multiple_of(a * rows, rows), rows)
        full[part, :] = total.astype(BF16)
        return [
            remote(full.at[part], full.at[part], send.at[2, j], recv.at[2, j], a_peer(j)[1])
            for j in range(1, na)
        ]

    def finish(copies, full, out, count):
        for copy in copies:
            copy.wait_recv()
        folds[: 9 * count, :] = full[: 9 * count, :].astype(F32)
        for dx in range(3):
            for j in range(count):
                out[dx, :, j * 128 : (j + 1) * 128] = folds[pl.ds(dx * 3 * count + j, 3, stride=count), :]

    fine_taps(0)
    for copy in ends:
        copy.wait()
    put_pool(0, hp[0].astype(F32) * is_first)
    put_pool(BE + 1, hp[1].astype(F32) * is_last)
    for dx in range(3):
        coarse_taps(dx)
    if na * coarse_rows > 432:
        red_c[432:, :] = jnp.zeros((na * coarse_rows - 432, 128), BF16)
    c1 = spread(red_c, got_c, coarse_rows, send_c, recv_c)
    fine_taps(1)
    fine_taps(2)
    lines[216:, :] = jnp.zeros((na * fine_rows - 216, 128), F32)
    red_f[...] = lines[...].astype(BF16)
    f1 = spread(red_f, got_f, fine_rows, send_f, recv_f)
    c2 = exchange(c1, red_c, got_c, mid_c, coarse_rows, send_c, recv_c)
    edge = jnp.concatenate([ep[k : k + BE].reshape(ROWS, 384) for k in range(3)], axis=1)
    from_edge = dot(edge, wce[...])
    for h in range(2):
        pieces = [
            pp[dy, dx : dx + BE, :, h * 256 : (h + 1) * 256].reshape(ROWS, 256)
            for dx in range(3)
            for dy in range(3)
        ]
        total = dot(jnp.concatenate(pieces, axis=1), wc[...].reshape(9 * 256, 512))
        parts = [total[:, t * 128 : (t + 1) * 128] for t in range(4)]
        parts[3 if h == 0 else 0] += from_edge[:, h * 128 : (h + 1) * 128]
        for t in range(4):
            base = h * 512 + t * 128
            out_coarse[0, :, :, base : base + 128] = parts[t].astype(BF16).reshape(BE, BE, 128)
    f2 = exchange(f1, red_f, got_f, mid_f, fine_rows, send_f, recv_f)
    c3 = gather(c2, mid_c, all_c, coarse_rows, send_c, recv_c)
    f3 = gather(f2, mid_f, all_f, fine_rows, send_f, recv_f)
    finish(c3, all_c, out_coarse_grad, 48)
    finish(f3, all_f, out_fine_grad, 24)
    for copy in f1 + f2 + f3 + c1 + c2 + c3:
        copy.wait_send()


def on_device(nb, ns, features, coords, neighbours, fine_weight, coarse_weight, cotangent):
    nq = 8 if nb % 16 == 0 else min(nb, 2)
    na = nb * ns // nq
    fine_rows = -(-216 // (na * 16)) * 16
    coarse_rows = -(-432 // (na * 16)) * 16
    vmem = pl.BlockSpec(memory_space=pltpu.VMEM)
    smem = pl.BlockSpec(memory_space=pltpu.SMEM)
    dma = pltpu.SemaphoreType.DMA
    peers = max(na, nq)
    coarse_out, fine_grad, coarse_grad, act_grad = pl.pallas_call(
        functools.partial(body, nb, ns, nq, fine_rows, coarse_rows),
        out_shape=(
            jax.ShapeDtypeStruct((1, BE, BE, BE * C2), BF16),
            jax.ShapeDtypeStruct((3, 3, 3 * C1 * C1), F32),
            jax.ShapeDtypeStruct((3, 3, 3 * C1 * C2), F32),
            jax.ShapeDtypeStruct((SLOTS, BE, BE, BE * C1), BF16),
        ),
        in_specs=[smem, smem, vmem, vmem, vmem, vmem],
        out_specs=(vmem, vmem, vmem, vmem),
        scratch_shapes=[
            pltpu.VMEM((2, SLOTS, BE, BE * C1), BF16),
            pltpu.VMEM((2, BE, BE * C2), BF16),
            pltpu.VMEM((2, BE, BE * C1), BF16),
            pltpu.VMEM((2, BE, BE * C1), BF16),
            pltpu.VMEM((3, SLOTS, BE + 2, BE, BE * C1), BF16),
            pltpu.VMEM((2, SLOTS, BE + 2, BE, 384), BF16),
            pltpu.VMEM((9 * 256 + 9 * 128, 256), BF16),
            pltpu.VMEM((9, 256, 512), BF16),
            pltpu.VMEM((9 * 128, 256), BF16),
            pltpu.VMEM((256, 9 * 128), BF16),
            pltpu.VMEM((3, BE + 2, BE, BE * C2), BF16),
            pltpu.VMEM((BE + 2, BE, 384), BF16),
            pltpu.VMEM((8, 8, 8, 256), F32),
            pltpu.VMEM((SLOTS, 8, BE, 512), F32),
            pltpu.VMEM((SLOTS, BE, BE, 512), F32),
            pltpu.VMEM((SLOTS, BE, BE, 512), BF16),
            pltpu.VMEM((2 * SLOTS, 256, 256), BF16),
            pltpu.VMEM((BE * C2, ROWS), BF16),
            pltpu.VMEM((SLOTS, 8, 8, 256), F32),
            pltpu.VMEM((BE, BE, BE * C1), F32),
            pltpu.VMEM((3, BE + 2, BE, BE * C1), BF16),
            pltpu.VMEM((BE + 2, BE, 384), BF16),
            pltpu.VMEM((432, 128), F32),
            pltpu.VMEM((128, 128), F32),
            pltpu.VMEM((na * fine_rows, 128), F32),
            pltpu.VMEM((na * fine_rows, 128), BF16),
            pltpu.VMEM((na * coarse_rows, 128), BF16),
            pltpu.VMEM((na, fine_rows, 128), BF16),
            pltpu.VMEM((na, coarse_rows, 128), BF16),
            pltpu.VMEM((nq, fine_rows, 128), BF16),
            pltpu.VMEM((nq, coarse_rows, 128), BF16),
            pltpu.VMEM((na * fine_rows, 128), BF16),
            pltpu.VMEM((na * coarse_rows, 128), BF16),
            dma((6,)), dma((6,)),
            dma((3, peers)), dma((3, peers)), dma((3, peers)), dma((3, peers)),
        ],
        compiler_params=pltpu.CompilerParams(
            collective_id=0, has_side_effects=True, vmem_limit_bytes=40 * 1024 * 1024
        ),
        name="unet_level",
    )(coords, neighbours, features, fine_weight, coarse_weight, cotangent)
    cell_grad = act_grad.astype(F32) * float(nb * ns * BE**3) ** 0.5

    return coarse_out, fine_grad, coarse_grad, cell_grad


def solution(mesh):
    nb, ns = mesh.shape["blocks"], mesh.shape["sub"]
    split = P(("blocks", "sub"), None, None, None)
    return jax.shard_map(
        functools.partial(on_device, nb, ns),
        mesh=mesh,
        in_specs=(split, P(("blocks", "sub"), None), P(("blocks", "sub"), None), P(), P(), split),
        out_specs=(split, P(), P(), split),
        check_vma=False,
    )
```

```python
import functools

import jax
import jax.numpy as jnp
from jax import lax
from jax.experimental import pallas as pl
from jax.experimental.pallas import tpu as pltpu
from jax.sharding import PartitionSpec as P

BE = 16
C1 = 32
C2 = 64
SLOTS = 4
ROWS = BE * BE
MESH = pl.DeviceIdType.MESH
F32 = jnp.float32
BF16 = jnp.bfloat16


def iota(shape, dim):
    return lax.broadcasted_iota(jnp.int32, shape, dim)


def eye_matrix(size):
    return (iota((size, size), 0) == iota((size, size), 1)).astype(BF16)


def dot(a, b):
    return jnp.dot(a, b, preferred_element_type=F32)


def dot_t(a, b):
    return lax.dot_general(a, b, (((1,), (1,)), ((), ())), preferred_element_type=F32)


def shifted(cells, row, k):
    if k == 1:
        return cells
    sub = iota(cells.shape, 0)
    if k == 0:
        return jnp.where(sub == 0, row, pltpu.roll(cells, 1, 0))
    return jnp.where(sub == BE - 1, row, pltpu.roll(cells, BE - 1, 0))


def tiled_weight(row, width):
    per_tile = 128 // width
    groups = []
    sub = iota((8, 128), 0)
    lane = iota((8, 128), 1)
    for g in range(C1 // 8):
        first = g * 8 // per_tile
        picked = row[:, first * 128 : (first + 1) * 128]
        picked = jnp.broadcast_to(picked, (8, 128))
        for t in range(1, 8 // per_tile):
            tile = row[:, (first + t) * 128 : (first + t + 1) * 128]
            picked = jnp.where(sub // per_tile == t, tile, picked)
        groups.append(jnp.where(lane // width == sub % per_tile, picked, 0.0))
    tiled = jnp.concatenate(groups, axis=0)
    step = 64
    while step >= width:
        tiled = tiled + pltpu.roll(tiled, step, 1)
        step //= 2
    return tiled


def fold_taps(block, edge_low, edge_high, width):
    quarter = iota((width, 128), 1) // C1
    total = None
    for cls in range(4):
        part = None
        for z_out in (cls, cls + 4):
            rows = block[z_out * width : (z_out + 1) * width]
            tiles = [rows[:, :128], rows[:, 128:]]
            if z_out == 0:
                picked = jnp.where(quarter == 3, edge_low, tiles[0])
            elif z_out == 7:
                picked = jnp.where(quarter == 0, edge_high, tiles[1])
            elif z_out == 3:
                picked = jnp.where(quarter == 0, tiles[1], tiles[0])
            elif z_out == 4:
                picked = jnp.where(quarter == 3, tiles[0], tiles[1])
            else:
                picked = tiles[z_out // 4]
            part = picked if part is None else part + picked
        shift = (1 - cls) % 4 * C1
        if shift:
            part = pltpu.roll(part, shift, 1)
        total = part if total is None else total + part
    return jnp.where(quarter < 3, total, 0.0)


def body(
    nb, ns, nq, fine_rows, coarse_rows,
    coords, neigh, feat, fw, cw, cot,
    coarse_hbm, out_fine_grad, out_coarse_grad, act_hbm,
    out_coarse, out_act, hx, hc, hp, ps_ends, xp, ex, wf, wc, wce, wct, cp, ec, pg, up, acts, hid, gt, ct, ps, pool, pp, ep,
    folds, turned, sum_f, sum_c, red_f, red_c, got_f, got_c, mid_f, mid_c, all_f, all_c,
    halo_send, halo_recv, send_f, recv_f, send_c, recv_c, out_sem,
):
    i0 = lax.axis_index("blocks")
    i1 = lax.axis_index("sub")
    count = nb * ns
    me = i0 * ns + i1
    nxt = lax.rem(me + 1, count)
    prv = lax.rem(me + count - 1, count)
    prev_id = (prv // ns, lax.rem(prv, ns))
    next_id = (nxt // ns, lax.rem(nxt, ns))
    na = count // nq
    q = lax.rem(i0, nq)
    a = (i0 // nq) * ns + i1

    nz = nb // nq
    zs = [lax.rem(i0 // nq + k, nz) for k in range(nz)]
    ys = [lax.rem(i1 + k, ns) for k in range(ns)]
    blocks = [z * nq + q for z in zs]
    a_peers = [
        (zs[k] * ns + ys[m], (blocks[k], ys[m])) for k in range(nz) for m in range(ns) if k + m > 0
    ]
    q_peers = [(i0 - q + lax.rem(q + k, nq), i1) for k in range(1, nq)]

    barrier = pltpu.get_barrier_semaphore()

    def greet(device):
        pl.semaphore_signal(barrier, inc=1, device_id=device, device_id_type=MESH)

    greet(prev_id)
    greet(next_id)
    for _, device in a_peers:
        greet(device)
    for device in q_peers:
        greet(device)

    def remote(src, dst, send, recv, device):
        copy = pltpu.make_async_remote_copy(
            src_ref=src, dst_ref=dst, send_sem=send, recv_sem=recv, device_id=device, device_id_type=MESH
        )
        copy.start()
        return copy

    first = me * SLOTS
    quarter8 = iota((C1, 256), 1) // C1
    half8 = iota((C1, 512), 1) // C2
    half4 = iota((C1, 256), 1) // C2
    half2 = iota((C1, 128), 1) // C2
    zeros = jnp.zeros((2 * C1, 256), BF16)
    for dx in range(3):
        for dy in range(3):
            tap = dx * 3 + dy
            row_f = fw[dx, dy : dy + 1, :].astype(F32)
            tiles = []
            for dz in range(3):
                t = tiled_weight(row_f[:, dz * C1 * C1 : (dz + 1) * C1 * C1], C1)
                tiles.append(jnp.concatenate([t, t], axis=1))
            for z_in in range(8):
                line = jnp.where(quarter8 == z_in, tiles[1], 0.0)
                line = jnp.where(quarter8 == z_in + 1, tiles[0], line)
                line = jnp.where(quarter8 == z_in - 1, tiles[2], line)
                wf[tap * 256 + z_in * C1 : tap * 256 + (z_in + 1) * C1, :] = line.astype(BF16)
            base = 2304 + dx * 384 + dy * 128
            wf[base : base + 32, :] = jnp.where(quarter8 == 7, tiles[2], 0.0).astype(BF16)
            wf[base + 32 : base + 96, :] = zeros
            wf[base + 96 : base + 128, :] = jnp.where(quarter8 == 0, tiles[0], 0.0).astype(BF16)

            row_c = cw[dx, dy : dy + 1, :].astype(F32)
            narrow = [
                tiled_weight(row_c[:, dz * C1 * C2 : (dz + 1) * C1 * C2], C2) for dz in range(3)
            ]
            wide = [jnp.concatenate([t] * 4, axis=1) for t in narrow]
            for z_in in range(8):
                line = jnp.where(half8 == z_in, wide[1], 0.0)
                line = jnp.where(half8 == z_in + 1, wide[0], line)
                line = jnp.where(half8 == z_in - 1, wide[2], line)
                wc[tap, z_in * C1 : (z_in + 1) * C1, :] = line.astype(BF16)
            base = dx * 384 + dy * 128
            pair = [jnp.concatenate([t] * 2, axis=1) for t in narrow]
            wce[base : base + 32, :] = jnp.where(half4 == 1, pair[2], 0.0).astype(BF16)
            wce[base + 32 : base + 96, :] = zeros
            wce[base + 96 : base + 128, :] = jnp.where(half4 == 2, pair[0], 0.0).astype(BF16)
            base = (2 - dx) * 384 + (2 - dy) * 128
            wct[0:96, base : base + 128] = jnp.zeros((96, 128), BF16)
            wct[96:128, base : base + 128] = jnp.where(half2 == 0, narrow[0], 0.0).astype(BF16)
            wct[128:160, base : base + 128] = jnp.where(half2 == 1, narrow[2], 0.0).astype(BF16)
            wct[160:256, base : base + 128] = jnp.zeros((96, 128), BF16)

    eye = eye_matrix(256)

    flat_cot = cot[0].reshape(ROWS, BE * C2)
    for j in range(4):
        ct[j * 256 : (j + 1) * 256, :] = dot_t(eye, flat_cot[:, j * 256 : (j + 1) * 256]).astype(BF16)

    def put_cot(layer, cells):
        lane = iota((BE, 128), 1)
        zero = jnp.zeros((1, BE * C2), F32)
        for k in range(3):
            plane = shifted(cells, zero, k)
            cp[k, layer] = plane.astype(BF16)
            ec[layer, :, k * 128 : (k + 1) * 128] = jnp.where(
                lane < C2, plane[:, 512:640], plane[:, 384:512]
            ).astype(BF16)

    def cot_layer(x, _):
        put_cot(x + 1, cot[0, x].astype(F32))
        return 0

    lax.fori_loop(0, BE, cot_layer, 0, unroll=2)

    pl.semaphore_wait(barrier, na + nq)
    halos = [
        remote(feat.at[:, BE - 1], hx.at[0], halo_send.at[0], halo_recv.at[0], next_id),
        remote(feat.at[:, 0], hx.at[1], halo_send.at[1], halo_recv.at[1], prev_id),
        remote(cot.at[0, BE - 1], hc.at[0], halo_send.at[2], halo_recv.at[2], next_id),
        remote(cot.at[0, 0], hc.at[1], halo_send.at[3], halo_recv.at[3], prev_id),
    ]

    def put_cells(s, layer, cells, row_low, row_high, z_low, z_high):
        lane = iota((BE, 128), 1)
        zero = jnp.zeros((1, 128), F32)
        for k in range(3):
            plane = shifted(cells, (row_low, None, row_high)[k], k)
            xp[k, s, layer] = plane.astype(BF16)
            low = 0.0 if z_low is None else shifted(z_low, zero, k)
            high = 0.0 if z_high is None else shifted(z_high, zero, k)
            ex[0, s, layer, :, k * 128 : (k + 1) * 128] = jnp.where(
                lane < C1, plane[:, 256:384], low
            ).astype(BF16)
            ex[1, s, layer, :, k * 128 : (k + 1) * 128] = jnp.where(
                lane < C1, high, plane[:, 128:256]
            ).astype(BF16)

    def across(s, column):
        target = neigh[s, column]
        local = target - first
        return jnp.clip(local, 0, SLOTS - 1), local, (target >= 0).astype(F32)

    for s in range(SLOTS):
        ylow, _, ylow_on = across(s, 2)
        yhigh, _, yhigh_on = across(s, 3)
        zlow, _, zlow_on = across(s, 4)
        zhigh, _, zhigh_on = across(s, 5)

        def cell_layer(x, _):
            put_cells(
                s,
                x + 1,
                feat[s, x].astype(F32),
                feat[ylow, x].astype(F32)[BE - 1 : BE] * ylow_on,
                feat[yhigh, x].astype(F32)[0:1] * yhigh_on,
                feat[zlow, x, :, 384:512].astype(F32) * zlow_on,
                feat[zhigh, x, :, 0:128].astype(F32) * zhigh_on,
            )
            return 0

        lax.fori_loop(0, BE, cell_layer, 0, unroll=2)

    for copy in halos:
        copy.wait()

    is_first = (me > 0).astype(F32)
    is_last = (me < count - 1).astype(F32)
    put_cot(0, hc[0].astype(F32) * is_first)
    put_cot(BE + 1, hc[1].astype(F32) * is_last)
    for s in range(SLOTS):
        zero = jnp.zeros((1, BE * C1), F32)
        near, local, on = across(s, 0)
        inside = (local >= 0).astype(F32) * on
        outside = (local < 0).astype(F32) * on
        far = jnp.clip(local + SLOTS, 0, SLOTS - 1)
        plane = feat[near, BE - 1].astype(F32) * inside + hx[0, far].astype(F32) * outside
        put_cells(s, 0, plane, zero, zero, None, None)
        near, local, on = across(s, 1)
        inside = (local < SLOTS).astype(F32) * on
        outside = (local >= SLOTS).astype(F32) * on
        far = jnp.clip(local - SLOTS, 0, SLOTS - 1)
        plane = feat[near, 0].astype(F32) * inside + hx[1, far].astype(F32) * outside
        put_cells(s, BE + 1, plane, zero, zero, None, None)

    edge = jnp.concatenate([ec[k : k + BE].reshape(ROWS, 384) for k in range(3)], axis=1)
    from_edge = dot_t(edge, wct[...])
    for h in range(2):
        total = None
        for dx in range(3):
            for dy in range(3):
                window = cp[2 - dy, 2 - dx : 2 - dx + BE, :, h * 512 : (h + 1) * 512]
                term = dot_t(window.reshape(ROWS, 512), wc[dx * 3 + dy])
                total = term if total is None else total + term
        parts = [total[:, :128], total[:, 128:]]
        parts[1 - h] = parts[1 - h] + from_edge[:, h * 128 : (h + 1) * 128]
        for t in range(2):
            part = parts[t].reshape(2, 8, 2, 8, 128)
            for ox in range(2):
                for oy in range(2):
                    pg[ox * 4 + oy * 2 + h, :, :, t * 128 : (t + 1) * 128] = part[ox, :, oy]

    r = iota((256, 512), 0)
    l = iota((256, 512), 1)
    spread_z = ((l // 64 == r // 32) & (l % 32 == r % 32)).astype(BF16)
    r = iota((128, 64), 0)
    l = iota((128, 64), 1)
    spread_y = (r // 2 == l).astype(BF16)
    r = iota((64, 256), 0)
    l = iota((64, 256), 1)
    sum_xy = ((l // 32 == r // 8) & (l % 16 // 2 == r % 8)).astype(BF16)
    r = iota((256, 128), 0)
    l = iota((256, 128), 1)
    sum_z = ((r // 64 == l // 32) & (r % 32 == l % 32)).astype(F32)
    sum_z = (sum_z * 0.125).astype(BF16)

    grads = []
    for s in range(SLOTS):
        live = (coords[s, 0] >= 0).astype(F32)
        octant = lax.rem(coords[s, 0], 2) * 4 + coords[s, 1] * 2 + coords[s, 2]
        grads.append(pg[jnp.clip(octant, 0, 7)].reshape(64, 256) * (live * 0.125))
    grads = dot(jnp.concatenate(grads, axis=0).astype(BF16), spread_z).astype(BF16)
    for s in range(SLOTS):
        up[s] = dot(spread_y, grads[s * 64 : (s + 1) * 64]).reshape(8, BE, 512)

    def fine_act(s, _):
        for h in range(2):
            lanes = slice(h * 256, (h + 1) * 256)
            pieces = [
                xp[dy, s, dx : dx + BE, :, lanes].reshape(ROWS, 256)
                for dx in range(3)
                for dy in range(3)
            ]
            pieces += [ex[h, s, dx : dx + BE].reshape(ROWS, 384) for dx in range(3)]
            act = dot(jnp.concatenate(pieces, axis=1), wf[...])
            acts[s, :, :, lanes] = act.reshape(BE, BE, 256)
        return 0

    def fine_layer(i, _):
        s = i // BE
        x = lax.rem(i, BE)
        act = acts[s, x]
        sigma = 0.5 * jnp.tanh(0.5 * act) + 0.5
        gated = act * sigma
        hid[s, x] = (feat[s, x].astype(F32) + gated).astype(BF16)
        slope = sigma + gated * (1.0 - sigma)
        out_act[s, x] = (up[s, x // 2] * slope).astype(BF16)
        return 0

    for s in range(SLOTS + 1):
        if s < SLOTS:
            fine_act(s, 0)
        if s > 0:
            for x in range(BE):
                fine_layer((s - 1) * BE + x, 0)

    sums = jnp.concatenate([dot(sum_xy, hid[s].reshape(ROWS, 512)) for s in range(SLOTS)], axis=0)
    top = sums.astype(BF16)
    rest = (sums - top.astype(F32)).astype(BF16)
    for h in range(2):
        lanes = slice(h * 256, (h + 1) * 256)
        both = jnp.concatenate([top[:, lanes], rest[:, lanes]], axis=1)
        small = dot(both, jnp.concatenate([sum_z, sum_z], axis=0))
        ps[:, :, :, h * 128 : (h + 1) * 128] = small.reshape(SLOTS, 8, 8, 128)

    for t in range(8):
        slot = jnp.int32(0)
        on = jnp.int32(0)
        for s in range(SLOTS):
            octant = lax.rem(coords[s, 0], 2) * 4 + coords[s, 1] * 2 + coords[s, 2]
            here = ((coords[s, 0] >= 0) & (octant == t)).astype(jnp.int32)
            slot = slot + here * s
            on = on + here
        block = ps[jnp.clip(slot, 0, SLOTS - 1)] * on.astype(F32)
        ox, oy, oz = t // 4, t // 2 % 2, t % 2
        pool[ox * 8 : (ox + 1) * 8, oy * 8 : (oy + 1) * 8, oz * 256 : (oz + 1) * 256] = block
    ps_ends[0] = pool[0].astype(BF16)
    ps_ends[1] = pool[BE - 1].astype(BF16)
    ends = [
        remote(ps_ends.at[1], hp.at[0], halo_send.at[4], halo_recv.at[4], next_id),
        remote(ps_ends.at[0], hp.at[1], halo_send.at[5], halo_recv.at[5], prev_id),
    ]

    def put_pool(layer, cells):
        lane = iota((BE, 128), 1)
        zero = jnp.zeros((1, BE * C1), F32)
        for k in range(3):
            plane = shifted(cells, zero, k)
            pp[k, layer] = plane.astype(BF16)
            ep[layer, :, k * 128 : (k + 1) * 128] = jnp.where(
                lane < C1, plane[:, 256:384], plane[:, 128:256]
            ).astype(BF16)

    def pool_layer(x, _):
        put_pool(x + 1, pool[x])
        return 0

    lax.fori_loop(0, BE, pool_layer, 0, unroll=2)

    save_act = pltpu.make_async_copy(out_act, act_hbm, out_sem.at[0])
    save_act.start()
    eye = eye_matrix(256)
    for i in range(2 * SLOTS):
        lanes = slice(i % 2 * 256, i % 2 * 256 + 256)
        gt[i] = dot_t(eye, out_act[i // 2, :, :, lanes].reshape(ROWS, 256)).astype(BF16)
    eye = eye_matrix(128)

    def turn(sums, width):
        copies = 128 // width
        count = 3 * C1 // copies
        rows = [sums[tap * width : (tap + 1) * width, :] for tap in range(9) for _ in range(copies)]
        flipped = dot_t(eye, jnp.concatenate(rows, axis=0))
        for tap in range(9):
            turned[tap * 128 : (tap + 1) * 128, :] = flipped[:, tap * 128 : (tap + 1) * 128]
        lane = iota((count, 128), 1) // width
        lines = []
        for tap in range(9):
            base = tap * 128
            picked = turned[pl.ds(base, count, stride=copies), :]
            for t in range(1, copies):
                picked = jnp.where(lane == t, turned[pl.ds(base + t, count, stride=copies), :], picked)
            lines.append(picked)
        return lines

    def fine_taps(dx):
        left = jnp.concatenate([gt[i] for i in range(8)], axis=1)
        border = jnp.concatenate(
            [jnp.concatenate([gt[i, 0:32, :], gt[i, 224:256, :]], axis=0) for i in range(8)], axis=1
        )
        edges = jnp.concatenate(
            [ex[i % 2, i // 2, dx : dx + BE].reshape(ROWS, 384) for i in range(8)], axis=0
        )
        edge = dot(border, edges)
        for dy in range(3):
            right = jnp.concatenate(
                [
                    xp[dy, i // 2, dx : dx + BE, :, i % 2 * 256 : i % 2 * 256 + 256].reshape(ROWS, 256)
                    for i in range(8)
                ],
                axis=0,
            )
            lanes = slice(dy * 128, (dy + 1) * 128)
            folded = fold_taps(dot(left, right), edge[:32, lanes], edge[32:, lanes], C1)
            tap = dx * 3 + dy
            sum_f[tap * C1 : (tap + 1) * C1, :] = folded.astype(BF16)

    def coarse_taps(dx):
        left = jnp.concatenate([ct[0:512, :], ct[512:1024, :]], axis=1)
        edge = dot(ct[448:576, :], ep[dx : dx + BE].reshape(ROWS, 384))
        for dy in range(3):
            window = pp[dy, dx : dx + BE].reshape(ROWS, 512)
            right = jnp.concatenate([window[:, :256], window[:, 256:]], axis=0)
            lanes = slice(dy * 128, (dy + 1) * 128)
            folded = fold_taps(dot(left, right), edge[64:, lanes], edge[:64, lanes], C2)
            tap = dx * 3 + dy
            sum_c[tap * C2 : (tap + 1) * C2, :] = folded.astype(BF16)

    def all_of(ref, send, recv):
        return pltpu.make_async_remote_copy(
            src_ref=ref, dst_ref=ref, send_sem=send, recv_sem=recv, device_id=next_id, device_id_type=MESH
        )

    def shard(i, rows):
        return pl.ds(pl.multiple_of(i * rows, rows), rows)

    def spread(red, got, rows, send, recv):
        for j, (other, device) in enumerate(a_peers):
            remote(red.at[shard(other, rows)], got.at[j], send.at[0], recv.at[0], device)
        return all_of(got, send.at[0], recv.at[0])

    def exchange(copies, red, got, mid, rows, send, recv):
        copies.wait_recv()
        total = red[shard(a, rows), :].astype(F32)
        for j in range(na - 1):
            total = total + got[j].astype(F32)
        mid[q] = total.astype(BF16)
        for device in q_peers:
            remote(mid.at[q], mid.at[q], send.at[1], recv.at[1], device)
        return all_of(mid.at[0 : nq - 1], send.at[1], recv.at[1])

    def gather(copies, mid, full, rows, send, recv):
        copies.wait_recv()
        total = mid[0].astype(F32)
        for j in range(1, nq):
            total = total + mid[j].astype(F32)
        part = shard(a, rows)
        full[part, :] = total.astype(BF16)
        for _, device in a_peers:
            remote(full.at[part], full.at[part], send.at[2], recv.at[2], device)
        return all_of(full.at[0 : (na - 1) * rows], send.at[2], recv.at[2])

    def finish(copies, full, out, count):
        copies.wait_recv()
        folds[: 9 * count, :] = full[: 9 * count, :].astype(F32)
        for dx in range(3):
            for j in range(count):
                out[dx, :, j * 128 : (j + 1) * 128] = folds[pl.ds(dx * 3 * count + j, 3, stride=count), :]

    fine_taps(0)
    for copy in ends:
        copy.wait()
    put_pool(0, hp[0].astype(F32) * is_first)
    put_pool(BE + 1, hp[1].astype(F32) * is_last)
    for dx in range(3):
        coarse_taps(dx)
    for tap, rows in enumerate(turn(sum_c, C2)):
        red_c[tap * 48 : (tap + 1) * 48, :] = rows.astype(BF16)
    if na * coarse_rows > 432:
        red_c[432:, :] = jnp.zeros((na * coarse_rows - 432, 128), BF16)
    c1 = spread(red_c, got_c, coarse_rows, send_c, recv_c)
    fine_taps(1)
    fine_taps(2)
    rows = turn(sum_f, C1) + [jnp.zeros((na * fine_rows - 216, 128), F32)]
    red_f[...] = jnp.concatenate(rows, axis=0).astype(BF16)
    f1 = spread(red_f, got_f, fine_rows, send_f, recv_f)
    c2 = exchange(c1, red_c, got_c, mid_c, coarse_rows, send_c, recv_c)
    edge = jnp.concatenate([ep[k : k + BE].reshape(ROWS, 384) for k in range(3)], axis=1)
    from_edge = dot(edge, wce[...])
    for h in range(2):
        pieces = [
            pp[dy, dx : dx + BE, :, h * 256 : (h + 1) * 256].reshape(ROWS, 256)
            for dx in range(3)
            for dy in range(3)
        ]
        total = dot(jnp.concatenate(pieces, axis=1), wc[...].reshape(9 * 256, 512))
        parts = [total[:, t * 128 : (t + 1) * 128] for t in range(4)]
        parts[3 if h == 0 else 0] += from_edge[:, h * 128 : (h + 1) * 128]
        for t in range(4):
            base = h * 512 + t * 128
            out_coarse[0, :, :, base : base + 128] = parts[t].astype(BF16).reshape(BE, BE, 128)
    save_coarse = pltpu.make_async_copy(out_coarse, coarse_hbm, out_sem.at[1])
    save_coarse.start()
    f2 = exchange(f1, red_f, got_f, mid_f, fine_rows, send_f, recv_f)
    c3 = gather(c2, mid_c, all_c, coarse_rows, send_c, recv_c)
    f3 = gather(f2, mid_f, all_f, fine_rows, send_f, recv_f)
    finish(c3, all_c, out_coarse_grad, 48)
    finish(f3, all_f, out_fine_grad, 24)
    for copy in (f1, f2, f3, c1, c2, c3):
        copy.wait_send()
    save_act.wait()
    save_coarse.wait()


def hand_over(
    scale, coarse, fine_grad, coarse_grad, act, out_coarse, out_fine_grad, out_coarse_grad, out_cell,
    narrow, wide, keep_coarse, keep_f, keep_c, in_sem, out_sem, other_sem,
):
    ins = [pltpu.make_async_copy(act.at[s], narrow.at[s], in_sem.at[s]) for s in range(SLOTS)]
    outs = [pltpu.make_async_copy(wide.at[s], out_cell.at[s], out_sem.at[s]) for s in range(SLOTS)]
    pairs = ((coarse, keep_coarse, out_coarse), (fine_grad, keep_f, out_fine_grad), (coarse_grad, keep_c, out_coarse_grad))
    first = [pltpu.make_async_copy(a, b, other_sem.at[i]) for i, (a, b, _) in enumerate(pairs)]
    second = [pltpu.make_async_copy(b, c, other_sem.at[i + 3]) for i, (_, b, c) in enumerate(pairs)]
    for copy in ins + first:
        copy.start()
    for s in range(SLOTS):
        ins[s].wait()
        wide[s] = narrow[s].astype(F32) * scale
        outs[s].start()
    for i in range(3):
        first[i].wait()
        second[i].start()
    for copy in outs + second:
        copy.wait()


def on_device(nb, ns, features, coords, neighbours, fine_weight, coarse_weight, cotangent):
    nq = 8 if nb % 16 == 0 else min(nb, 2)
    na = nb * ns // nq
    fine_rows = -(-216 // (na * 16)) * 16
    coarse_rows = -(-432 // (na * 16)) * 16
    vmem = pl.BlockSpec(memory_space=pltpu.VMEM)
    smem = pl.BlockSpec(memory_space=pltpu.SMEM)
    hbm = pl.BlockSpec(memory_space=pl.ANY)
    dma = pltpu.SemaphoreType.DMA
    coarse_out, fine_grad, coarse_grad, act_grad = pl.pallas_call(
        functools.partial(body, nb, ns, nq, fine_rows, coarse_rows),
        out_shape=(
            jax.ShapeDtypeStruct((1, BE, BE, BE * C2), BF16),
            jax.ShapeDtypeStruct((3, 3, 3 * C1 * C1), F32),
            jax.ShapeDtypeStruct((3, 3, 3 * C1 * C2), F32),
            jax.ShapeDtypeStruct((SLOTS, BE, BE, BE * C1), BF16),
        ),
        in_specs=[smem, smem, vmem, vmem, vmem, vmem],
        out_specs=(hbm, vmem, vmem, hbm),
        scratch_shapes=[
            pltpu.VMEM((1, BE, BE, BE * C2), BF16),
            pltpu.VMEM((SLOTS, BE, BE, BE * C1), BF16),
            pltpu.VMEM((2, SLOTS, BE, BE * C1), BF16),
            pltpu.VMEM((2, BE, BE * C2), BF16),
            pltpu.VMEM((2, BE, BE * C1), BF16),
            pltpu.VMEM((2, BE, BE * C1), BF16),
            pltpu.VMEM((3, SLOTS, BE + 2, BE, BE * C1), BF16),
            pltpu.VMEM((2, SLOTS, BE + 2, BE, 384), BF16),
            pltpu.VMEM((9 * 256 + 9 * 128, 256), BF16),
            pltpu.VMEM((9, 256, 512), BF16),
            pltpu.VMEM((9 * 128, 256), BF16),
            pltpu.VMEM((256, 9 * 128), BF16),
            pltpu.VMEM((3, BE + 2, BE, BE * C2), BF16),
            pltpu.VMEM((BE + 2, BE, 384), BF16),
            pltpu.VMEM((8, 8, 8, 256), F32),
            pltpu.VMEM((SLOTS, 8, BE, 512), F32),
            pltpu.VMEM((SLOTS, BE, BE, 512), F32),
            pltpu.VMEM((SLOTS, BE, BE, 512), BF16),
            pltpu.VMEM((2 * SLOTS, 256, 256), BF16),
            pltpu.VMEM((BE * C2, ROWS), BF16),
            pltpu.VMEM((SLOTS, 8, 8, 256), F32),
            pltpu.VMEM((BE, BE, BE * C1), F32),
            pltpu.VMEM((3, BE + 2, BE, BE * C1), BF16),
            pltpu.VMEM((BE + 2, BE, 384), BF16),
            pltpu.VMEM((432, 128), F32),
            pltpu.VMEM((9 * 128, 128), F32),
            pltpu.VMEM((9 * C1, 128), BF16),
            pltpu.VMEM((9 * C2, 128), BF16),
            pltpu.VMEM((na * fine_rows, 128), BF16),
            pltpu.VMEM((na * coarse_rows, 128), BF16),
            pltpu.VMEM((na - 1, fine_rows, 128), BF16),
            pltpu.VMEM((na - 1, coarse_rows, 128), BF16),
            pltpu.VMEM((nq, fine_rows, 128), BF16),
            pltpu.VMEM((nq, coarse_rows, 128), BF16),
            pltpu.VMEM((na * fine_rows, 128), BF16),
            pltpu.VMEM((na * coarse_rows, 128), BF16),
            dma((6,)), dma((6,)),
            dma((3,)), dma((3,)), dma((3,)), dma((3,)), dma((2,)),
        ],
        compiler_params=pltpu.CompilerParams(
            collective_id=0, has_side_effects=True, vmem_limit_bytes=58 * 1024 * 1024
        ),
        name="unet_level",
    )(coords, neighbours, features, fine_weight, coarse_weight, cotangent)
    scale = float(nb * ns * BE**3) ** 0.5
    return pl.pallas_call(
        functools.partial(hand_over, scale),
        out_shape=(
            jax.ShapeDtypeStruct(coarse_out.shape, BF16),
            jax.ShapeDtypeStruct(fine_grad.shape, F32),
            jax.ShapeDtypeStruct(coarse_grad.shape, F32),
            jax.ShapeDtypeStruct(act_grad.shape, F32),
        ),
        in_specs=[hbm] * 4,
        out_specs=(hbm,) * 4,
        scratch_shapes=[
            pltpu.VMEM(act_grad.shape, BF16),
            pltpu.VMEM(act_grad.shape, F32),
            pltpu.VMEM(coarse_out.shape, BF16),
            pltpu.VMEM(fine_grad.shape, F32),
            pltpu.VMEM(coarse_grad.shape, F32),
            dma((SLOTS,)), dma((SLOTS,)), dma((6,)),
        ],
        compiler_params=pltpu.CompilerParams(vmem_limit_bytes=58 * 1024 * 1024),
        name="hand_over",
    )(coarse_out, fine_grad, coarse_grad, act_grad)


def solution(mesh):
    nb, ns = mesh.shape["blocks"], mesh.shape["sub"]
    split = P(("blocks", "sub"), None, None, None)
    return jax.shard_map(
        functools.partial(on_device, nb, ns),
        mesh=mesh,
        in_specs=(split, P(("blocks", "sub"), None), P(("blocks", "sub"), None), P(), P(), split),
        out_specs=(split, P(), P(), split),
        check_vma=False,
    )
```

```python
import functools

import jax
import jax.numpy as jnp
from jax import lax
from jax.experimental import pallas as pl
from jax.experimental.pallas import tpu as pltpu
from jax.sharding import PartitionSpec as P

BE = 16
C1 = 32
C2 = 64
SLOTS = 4
ROWS = BE * BE
MESH = pl.DeviceIdType.MESH
F32 = jnp.float32
BF16 = jnp.bfloat16


def iota(shape, dim):
    return lax.broadcasted_iota(jnp.int32, shape, dim)


def eye_matrix(size):
    return (iota((size, size), 0) == iota((size, size), 1)).astype(BF16)


def dot(a, b):
    return jnp.dot(a, b, preferred_element_type=F32)


def dot_t(a, b):
    return lax.dot_general(a, b, (((1,), (1,)), ((), ())), preferred_element_type=F32)


def shifted(cells, row, k):
    if k == 1:
        return cells
    sub = iota(cells.shape, 0)
    if k == 0:
        return jnp.where(sub == 0, row, pltpu.roll(cells, 1, 0))
    return jnp.where(sub == BE - 1, row, pltpu.roll(cells, BE - 1, 0))


def tiled_weight(row, width):
    per_tile = 128 // width
    groups = []
    sub = iota((8, 128), 0)
    lane = iota((8, 128), 1)
    for g in range(C1 // 8):
        first = g * 8 // per_tile
        picked = row[:, first * 128 : (first + 1) * 128]
        picked = jnp.broadcast_to(picked, (8, 128))
        for t in range(1, 8 // per_tile):
            tile = row[:, (first + t) * 128 : (first + t + 1) * 128]
            picked = jnp.where(sub // per_tile == t, tile, picked)
        groups.append(jnp.where(lane // width == sub % per_tile, picked, 0.0))
    tiled = jnp.concatenate(groups, axis=0)
    step = 64
    while step >= width:
        tiled = tiled + pltpu.roll(tiled, step, 1)
        step //= 2
    return tiled


def fold_taps(block, edge_low, edge_high, width):
    quarter = iota((width, 128), 1) // C1
    total = None
    for cls in range(4):
        part = None
        for z_out in (cls, cls + 4):
            rows = block[z_out * width : (z_out + 1) * width]
            tiles = [rows[:, :128], rows[:, 128:]]
            if z_out == 0:
                picked = jnp.where(quarter == 3, edge_low, tiles[0])
            elif z_out == 7:
                picked = jnp.where(quarter == 0, edge_high, tiles[1])
            elif z_out == 3:
                picked = jnp.where(quarter == 0, tiles[1], tiles[0])
            elif z_out == 4:
                picked = jnp.where(quarter == 3, tiles[0], tiles[1])
            else:
                picked = tiles[z_out // 4]
            part = picked if part is None else part + picked
        shift = (1 - cls) % 4 * C1
        if shift:
            part = pltpu.roll(part, shift, 1)
        total = part if total is None else total + part
    return jnp.where(quarter < 3, total, 0.0)


def body(
    nb, ns, nq, fine_rows, coarse_rows,
    coords, neigh, feat_hbm, fw_hbm, cw_hbm, cot_hbm,
    coarse_hbm, out_fine_grad, out_coarse_grad, act_hbm,
    feat, fw, cw, cot, out_coarse, out_act, hx, hc, hp, ps_ends, xp, ex, wf, wc, wce, wct, cp, ec, pg, up, acts, hid, gt, ct, ps, pool, pp, ep,
    folds, turned, sum_f, sum_c, red_f, red_c, got_f, got_c, mid_f, mid_c, all_f, all_c,
    halo_send, halo_recv, send_f, recv_f, send_c, recv_c, out_sem, in_sem,
):
    loads = [
        pltpu.make_async_copy(src, dst, in_sem.at[i])
        for i, (src, dst) in enumerate(((fw_hbm, fw), (cw_hbm, cw), (cot_hbm, cot), (feat_hbm, feat)))
    ]
    for copy in loads:
        copy.start()

    i0 = lax.axis_index("blocks")
    i1 = lax.axis_index("sub")
    count = nb * ns
    me = i0 * ns + i1
    nxt = lax.rem(me + 1, count)
    prv = lax.rem(me + count - 1, count)
    prev_id = (prv // ns, lax.rem(prv, ns))
    next_id = (nxt // ns, lax.rem(nxt, ns))
    na = count // nq
    q = lax.rem(i0, nq)
    a = (i0 // nq) * ns + i1

    nz = nb // nq
    zs = [lax.rem(i0 // nq + k, nz) for k in range(nz)]
    ys = [lax.rem(i1 + k, ns) for k in range(ns)]
    blocks = [z * nq + q for z in zs]
    def way(k, size):
        return min(k, size - k)

    offsets = [(k, m) for k in range(nz) for m in range(ns) if k + m > 0]
    offsets.sort(key=lambda o: -way(o[0], nz) - way(o[1], ns))
    a_peers = [(zs[k] * ns + ys[m], (blocks[k], ys[m])) for k, m in offsets]
    nx = nq // 2
    xs = [lax.rem(q // 2 + k, nx) * 2 for k in range(nx)]
    cores = [lax.rem(q + k, 2) for k in range(2)]
    offsets = [(k, m) for k in range(nx) for m in range(2) if k + m > 0]
    offsets.sort(key=lambda o: -way(o[0], nx) - o[1])
    q_peers = [(i0 - q + xs[k] + cores[m], i1) for k, m in offsets]

    barrier = pltpu.get_barrier_semaphore()

    def greet(device):
        pl.semaphore_signal(barrier, inc=1, device_id=device, device_id_type=MESH)

    has_prev = me > 0
    has_next = me < count - 1
    pl.when(has_prev)(lambda: greet(prev_id))
    pl.when(has_next)(lambda: greet(next_id))
    for _, device in a_peers:
        greet(device)
    for device in q_peers:
        greet(device)

    def describe(src, dst, send, recv, device):
        return pltpu.make_async_remote_copy(
            src_ref=src, dst_ref=dst, send_sem=send, recv_sem=recv, device_id=device, device_id_type=MESH
        )

    def remote(src, dst, send, recv, device):
        describe(src, dst, send, recv, device).start()

    def swap(high, low, dst, k):
        up = describe(high, dst.at[0], halo_send.at[k], halo_recv.at[k], next_id)
        down = describe(low, dst.at[1], halo_send.at[k + 1], halo_recv.at[k + 1], prev_id)
        pl.when(has_next)(up.start)
        pl.when(has_prev)(down.start)

        def clear(side):
            dst[side] = jnp.zeros(dst.shape[1:], dst.dtype)

        def finish_swap():
            pl.when(has_prev)(up.wait_recv)
            pl.when(has_next)(down.wait_recv)
            pl.when(has_next)(up.wait_send)
            pl.when(has_prev)(down.wait_send)
            pl.when(jnp.logical_not(has_prev))(lambda: clear(0))
            pl.when(jnp.logical_not(has_next))(lambda: clear(1))

        return finish_swap

    loads[0].wait()
    loads[1].wait()
    first = me * SLOTS
    quarter8 = iota((C1, 256), 1) // C1
    half8 = iota((C1, 512), 1) // C2
    half4 = iota((C1, 256), 1) // C2
    half2 = iota((C1, 128), 1) // C2
    zeros = jnp.zeros((2 * C1, 256), BF16)
    for dx in range(3):
        for dy in range(3):
            tap = dx * 3 + dy
            row_f = fw[dx, dy : dy + 1, :].astype(F32)
            tiles = []
            for dz in range(3):
                t = tiled_weight(row_f[:, dz * C1 * C1 : (dz + 1) * C1 * C1], C1)
                tiles.append(jnp.concatenate([t, t], axis=1))
            for z_in in range(8):
                line = jnp.where(quarter8 == z_in, tiles[1], 0.0)
                line = jnp.where(quarter8 == z_in + 1, tiles[0], line)
                line = jnp.where(quarter8 == z_in - 1, tiles[2], line)
                wf[tap * 256 + z_in * C1 : tap * 256 + (z_in + 1) * C1, :] = line.astype(BF16)
            base = 2304 + dx * 384 + dy * 128
            wf[base : base + 32, :] = jnp.where(quarter8 == 7, tiles[2], 0.0).astype(BF16)
            wf[base + 32 : base + 96, :] = zeros
            wf[base + 96 : base + 128, :] = jnp.where(quarter8 == 0, tiles[0], 0.0).astype(BF16)

            row_c = cw[dx, dy : dy + 1, :].astype(F32)
            narrow = [
                tiled_weight(row_c[:, dz * C1 * C2 : (dz + 1) * C1 * C2], C2) for dz in range(3)
            ]
            wide = [jnp.concatenate([t] * 4, axis=1) for t in narrow]
            for z_in in range(8):
                line = jnp.where(half8 == z_in, wide[1], 0.0)
                line = jnp.where(half8 == z_in + 1, wide[0], line)
                line = jnp.where(half8 == z_in - 1, wide[2], line)
                wc[tap, z_in * C1 : (z_in + 1) * C1, :] = line.astype(BF16)
            base = dx * 384 + dy * 128
            pair = [jnp.concatenate([t] * 2, axis=1) for t in narrow]
            wce[base : base + 32, :] = jnp.where(half4 == 1, pair[2], 0.0).astype(BF16)
            wce[base + 32 : base + 96, :] = zeros
            wce[base + 96 : base + 128, :] = jnp.where(half4 == 2, pair[0], 0.0).astype(BF16)
            base = (2 - dx) * 384 + (2 - dy) * 128
            wct[0:96, base : base + 128] = jnp.zeros((96, 128), BF16)
            wct[96:128, base : base + 128] = jnp.where(half2 == 0, narrow[0], 0.0).astype(BF16)
            wct[128:160, base : base + 128] = jnp.where(half2 == 1, narrow[2], 0.0).astype(BF16)
            wct[160:256, base : base + 128] = jnp.zeros((96, 128), BF16)

    eye = eye_matrix(256)

    loads[2].wait()
    loads[3].wait()
    pl.semaphore_wait(barrier, na + nq - 2 + has_prev.astype(jnp.int32) + has_next.astype(jnp.int32))
    end_swaps = [
        swap(feat.at[:, BE - 1], feat.at[:, 0], hx, 0),
        swap(cot.at[0, BE - 1], cot.at[0, 0], hc, 2),
    ]
    flat_cot = cot[0].reshape(ROWS, BE * C2)
    for j in range(4):
        ct[j * 256 : (j + 1) * 256, :] = dot_t(eye, flat_cot[:, j * 256 : (j + 1) * 256]).astype(BF16)

    def put_cot(layer, cells):
        lane = iota((BE, 128), 1)
        zero = jnp.zeros((1, BE * C2), F32)
        for k in range(3):
            plane = shifted(cells, zero, k)
            cp[k, layer] = plane.astype(BF16)
            ec[layer, :, k * 128 : (k + 1) * 128] = jnp.where(
                lane < C2, plane[:, 512:640], plane[:, 384:512]
            ).astype(BF16)

    def cot_layer(x, _):
        put_cot(x + 1, cot[0, x].astype(F32))
        return 0

    lax.fori_loop(0, BE, cot_layer, 0, unroll=2)

    def put_cells(s, layer, cells, row_low, row_high, z_low, z_high):
        lane = iota((BE, 128), 1)
        zero = jnp.zeros((1, 128), F32)
        for k in range(3):
            plane = shifted(cells, (row_low, None, row_high)[k], k)
            xp[k, s, layer] = plane.astype(BF16)
            low = 0.0 if z_low is None else shifted(z_low, zero, k)
            high = 0.0 if z_high is None else shifted(z_high, zero, k)
            ex[0, s, layer, :, k * 128 : (k + 1) * 128] = jnp.where(
                lane < C1, plane[:, 256:384], low
            ).astype(BF16)
            ex[1, s, layer, :, k * 128 : (k + 1) * 128] = jnp.where(
                lane < C1, high, plane[:, 128:256]
            ).astype(BF16)

    def across(s, column):
        target = neigh[s, column]
        local = target - first
        return jnp.clip(local, 0, SLOTS - 1), local, (target >= 0).astype(F32)

    for s in range(SLOTS):
        ylow, _, ylow_on = across(s, 2)
        yhigh, _, yhigh_on = across(s, 3)
        zlow, _, zlow_on = across(s, 4)
        zhigh, _, zhigh_on = across(s, 5)

        def cell_layer(x, _):
            put_cells(
                s,
                x + 1,
                feat[s, x].astype(F32),
                feat[ylow, x].astype(F32)[BE - 1 : BE] * ylow_on,
                feat[yhigh, x].astype(F32)[0:1] * yhigh_on,
                feat[zlow, x, :, 384:512].astype(F32) * zlow_on,
                feat[zhigh, x, :, 0:128].astype(F32) * zhigh_on,
            )
            return 0

        lax.fori_loop(0, BE, cell_layer, 0, unroll=2)

    for finish_swap in end_swaps:
        finish_swap()

    put_cot(0, hc[0].astype(F32))
    put_cot(BE + 1, hc[1].astype(F32))
    for s in range(SLOTS):
        zero = jnp.zeros((1, BE * C1), F32)
        near, local, on = across(s, 0)
        inside = (local >= 0).astype(F32) * on
        outside = (local < 0).astype(F32) * on
        far = jnp.clip(local + SLOTS, 0, SLOTS - 1)
        plane = feat[near, BE - 1].astype(F32) * inside + hx[0, far].astype(F32) * outside
        put_cells(s, 0, plane, zero, zero, None, None)
        near, local, on = across(s, 1)
        inside = (local < SLOTS).astype(F32) * on
        outside = (local >= SLOTS).astype(F32) * on
        far = jnp.clip(local - SLOTS, 0, SLOTS - 1)
        plane = feat[near, 0].astype(F32) * inside + hx[1, far].astype(F32) * outside
        put_cells(s, BE + 1, plane, zero, zero, None, None)

    edge = jnp.concatenate([ec[k : k + BE].reshape(ROWS, 384) for k in range(3)], axis=1)
    from_edge = dot_t(edge, wct[...])
    for h in range(2):
        total = None
        for dx in range(3):
            for dy in range(3):
                window = cp[2 - dy, 2 - dx : 2 - dx + BE, :, h * 512 : (h + 1) * 512]
                term = dot_t(window.reshape(ROWS, 512), wc[dx * 3 + dy])
                total = term if total is None else total + term
        parts = [total[:, :128], total[:, 128:]]
        parts[1 - h] = parts[1 - h] + from_edge[:, h * 128 : (h + 1) * 128]
        for t in range(2):
            part = parts[t].reshape(2, 8, 2, 8, 128)
            for ox in range(2):
                for oy in range(2):
                    pg[ox * 4 + oy * 2 + h, :, :, t * 128 : (t + 1) * 128] = part[ox, :, oy]

    r = iota((256, 512), 0)
    l = iota((256, 512), 1)
    spread_z = ((l // 64 == r // 32) & (l % 32 == r % 32)).astype(BF16)
    r = iota((128, 64), 0)
    l = iota((128, 64), 1)
    spread_y = (r // 2 == l).astype(BF16)
    r = iota((64, 256), 0)
    l = iota((64, 256), 1)
    sum_xy = ((l // 32 == r // 8) & (l % 16 // 2 == r % 8)).astype(BF16)
    r = iota((256, 128), 0)
    l = iota((256, 128), 1)
    sum_z = ((r // 64 == l // 32) & (r % 32 == l % 32)).astype(F32)
    sum_z = (sum_z * 0.125).astype(BF16)

    grads = []
    for s in range(SLOTS):
        live = (coords[s, 0] >= 0).astype(F32)
        octant = lax.rem(coords[s, 0], 2) * 4 + coords[s, 1] * 2 + coords[s, 2]
        grads.append(pg[jnp.clip(octant, 0, 7)].reshape(64, 256) * (live * 0.125))
    grads = dot(jnp.concatenate(grads, axis=0).astype(BF16), spread_z).astype(BF16)
    for s in range(SLOTS):
        up[s] = dot(spread_y, grads[s * 64 : (s + 1) * 64]).reshape(8, BE, 512)

    def fine_act(s, _):
        for h in range(2):
            lanes = slice(h * 256, (h + 1) * 256)
            pieces = [
                xp[dy, s, dx : dx + BE, :, lanes].reshape(ROWS, 256)
                for dx in range(3)
                for dy in range(3)
            ]
            pieces += [ex[h, s, dx : dx + BE].reshape(ROWS, 384) for dx in range(3)]
            act = dot(jnp.concatenate(pieces, axis=1), wf[...])
            acts[s, :, :, lanes] = act.reshape(BE, BE, 256)
        return 0

    def fine_layer(i, _):
        s = i // BE
        x = lax.rem(i, BE)
        act = acts[s, x]
        sigma = 0.5 * jnp.tanh(0.5 * act) + 0.5
        gated = act * sigma
        hid[s, x] = (feat[s, x].astype(F32) + gated).astype(BF16)
        slope = sigma + gated * (1.0 - sigma)
        out_act[s, x] = (up[s, x // 2] * slope).astype(BF16)
        return 0

    for s in range(SLOTS + 1):
        if s < SLOTS:
            fine_act(s, 0)
        if s > 0:
            for x in range(BE):
                fine_layer((s - 1) * BE + x, 0)

    sums = jnp.concatenate([dot(sum_xy, hid[s].reshape(ROWS, 512)) for s in range(SLOTS)], axis=0)
    top = sums.astype(BF16)
    rest = (sums - top.astype(F32)).astype(BF16)
    for h in range(2):
        lanes = slice(h * 256, (h + 1) * 256)
        both = jnp.concatenate([top[:, lanes], rest[:, lanes]], axis=1)
        small = dot(both, jnp.concatenate([sum_z, sum_z], axis=0))
        ps[:, :, :, h * 128 : (h + 1) * 128] = small.reshape(SLOTS, 8, 8, 128)

    for t in range(8):
        slot = jnp.int32(0)
        on = jnp.int32(0)
        for s in range(SLOTS):
            octant = lax.rem(coords[s, 0], 2) * 4 + coords[s, 1] * 2 + coords[s, 2]
            here = ((coords[s, 0] >= 0) & (octant == t)).astype(jnp.int32)
            slot = slot + here * s
            on = on + here
        block = ps[jnp.clip(slot, 0, SLOTS - 1)] * on.astype(F32)
        ox, oy, oz = t // 4, t // 2 % 2, t % 2
        pool[ox * 8 : (ox + 1) * 8, oy * 8 : (oy + 1) * 8, oz * 256 : (oz + 1) * 256] = block
    ps_ends[0] = pool[0].astype(BF16)
    ps_ends[1] = pool[BE - 1].astype(BF16)
    end_pools = swap(ps_ends.at[1], ps_ends.at[0], hp, 4)

    def put_pool(layer, cells):
        lane = iota((BE, 128), 1)
        zero = jnp.zeros((1, BE * C1), F32)
        for k in range(3):
            plane = shifted(cells, zero, k)
            pp[k, layer] = plane.astype(BF16)
            ep[layer, :, k * 128 : (k + 1) * 128] = jnp.where(
                lane < C1, plane[:, 256:384], plane[:, 128:256]
            ).astype(BF16)

    def pool_layer(x, _):
        put_pool(x + 1, pool[x])
        return 0

    lax.fori_loop(0, BE, pool_layer, 0, unroll=2)

    save_act = pltpu.make_async_copy(out_act, act_hbm, out_sem.at[0])
    save_act.start()
    eye = eye_matrix(256)
    for i in range(2 * SLOTS):
        lanes = slice(i % 2 * 256, i % 2 * 256 + 256)
        gt[i] = dot_t(eye, out_act[i // 2, :, :, lanes].reshape(ROWS, 256)).astype(BF16)
    eye = eye_matrix(128)

    def turn(sums, width):
        copies = 128 // width
        count = 3 * C1 // copies
        rows = [sums[tap * width : (tap + 1) * width, :] for tap in range(9) for _ in range(copies)]
        flipped = dot_t(eye, jnp.concatenate(rows, axis=0))
        for tap in range(9):
            turned[tap * 128 : (tap + 1) * 128, :] = flipped[:, tap * 128 : (tap + 1) * 128]
        lane = iota((count, 128), 1) // width
        lines = []
        for tap in range(9):
            base = tap * 128
            picked = turned[pl.ds(base, count, stride=copies), :]
            for t in range(1, copies):
                picked = jnp.where(lane == t, turned[pl.ds(base + t, count, stride=copies), :], picked)
            lines.append(picked)
        return lines

    def fine_taps(dx):
        left = jnp.concatenate([gt[i] for i in range(8)], axis=1)
        border = jnp.concatenate(
            [jnp.concatenate([gt[i, 0:32, :], gt[i, 224:256, :]], axis=0) for i in range(8)], axis=1
        )
        edges = jnp.concatenate(
            [ex[i % 2, i // 2, dx : dx + BE].reshape(ROWS, 384) for i in range(8)], axis=0
        )
        edge = dot(border, edges)
        for dy in range(3):
            right = jnp.concatenate(
                [
                    xp[dy, i // 2, dx : dx + BE, :, i % 2 * 256 : i % 2 * 256 + 256].reshape(ROWS, 256)
                    for i in range(8)
                ],
                axis=0,
            )
            lanes = slice(dy * 128, (dy + 1) * 128)
            folded = fold_taps(dot(left, right), edge[:32, lanes], edge[32:, lanes], C1)
            tap = dx * 3 + dy
            sum_f[tap * C1 : (tap + 1) * C1, :] = folded.astype(BF16)

    def coarse_taps(dx):
        left = jnp.concatenate([ct[0:512, :], ct[512:1024, :]], axis=1)
        edge = dot(ct[448:576, :], ep[dx : dx + BE].reshape(ROWS, 384))
        for dy in range(3):
            window = pp[dy, dx : dx + BE].reshape(ROWS, 512)
            right = jnp.concatenate([window[:, :256], window[:, 256:]], axis=0)
            lanes = slice(dy * 128, (dy + 1) * 128)
            folded = fold_taps(dot(left, right), edge[64:, lanes], edge[:64, lanes], C2)
            tap = dx * 3 + dy
            sum_c[tap * C2 : (tap + 1) * C2, :] = folded.astype(BF16)

    def all_of(ref, send, recv):
        return pltpu.make_async_remote_copy(
            src_ref=ref, dst_ref=ref, send_sem=send, recv_sem=recv, device_id=next_id, device_id_type=MESH
        )

    def shard(i, rows):
        return pl.ds(pl.multiple_of(i * rows, rows), rows)

    def spread(red, got, rows, send, recv):
        for j, (other, device) in enumerate(a_peers):
            remote(red.at[shard(other, rows)], got.at[j], send.at[0], recv.at[0], device)
        return all_of(got, send.at[0], recv.at[0])

    def exchange(copies, red, got, mid, rows, send, recv):
        copies.wait_recv()
        total = red[shard(a, rows), :].astype(F32)
        for j in range(na - 1):
            total = total + got[j].astype(F32)
        mid[q] = total.astype(BF16)
        for device in q_peers:
            remote(mid.at[q], mid.at[q], send.at[1], recv.at[1], device)
        return all_of(mid.at[0 : nq - 1], send.at[1], recv.at[1])

    def gather(copies, mid, full, rows, send, recv):
        copies.wait_recv()
        total = mid[0].astype(F32)
        for j in range(1, nq):
            total = total + mid[j].astype(F32)
        part = shard(a, rows)
        full[part, :] = total.astype(BF16)
        for _, device in a_peers:
            remote(full.at[part], full.at[part], send.at[2], recv.at[2], device)
        return all_of(full.at[0 : (na - 1) * rows], send.at[2], recv.at[2])

    def finish(copies, full, out, count):
        copies.wait_recv()
        folds[: 9 * count, :] = full[: 9 * count, :].astype(F32)
        for dx in range(3):
            for j in range(count):
                out[dx, :, j * 128 : (j + 1) * 128] = folds[pl.ds(dx * 3 * count + j, 3, stride=count), :]

    fine_taps(0)
    fine_taps(1)
    fine_taps(2)
    rows = turn(sum_f, C1) + [jnp.zeros((na * fine_rows - 216, 128), F32)]
    red_f[...] = jnp.concatenate(rows, axis=0).astype(BF16)
    f1 = spread(red_f, got_f, fine_rows, send_f, recv_f)
    end_pools()
    put_pool(0, hp[0].astype(F32))
    put_pool(BE + 1, hp[1].astype(F32))
    for dx in range(3):
        coarse_taps(dx)
    for tap, rows in enumerate(turn(sum_c, C2)):
        red_c[tap * 48 : (tap + 1) * 48, :] = rows.astype(BF16)
    if na * coarse_rows > 432:
        red_c[432:, :] = jnp.zeros((na * coarse_rows - 432, 128), BF16)
    c1 = spread(red_c, got_c, coarse_rows, send_c, recv_c)
    f2 = exchange(f1, red_f, got_f, mid_f, fine_rows, send_f, recv_f)
    edge = jnp.concatenate([ep[k : k + BE].reshape(ROWS, 384) for k in range(3)], axis=1)
    from_edge = dot(edge, wce[...])
    for h in range(2):
        pieces = [
            pp[dy, dx : dx + BE, :, h * 256 : (h + 1) * 256].reshape(ROWS, 256)
            for dx in range(3)
            for dy in range(3)
        ]
        total = dot(jnp.concatenate(pieces, axis=1), wc[...].reshape(9 * 256, 512))
        parts = [total[:, t * 128 : (t + 1) * 128] for t in range(4)]
        parts[3 if h == 0 else 0] += from_edge[:, h * 128 : (h + 1) * 128]
        for t in range(4):
            base = h * 512 + t * 128
            out_coarse[0, :, :, base : base + 128] = parts[t].astype(BF16).reshape(BE, BE, 128)
    save_coarse = pltpu.make_async_copy(out_coarse, coarse_hbm, out_sem.at[1])
    save_coarse.start()
    c2 = exchange(c1, red_c, got_c, mid_c, coarse_rows, send_c, recv_c)
    f3 = gather(f2, mid_f, all_f, fine_rows, send_f, recv_f)
    c3 = gather(c2, mid_c, all_c, coarse_rows, send_c, recv_c)
    finish(f3, all_f, out_fine_grad, 24)
    finish(c3, all_c, out_coarse_grad, 48)
    for copy in (f1, f2, f3, c1, c2, c3):
        copy.wait_send()
    save_act.wait()
    save_coarse.wait()


def hand_over(
    scale, coarse, fine_grad, coarse_grad, act, out_coarse, out_fine_grad, out_coarse_grad, out_cell,
    narrow, wide, keep_coarse, keep_f, keep_c, in_sem, out_sem, other_sem,
):
    half = BE // 2
    cuts = [(s, slice(h * half, (h + 1) * half)) for s in range(SLOTS) for h in range(2)]
    ins = [pltpu.make_async_copy(act.at[c], narrow.at[c], in_sem.at[i]) for i, c in enumerate(cuts)]
    outs = [pltpu.make_async_copy(wide.at[c], out_cell.at[c], out_sem.at[i]) for i, c in enumerate(cuts)]
    pairs = ((coarse, keep_coarse, out_coarse), (fine_grad, keep_f, out_fine_grad), (coarse_grad, keep_c, out_coarse_grad))
    first = [pltpu.make_async_copy(a, b, other_sem.at[i]) for i, (a, b, _) in enumerate(pairs)]
    second = [pltpu.make_async_copy(b, c, other_sem.at[i + 3]) for i, (_, b, c) in enumerate(pairs)]
    for copy in ins + first:
        copy.start()
    for i, cut in enumerate(cuts):
        ins[i].wait()
        wide[cut] = narrow[cut].astype(F32) * scale
        outs[i].start()
        if i in (3, 5, 7):
            first[i // 2 - 1].wait()
            second[i // 2 - 1].start()
    for copy in outs + second:
        copy.wait()


def on_device(nb, ns, features, coords, neighbours, fine_weight, coarse_weight, cotangent):
    nq = 8 if nb % 16 == 0 else min(nb, 2)
    na = nb * ns // nq
    fine_rows = -(-216 // (na * 16)) * 16
    coarse_rows = -(-432 // (na * 16)) * 16
    vmem = pl.BlockSpec(memory_space=pltpu.VMEM)
    smem = pl.BlockSpec(memory_space=pltpu.SMEM)
    hbm = pl.BlockSpec(memory_space=pl.ANY)
    dma = pltpu.SemaphoreType.DMA
    coarse_out, fine_grad, coarse_grad, act_grad = pl.pallas_call(
        functools.partial(body, nb, ns, nq, fine_rows, coarse_rows),
        out_shape=(
            jax.ShapeDtypeStruct((1, BE, BE, BE * C2), BF16),
            jax.ShapeDtypeStruct((3, 3, 3 * C1 * C1), F32),
            jax.ShapeDtypeStruct((3, 3, 3 * C1 * C2), F32),
            jax.ShapeDtypeStruct((SLOTS, BE, BE, BE * C1), BF16),
        ),
        in_specs=[smem, smem, hbm, hbm, hbm, hbm],
        out_specs=(hbm, vmem, vmem, hbm),
        scratch_shapes=[
            pltpu.VMEM((SLOTS, BE, BE, BE * C1), BF16),
            pltpu.VMEM((3, 3, 3 * C1 * C1), BF16),
            pltpu.VMEM((3, 3, 3 * C1 * C2), BF16),
            pltpu.VMEM((1, BE, BE, BE * C2), BF16),
            pltpu.VMEM((1, BE, BE, BE * C2), BF16),
            pltpu.VMEM((SLOTS, BE, BE, BE * C1), BF16),
            pltpu.VMEM((2, SLOTS, BE, BE * C1), BF16),
            pltpu.VMEM((2, BE, BE * C2), BF16),
            pltpu.VMEM((2, BE, BE * C1), BF16),
            pltpu.VMEM((2, BE, BE * C1), BF16),
            pltpu.VMEM((3, SLOTS, BE + 2, BE, BE * C1), BF16),
            pltpu.VMEM((2, SLOTS, BE + 2, BE, 384), BF16),
            pltpu.VMEM((9 * 256 + 9 * 128, 256), BF16),
            pltpu.VMEM((9, 256, 512), BF16),
            pltpu.VMEM((9 * 128, 256), BF16),
            pltpu.VMEM((256, 9 * 128), BF16),
            pltpu.VMEM((3, BE + 2, BE, BE * C2), BF16),
            pltpu.VMEM((BE + 2, BE, 384), BF16),
            pltpu.VMEM((8, 8, 8, 256), F32),
            pltpu.VMEM((SLOTS, 8, BE, 512), F32),
            pltpu.VMEM((SLOTS, BE, BE, 512), F32),
            pltpu.VMEM((SLOTS, BE, BE, 512), BF16),
            pltpu.VMEM((2 * SLOTS, 256, 256), BF16),
            pltpu.VMEM((BE * C2, ROWS), BF16),
            pltpu.VMEM((SLOTS, 8, 8, 256), F32),
            pltpu.VMEM((BE, BE, BE * C1), F32),
            pltpu.VMEM((3, BE + 2, BE, BE * C1), BF16),
            pltpu.VMEM((BE + 2, BE, 384), BF16),
            pltpu.VMEM((432, 128), F32),
            pltpu.VMEM((9 * 128, 128), F32),
            pltpu.VMEM((9 * C1, 128), BF16),
            pltpu.VMEM((9 * C2, 128), BF16),
            pltpu.VMEM((na * fine_rows, 128), BF16),
            pltpu.VMEM((na * coarse_rows, 128), BF16),
            pltpu.VMEM((na - 1, fine_rows, 128), BF16),
            pltpu.VMEM((na - 1, coarse_rows, 128), BF16),
            pltpu.VMEM((nq, fine_rows, 128), BF16),
            pltpu.VMEM((nq, coarse_rows, 128), BF16),
            pltpu.VMEM((na * fine_rows, 128), BF16),
            pltpu.VMEM((na * coarse_rows, 128), BF16),
            dma((6,)), dma((6,)),
            dma((3,)), dma((3,)), dma((3,)), dma((3,)), dma((2,)), dma((4,)),
        ],
        compiler_params=pltpu.CompilerParams(
            collective_id=0, has_side_effects=True, vmem_limit_bytes=58 * 1024 * 1024
        ),
        name="unet_level",
    )(coords, neighbours, features, fine_weight, coarse_weight, cotangent)
    scale = float(nb * ns * BE**3) ** 0.5
    return pl.pallas_call(
        functools.partial(hand_over, scale),
        out_shape=(
            jax.ShapeDtypeStruct(coarse_out.shape, BF16),
            jax.ShapeDtypeStruct(fine_grad.shape, F32),
            jax.ShapeDtypeStruct(coarse_grad.shape, F32),
            jax.ShapeDtypeStruct(act_grad.shape, F32),
        ),
        in_specs=[hbm] * 4,
        out_specs=(hbm,) * 4,
        scratch_shapes=[
            pltpu.VMEM(act_grad.shape, BF16),
            pltpu.VMEM(act_grad.shape, F32),
            pltpu.VMEM(coarse_out.shape, BF16),
            pltpu.VMEM(fine_grad.shape, F32),
            pltpu.VMEM(coarse_grad.shape, F32),
            dma((2 * SLOTS,)), dma((2 * SLOTS,)), dma((6,)),
        ],
        compiler_params=pltpu.CompilerParams(vmem_limit_bytes=58 * 1024 * 1024),
        name="hand_over",
    )(coarse_out, fine_grad, coarse_grad, act_grad)


def solution(mesh):
    nb, ns = mesh.shape["blocks"], mesh.shape["sub"]
    split = P(("blocks", "sub"), None, None, None)
    return jax.shard_map(
        functools.partial(on_device, nb, ns),
        mesh=mesh,
        in_specs=(split, P(("blocks", "sub"), None), P(("blocks", "sub"), None), P(), P(), split),
        out_specs=(split, P(), P(), split),
        check_vma=False,
    )
```

```python
import functools

import jax
import jax.numpy as jnp
from jax import lax
from jax.experimental import pallas as pl
from jax.experimental.pallas import tpu as pltpu
from jax.sharding import PartitionSpec as P

BE = 16
C1 = 32
C2 = 64
SLOTS = 4
ROWS = BE * BE
MESH = pl.DeviceIdType.MESH
F32 = jnp.float32
BF16 = jnp.bfloat16


def iota(shape, dim):
    return lax.broadcasted_iota(jnp.int32, shape, dim)


def eye_matrix(size):
    return (iota((size, size), 0) == iota((size, size), 1)).astype(BF16)


def dot(a, b):
    return jnp.dot(a, b, preferred_element_type=F32)


def dot_t(a, b):
    return lax.dot_general(a, b, (((1,), (1,)), ((), ())), preferred_element_type=F32)


def shifted(cells, row, k):
    if k == 1:
        return cells
    sub = iota(cells.shape, 0)
    if k == 0:
        return jnp.where(sub == 0, row, pltpu.roll(cells, 1, 0))
    return jnp.where(sub == BE - 1, row, pltpu.roll(cells, BE - 1, 0))


def tiled_weight(row, width):
    per_tile = 128 // width
    groups = []
    sub = iota((8, 128), 0)
    lane = iota((8, 128), 1)
    for g in range(C1 // 8):
        first = g * 8 // per_tile
        picked = row[:, first * 128 : (first + 1) * 128]
        picked = jnp.broadcast_to(picked, (8, 128))
        for t in range(1, 8 // per_tile):
            tile = row[:, (first + t) * 128 : (first + t + 1) * 128]
            picked = jnp.where(sub // per_tile == t, tile, picked)
        groups.append(jnp.where(lane // width == sub % per_tile, picked, 0.0))
    tiled = jnp.concatenate(groups, axis=0)
    step = 64
    while step >= width:
        tiled = tiled + pltpu.roll(tiled, step, 1)
        step //= 2
    return tiled


def fold_taps(block, edge_low, edge_high, width):
    quarter = iota((width, 128), 1) // C1
    total = None
    for cls in range(4):
        part = None
        for z_out in (cls, cls + 4):
            rows = block[z_out * width : (z_out + 1) * width]
            tiles = [rows[:, :128], rows[:, 128:]]
            if z_out == 0:
                picked = jnp.where(quarter == 3, edge_low, tiles[0])
            elif z_out == 7:
                picked = jnp.where(quarter == 0, edge_high, tiles[1])
            elif z_out == 3:
                picked = jnp.where(quarter == 0, tiles[1], tiles[0])
            elif z_out == 4:
                picked = jnp.where(quarter == 3, tiles[0], tiles[1])
            else:
                picked = tiles[z_out // 4]
            part = picked if part is None else part + picked
        shift = (1 - cls) % 4 * C1
        if shift:
            part = pltpu.roll(part, shift, 1)
        total = part if total is None else total + part
    return jnp.where(quarter < 3, total, 0.0)


def body(
    nb, ns, nq, fine_rows, coarse_rows,
    coords, neigh, feat_hbm, fw_hbm, cw_hbm, cot_hbm,
    out_coarse, out_fine_grad, out_coarse_grad, out_act,
    feat, fw, cw, cot, hx, hc, hp, ps_ends, xp, ex, wf, wc, wce, wct, cp, ec, pg, up, acts, hid, gt, ct, ps, pool, pp, ep,
    folds, turned, sum_f, sum_c, red_f, red_c, got_f, got_c, mid_f, mid_c, all_f, all_c,
    halo_send, halo_recv, send_f, recv_f, send_c, recv_c, in_sem,
):
    loads = [
        pltpu.make_async_copy(src, dst, in_sem.at[i])
        for i, (src, dst) in enumerate(((fw_hbm, fw), (cw_hbm, cw), (cot_hbm, cot), (feat_hbm, feat)))
    ]
    for copy in loads:
        copy.start()

    i0 = lax.axis_index("blocks")
    i1 = lax.axis_index("sub")
    count = nb * ns
    me = i0 * ns + i1
    nxt = lax.rem(me + 1, count)
    prv = lax.rem(me + count - 1, count)
    prev_id = (prv // ns, lax.rem(prv, ns))
    next_id = (nxt // ns, lax.rem(nxt, ns))
    na = count // nq
    q = lax.rem(i0, nq)
    a = (i0 // nq) * ns + i1

    nz = nb // nq
    zs = [lax.rem(i0 // nq + k, nz) for k in range(nz)]
    ys = [lax.rem(i1 + k, ns) for k in range(ns)]
    blocks = [z * nq + q for z in zs]
    def way(k, size):
        return min(k, size - k)

    offsets = [(k, m) for k in range(nz) for m in range(ns) if k + m > 0]
    offsets.sort(key=lambda o: -way(o[0], nz) - way(o[1], ns))
    a_peers = [(zs[k] * ns + ys[m], (blocks[k], ys[m])) for k, m in offsets]
    nx = nq // 2
    xs = [lax.rem(q // 2 + k, nx) * 2 for k in range(nx)]
    cores = [lax.rem(q + k, 2) for k in range(2)]
    offsets = [(k, m) for k in range(nx) for m in range(2) if k + m > 0]
    offsets.sort(key=lambda o: -way(o[0], nx) - o[1])
    q_peers = [(i0 - q + xs[k] + cores[m], i1) for k, m in offsets]

    barrier = pltpu.get_barrier_semaphore()

    def greet(device):
        pl.semaphore_signal(barrier, inc=1, device_id=device, device_id_type=MESH)

    has_prev = me > 0
    has_next = me < count - 1
    pl.when(has_prev)(lambda: greet(prev_id))
    pl.when(has_next)(lambda: greet(next_id))
    for _, device in a_peers:
        greet(device)
    for device in q_peers:
        greet(device)

    def describe(src, dst, send, recv, device):
        return pltpu.make_async_remote_copy(
            src_ref=src, dst_ref=dst, send_sem=send, recv_sem=recv, device_id=device, device_id_type=MESH
        )

    def remote(src, dst, send, recv, device):
        describe(src, dst, send, recv, device).start()

    def swap(high, low, dst, k):
        up = describe(high, dst.at[0], halo_send.at[k], halo_recv.at[k], next_id)
        down = describe(low, dst.at[1], halo_send.at[k + 1], halo_recv.at[k + 1], prev_id)
        pl.when(has_next)(up.start)
        pl.when(has_prev)(down.start)

        def clear(side):
            dst[side] = jnp.zeros(dst.shape[1:], dst.dtype)

        def finish_swap():
            pl.when(has_prev)(up.wait_recv)
            pl.when(has_next)(down.wait_recv)
            pl.when(has_next)(up.wait_send)
            pl.when(has_prev)(down.wait_send)
            pl.when(jnp.logical_not(has_prev))(lambda: clear(0))
            pl.when(jnp.logical_not(has_next))(lambda: clear(1))

        return finish_swap

    loads[0].wait()
    loads[1].wait()
    first = me * SLOTS
    quarter8 = iota((C1, 256), 1) // C1
    half8 = iota((C1, 512), 1) // C2
    half4 = iota((C1, 256), 1) // C2
    half2 = iota((C1, 128), 1) // C2
    zeros = jnp.zeros((2 * C1, 256), BF16)
    for dx in range(3):
        for dy in range(3):
            tap = dx * 3 + dy
            row_f = fw[dx, dy : dy + 1, :].astype(F32)
            tiles = []
            for dz in range(3):
                t = tiled_weight(row_f[:, dz * C1 * C1 : (dz + 1) * C1 * C1], C1)
                tiles.append(jnp.concatenate([t, t], axis=1))
            for z_in in range(8):
                line = jnp.where(quarter8 == z_in, tiles[1], 0.0)
                line = jnp.where(quarter8 == z_in + 1, tiles[0], line)
                line = jnp.where(quarter8 == z_in - 1, tiles[2], line)
                wf[tap * 256 + z_in * C1 : tap * 256 + (z_in + 1) * C1, :] = line.astype(BF16)
            base = 2304 + dx * 384 + dy * 128
            wf[base : base + 32, :] = jnp.where(quarter8 == 7, tiles[2], 0.0).astype(BF16)
            wf[base + 32 : base + 96, :] = zeros
            wf[base + 96 : base + 128, :] = jnp.where(quarter8 == 0, tiles[0], 0.0).astype(BF16)

            row_c = cw[dx, dy : dy + 1, :].astype(F32)
            narrow = [
                tiled_weight(row_c[:, dz * C1 * C2 : (dz + 1) * C1 * C2], C2) for dz in range(3)
            ]
            wide = [jnp.concatenate([t] * 4, axis=1) for t in narrow]
            for z_in in range(8):
                line = jnp.where(half8 == z_in, wide[1], 0.0)
                line = jnp.where(half8 == z_in + 1, wide[0], line)
                line = jnp.where(half8 == z_in - 1, wide[2], line)
                wc[tap, z_in * C1 : (z_in + 1) * C1, :] = line.astype(BF16)
            base = dx * 384 + dy * 128
            pair = [jnp.concatenate([t] * 2, axis=1) for t in narrow]
            wce[base : base + 32, :] = jnp.where(half4 == 1, pair[2], 0.0).astype(BF16)
            wce[base + 32 : base + 96, :] = zeros
            wce[base + 96 : base + 128, :] = jnp.where(half4 == 2, pair[0], 0.0).astype(BF16)
            base = (2 - dx) * 384 + (2 - dy) * 128
            wct[0:96, base : base + 128] = jnp.zeros((96, 128), BF16)
            wct[96:128, base : base + 128] = jnp.where(half2 == 0, narrow[0], 0.0).astype(BF16)
            wct[128:160, base : base + 128] = jnp.where(half2 == 1, narrow[2], 0.0).astype(BF16)
            wct[160:256, base : base + 128] = jnp.zeros((96, 128), BF16)

    eye = eye_matrix(256)

    loads[2].wait()
    loads[3].wait()
    pl.semaphore_wait(barrier, na + nq - 2 + has_prev.astype(jnp.int32) + has_next.astype(jnp.int32))
    end_swaps = [
        swap(feat.at[:, BE - 1], feat.at[:, 0], hx, 0),
        swap(cot.at[0, BE - 1], cot.at[0, 0], hc, 2),
    ]
    flat_cot = cot[0].reshape(ROWS, BE * C2)
    for j in range(4):
        ct[j * 256 : (j + 1) * 256, :] = dot_t(eye, flat_cot[:, j * 256 : (j + 1) * 256]).astype(BF16)

    def put_cot(layer, cells):
        lane = iota((BE, 128), 1)
        zero = jnp.zeros((1, BE * C2), F32)
        for k in range(3):
            plane = shifted(cells, zero, k)
            cp[k, layer] = plane.astype(BF16)
            ec[layer, :, k * 128 : (k + 1) * 128] = jnp.where(
                lane < C2, plane[:, 512:640], plane[:, 384:512]
            ).astype(BF16)

    def cot_layer(x, _):
        put_cot(x + 1, cot[0, x].astype(F32))
        return 0

    for x in range(BE):
        cot_layer(x, 0)

    def put_cells(s, layer, cells, row_low, row_high, z_low, z_high):
        lane = iota((BE, 128), 1)
        zero = jnp.zeros((1, 128), F32)
        for k in range(3):
            plane = shifted(cells, (row_low, None, row_high)[k], k)
            xp[k, s, layer] = plane.astype(BF16)
            low = 0.0 if z_low is None else shifted(z_low, zero, k)
            high = 0.0 if z_high is None else shifted(z_high, zero, k)
            ex[0, s, layer, :, k * 128 : (k + 1) * 128] = jnp.where(
                lane < C1, plane[:, 256:384], low
            ).astype(BF16)
            ex[1, s, layer, :, k * 128 : (k + 1) * 128] = jnp.where(
                lane < C1, high, plane[:, 128:256]
            ).astype(BF16)

    def across(s, column):
        target = neigh[s, column]
        local = target - first
        return jnp.clip(local, 0, SLOTS - 1), local, (target >= 0).astype(F32)

    for s in range(SLOTS):
        ylow, _, ylow_on = across(s, 2)
        yhigh, _, yhigh_on = across(s, 3)
        zlow, _, zlow_on = across(s, 4)
        zhigh, _, zhigh_on = across(s, 5)

        def cell_layer(x, _):
            put_cells(
                s,
                x + 1,
                feat[s, x].astype(F32),
                feat[ylow, x].astype(F32)[BE - 1 : BE] * ylow_on,
                feat[yhigh, x].astype(F32)[0:1] * yhigh_on,
                feat[zlow, x, :, 384:512].astype(F32) * zlow_on,
                feat[zhigh, x, :, 0:128].astype(F32) * zhigh_on,
            )
            return 0

        for x in range(BE):
            cell_layer(x, 0)

    for finish_swap in end_swaps:
        finish_swap()

    put_cot(0, hc[0].astype(F32))
    put_cot(BE + 1, hc[1].astype(F32))
    for s in range(SLOTS):
        zero = jnp.zeros((1, BE * C1), F32)
        near, local, on = across(s, 0)
        inside = (local >= 0).astype(F32) * on
        outside = (local < 0).astype(F32) * on
        far = jnp.clip(local + SLOTS, 0, SLOTS - 1)
        plane = feat[near, BE - 1].astype(F32) * inside + hx[0, far].astype(F32) * outside
        put_cells(s, 0, plane, zero, zero, None, None)
        near, local, on = across(s, 1)
        inside = (local < SLOTS).astype(F32) * on
        outside = (local >= SLOTS).astype(F32) * on
        far = jnp.clip(local - SLOTS, 0, SLOTS - 1)
        plane = feat[near, 0].astype(F32) * inside + hx[1, far].astype(F32) * outside
        put_cells(s, BE + 1, plane, zero, zero, None, None)

    edge = jnp.concatenate([ec[k : k + BE].reshape(ROWS, 384) for k in range(3)], axis=1)
    from_edge = dot_t(edge, wct[...])
    for h in range(2):
        total = None
        for dx in range(3):
            for dy in range(3):
                window = cp[2 - dy, 2 - dx : 2 - dx + BE, :, h * 512 : (h + 1) * 512]
                term = dot_t(window.reshape(ROWS, 512), wc[dx * 3 + dy])
                total = term if total is None else total + term
        parts = [total[:, :128], total[:, 128:]]
        parts[1 - h] = parts[1 - h] + from_edge[:, h * 128 : (h + 1) * 128]
        for t in range(2):
            part = parts[t].reshape(2, 8, 2, 8, 128)
            for ox in range(2):
                for oy in range(2):
                    pg[ox * 4 + oy * 2 + h, :, :, t * 128 : (t + 1) * 128] = part[ox, :, oy]

    r = iota((256, 512), 0)
    l = iota((256, 512), 1)
    spread_z = ((l // 64 == r // 32) & (l % 32 == r % 32)).astype(BF16)
    r = iota((128, 64), 0)
    l = iota((128, 64), 1)
    spread_y = (r // 2 == l).astype(BF16)
    r = iota((64, 256), 0)
    l = iota((64, 256), 1)
    sum_xy = ((l // 32 == r // 8) & (l % 16 // 2 == r % 8)).astype(BF16)
    r = iota((256, 128), 0)
    l = iota((256, 128), 1)
    sum_z = ((r // 64 == l // 32) & (r % 32 == l % 32)).astype(F32)
    sum_z = (sum_z * 0.125).astype(BF16)

    grads = []
    for s in range(SLOTS):
        live = (coords[s, 0] >= 0).astype(F32)
        octant = lax.rem(coords[s, 0], 2) * 4 + coords[s, 1] * 2 + coords[s, 2]
        grads.append(pg[jnp.clip(octant, 0, 7)].reshape(64, 256) * (live * 0.125))
    grads = dot(jnp.concatenate(grads, axis=0).astype(BF16), spread_z).astype(BF16)
    for s in range(SLOTS):
        up[s] = dot(spread_y, grads[s * 64 : (s + 1) * 64]).reshape(8, BE, 512)

    def fine_act(s, _):
        for h in range(2):
            lanes = slice(h * 256, (h + 1) * 256)
            pieces = [
                xp[dy, s, dx : dx + BE, :, lanes].reshape(ROWS, 256)
                for dx in range(3)
                for dy in range(3)
            ]
            pieces += [ex[h, s, dx : dx + BE].reshape(ROWS, 384) for dx in range(3)]
            act = dot(jnp.concatenate(pieces, axis=1), wf[...])
            acts[s, :, :, lanes] = act.reshape(BE, BE, 256)
        return 0

    def fine_layer(i, _):
        s = i // BE
        x = lax.rem(i, BE)
        act = acts[s, x]
        sigma = 0.5 * jnp.tanh(0.5 * act) + 0.5
        gated = act * sigma
        hid[s, x] = (feat[s, x].astype(F32) + gated).astype(BF16)
        slope = sigma + gated * (1.0 - sigma)
        out_act[s, x] = (up[s, x // 2] * slope).astype(BF16)
        return 0

    for s in range(SLOTS + 1):
        if s < SLOTS:
            fine_act(s, 0)
        if s > 0:
            for x in range(BE):
                fine_layer((s - 1) * BE + x, 0)

    sums = jnp.concatenate([dot(sum_xy, hid[s].reshape(ROWS, 512)) for s in range(SLOTS)], axis=0)
    top = sums.astype(BF16)
    rest = (sums - top.astype(F32)).astype(BF16)
    for h in range(2):
        lanes = slice(h * 256, (h + 1) * 256)
        both = jnp.concatenate([top[:, lanes], rest[:, lanes]], axis=1)
        small = dot(both, jnp.concatenate([sum_z, sum_z], axis=0))
        ps[:, :, :, h * 128 : (h + 1) * 128] = small.reshape(SLOTS, 8, 8, 128)

    for t in range(8):
        slot = jnp.int32(0)
        on = jnp.int32(0)
        for s in range(SLOTS):
            octant = lax.rem(coords[s, 0], 2) * 4 + coords[s, 1] * 2 + coords[s, 2]
            here = ((coords[s, 0] >= 0) & (octant == t)).astype(jnp.int32)
            slot = slot + here * s
            on = on + here
        block = ps[jnp.clip(slot, 0, SLOTS - 1)] * on.astype(F32)
        ox, oy, oz = t // 4, t // 2 % 2, t % 2
        pool[ox * 8 : (ox + 1) * 8, oy * 8 : (oy + 1) * 8, oz * 256 : (oz + 1) * 256] = block
    ps_ends[0] = pool[0].astype(BF16)
    ps_ends[1] = pool[BE - 1].astype(BF16)
    end_pools = swap(ps_ends.at[1], ps_ends.at[0], hp, 4)

    def put_pool(layer, cells):
        lane = iota((BE, 128), 1)
        zero = jnp.zeros((1, BE * C1), F32)
        for k in range(3):
            plane = shifted(cells, zero, k)
            pp[k, layer] = plane.astype(BF16)
            ep[layer, :, k * 128 : (k + 1) * 128] = jnp.where(
                lane < C1, plane[:, 256:384], plane[:, 128:256]
            ).astype(BF16)

    def pool_layer(x, _):
        put_pool(x + 1, pool[x])
        return 0

    for x in range(BE):
        pool_layer(x, 0)

    eye = eye_matrix(256)
    for i in range(2 * SLOTS):
        lanes = slice(i % 2 * 256, i % 2 * 256 + 256)
        gt[i] = dot_t(eye, out_act[i // 2, :, :, lanes].reshape(ROWS, 256)).astype(BF16)
    eye = eye_matrix(128)

    def turn(sums, width):
        copies = 128 // width
        count = 3 * C1 // copies
        rows = [sums[tap * width : (tap + 1) * width, :] for tap in range(9) for _ in range(copies)]
        flipped = dot_t(eye, jnp.concatenate(rows, axis=0))
        for tap in range(9):
            turned[tap * 128 : (tap + 1) * 128, :] = flipped[:, tap * 128 : (tap + 1) * 128]
        lane = iota((count, 128), 1) // width
        lines = []
        for tap in range(9):
            base = tap * 128
            picked = turned[pl.ds(base, count, stride=copies), :]
            for t in range(1, copies):
                picked = jnp.where(lane == t, turned[pl.ds(base + t, count, stride=copies), :], picked)
            lines.append(picked)
        return lines

    def fine_taps(dx):
        left = jnp.concatenate([gt[i] for i in range(8)], axis=1)
        border = jnp.concatenate(
            [jnp.concatenate([gt[i, 0:32, :], gt[i, 224:256, :]], axis=0) for i in range(8)], axis=1
        )
        edges = jnp.concatenate(
            [ex[i % 2, i // 2, dx : dx + BE].reshape(ROWS, 384) for i in range(8)], axis=0
        )
        edge = dot(border, edges)
        for dy in range(3):
            right = jnp.concatenate(
                [
                    xp[dy, i // 2, dx : dx + BE, :, i % 2 * 256 : i % 2 * 256 + 256].reshape(ROWS, 256)
                    for i in range(8)
                ],
                axis=0,
            )
            lanes = slice(dy * 128, (dy + 1) * 128)
            folded = fold_taps(dot(left, right), edge[:32, lanes], edge[32:, lanes], C1)
            tap = dx * 3 + dy
            sum_f[tap * C1 : (tap + 1) * C1, :] = folded.astype(BF16)

    def coarse_taps(dx):
        left = jnp.concatenate([ct[0:512, :], ct[512:1024, :]], axis=1)
        edge = dot(ct[448:576, :], ep[dx : dx + BE].reshape(ROWS, 384))
        for dy in range(3):
            window = pp[dy, dx : dx + BE].reshape(ROWS, 512)
            right = jnp.concatenate([window[:, :256], window[:, 256:]], axis=0)
            lanes = slice(dy * 128, (dy + 1) * 128)
            folded = fold_taps(dot(left, right), edge[64:, lanes], edge[:64, lanes], C2)
            tap = dx * 3 + dy
            sum_c[tap * C2 : (tap + 1) * C2, :] = folded.astype(BF16)

    def all_of(ref, send, recv):
        return pltpu.make_async_remote_copy(
            src_ref=ref, dst_ref=ref, send_sem=send, recv_sem=recv, device_id=next_id, device_id_type=MESH
        )

    def shard(i, rows):
        return pl.ds(pl.multiple_of(i * rows, rows), rows)

    def spread(red, got, rows, send, recv):
        for j, (other, device) in enumerate(a_peers):
            remote(red.at[shard(other, rows)], got.at[j], send.at[0], recv.at[0], device)
        return all_of(got, send.at[0], recv.at[0])

    def exchange(copies, red, got, mid, rows, send, recv):
        copies.wait_recv()
        total = red[shard(a, rows), :].astype(F32)
        for j in range(na - 1):
            total = total + got[j].astype(F32)
        mid[q] = total.astype(BF16)
        for device in q_peers:
            remote(mid.at[q], mid.at[q], send.at[1], recv.at[1], device)
        return all_of(mid.at[0 : nq - 1], send.at[1], recv.at[1])

    def gather(copies, mid, full, rows, send, recv):
        copies.wait_recv()
        total = mid[0].astype(F32)
        for j in range(1, nq):
            total = total + mid[j].astype(F32)
        part = shard(a, rows)
        full[part, :] = total.astype(BF16)
        for _, device in a_peers:
            remote(full.at[part], full.at[part], send.at[2], recv.at[2], device)
        return all_of(full.at[0 : (na - 1) * rows], send.at[2], recv.at[2])

    def finish(copies, full, out, count):
        copies.wait_recv()
        folds[: 9 * count, :] = full[: 9 * count, :].astype(F32)
        for dx in range(3):
            for j in range(count):
                out[dx, :, j * 128 : (j + 1) * 128] = folds[pl.ds(dx * 3 * count + j, 3, stride=count), :]

    fine_taps(0)
    fine_taps(1)
    fine_taps(2)
    rows = turn(sum_f, C1) + [jnp.zeros((na * fine_rows - 216, 128), F32)]
    red_f[...] = jnp.concatenate(rows, axis=0).astype(BF16)
    f1 = spread(red_f, got_f, fine_rows, send_f, recv_f)
    end_pools()
    put_pool(0, hp[0].astype(F32))
    put_pool(BE + 1, hp[1].astype(F32))
    for dx in range(3):
        coarse_taps(dx)
    for tap, rows in enumerate(turn(sum_c, C2)):
        red_c[tap * 48 : (tap + 1) * 48, :] = rows.astype(BF16)
    if na * coarse_rows > 432:
        red_c[432:, :] = jnp.zeros((na * coarse_rows - 432, 128), BF16)
    c1 = spread(red_c, got_c, coarse_rows, send_c, recv_c)
    f2 = exchange(f1, red_f, got_f, mid_f, fine_rows, send_f, recv_f)
    edge = jnp.concatenate([ep[k : k + BE].reshape(ROWS, 384) for k in range(3)], axis=1)
    from_edge = dot(edge, wce[...])
    for h in range(2):
        pieces = [
            pp[dy, dx : dx + BE, :, h * 256 : (h + 1) * 256].reshape(ROWS, 256)
            for dx in range(3)
            for dy in range(3)
        ]
        total = dot(jnp.concatenate(pieces, axis=1), wc[...].reshape(9 * 256, 512))
        parts = [total[:, t * 128 : (t + 1) * 128] for t in range(4)]
        parts[3 if h == 0 else 0] += from_edge[:, h * 128 : (h + 1) * 128]
        for t in range(4):
            base = h * 512 + t * 128
            out_coarse[0, :, :, base : base + 128] = parts[t].astype(BF16).reshape(BE, BE, 128)
    c2 = exchange(c1, red_c, got_c, mid_c, coarse_rows, send_c, recv_c)
    f3 = gather(f2, mid_f, all_f, fine_rows, send_f, recv_f)
    c3 = gather(c2, mid_c, all_c, coarse_rows, send_c, recv_c)
    finish(f3, all_f, out_fine_grad, 24)
    finish(c3, all_c, out_coarse_grad, 48)
    for copy in (f1, f2, f3, c1, c2, c3):
        copy.wait_send()


def hand_over(
    scale, coarse, fine_grad, coarse_grad, act, out_coarse, out_fine_grad, out_coarse_grad, out_cell,
    wide, out_sem, other_sem,
):
    half = BE // 2
    cuts = [(s, slice(h * half, (h + 1) * half)) for s in range(SLOTS) for h in range(2)]
    outs = [pltpu.make_async_copy(wide.at[c], out_cell.at[c], out_sem.at[i]) for i, c in enumerate(cuts)]
    pairs = ((coarse, out_coarse), (fine_grad, out_fine_grad), (coarse_grad, out_coarse_grad))
    others = [pltpu.make_async_copy(b, c, other_sem.at[i]) for i, (b, c) in enumerate(pairs)]
    for i, cut in enumerate(cuts):
        wide[cut] = act[cut].astype(F32) * scale
        outs[i].start()
        if i == 0:
            for copy in others:
                copy.start()
    for copy in outs + others:
        copy.wait()


def on_device(nb, ns, features, coords, neighbours, fine_weight, coarse_weight, cotangent):
    nq = 8 if nb % 16 == 0 else min(nb, 2)
    na = nb * ns // nq
    fine_rows = -(-216 // (na * 16)) * 16
    coarse_rows = -(-432 // (na * 16)) * 16
    vmem = pl.BlockSpec(memory_space=pltpu.VMEM)
    smem = pl.BlockSpec(memory_space=pltpu.SMEM)
    hbm = pl.BlockSpec(memory_space=pl.ANY)
    dma = pltpu.SemaphoreType.DMA
    coarse_out, fine_grad, coarse_grad, act_grad = pl.pallas_call(
        functools.partial(body, nb, ns, nq, fine_rows, coarse_rows),
        out_shape=(
            pltpu.VMEM((1, BE, BE, BE * C2), BF16),
            pltpu.VMEM((3, 3, 3 * C1 * C1), F32),
            pltpu.VMEM((3, 3, 3 * C1 * C2), F32),
            pltpu.VMEM((SLOTS, BE, BE, BE * C1), BF16),
        ),
        in_specs=[smem, smem, hbm, hbm, hbm, hbm],
        out_specs=(vmem, vmem, vmem, vmem),
        scratch_shapes=[
            pltpu.VMEM((SLOTS, BE, BE, BE * C1), BF16),
            pltpu.VMEM((3, 3, 3 * C1 * C1), BF16),
            pltpu.VMEM((3, 3, 3 * C1 * C2), BF16),
            pltpu.VMEM((1, BE, BE, BE * C2), BF16),
            pltpu.VMEM((2, SLOTS, BE, BE * C1), BF16),
            pltpu.VMEM((2, BE, BE * C2), BF16),
            pltpu.VMEM((2, BE, BE * C1), BF16),
            pltpu.VMEM((2, BE, BE * C1), BF16),
            pltpu.VMEM((3, SLOTS, BE + 2, BE, BE * C1), BF16),
            pltpu.VMEM((2, SLOTS, BE + 2, BE, 384), BF16),
            pltpu.VMEM((9 * 256 + 9 * 128, 256), BF16),
            pltpu.VMEM((9, 256, 512), BF16),
            pltpu.VMEM((9 * 128, 256), BF16),
            pltpu.VMEM((256, 9 * 128), BF16),
            pltpu.VMEM((3, BE + 2, BE, BE * C2), BF16),
            pltpu.VMEM((BE + 2, BE, 384), BF16),
            pltpu.VMEM((8, 8, 8, 256), F32),
            pltpu.VMEM((SLOTS, 8, BE, 512), F32),
            pltpu.VMEM((SLOTS, BE, BE, 512), F32),
            pltpu.VMEM((SLOTS, BE, BE, 512), BF16),
            pltpu.VMEM((2 * SLOTS, 256, 256), BF16),
            pltpu.VMEM((BE * C2, ROWS), BF16),
            pltpu.VMEM((SLOTS, 8, 8, 256), F32),
            pltpu.VMEM((BE, BE, BE * C1), F32),
            pltpu.VMEM((3, BE + 2, BE, BE * C1), BF16),
            pltpu.VMEM((BE + 2, BE, 384), BF16),
            pltpu.VMEM((432, 128), F32),
            pltpu.VMEM((9 * 128, 128), F32),
            pltpu.VMEM((9 * C1, 128), BF16),
            pltpu.VMEM((9 * C2, 128), BF16),
            pltpu.VMEM((na * fine_rows, 128), BF16),
            pltpu.VMEM((na * coarse_rows, 128), BF16),
            pltpu.VMEM((na - 1, fine_rows, 128), BF16),
            pltpu.VMEM((na - 1, coarse_rows, 128), BF16),
            pltpu.VMEM((nq, fine_rows, 128), BF16),
            pltpu.VMEM((nq, coarse_rows, 128), BF16),
            pltpu.VMEM((na * fine_rows, 128), BF16),
            pltpu.VMEM((na * coarse_rows, 128), BF16),
            dma((6,)), dma((6,)),
            dma((3,)), dma((3,)), dma((3,)), dma((3,)), dma((4,)),
        ],
        compiler_params=pltpu.CompilerParams(
            collective_id=0, has_side_effects=True, vmem_limit_bytes=58 * 1024 * 1024
        ),
        name="unet_level",
    )(coords, neighbours, features, fine_weight, coarse_weight, cotangent)
    scale = float(nb * ns * BE**3) ** 0.5
    return pl.pallas_call(
        functools.partial(hand_over, scale),
        out_shape=(
            jax.ShapeDtypeStruct(coarse_out.shape, BF16),
            jax.ShapeDtypeStruct(fine_grad.shape, F32),
            jax.ShapeDtypeStruct(coarse_grad.shape, F32),
            jax.ShapeDtypeStruct(act_grad.shape, F32),
        ),
        in_specs=[vmem] * 4,
        out_specs=(hbm,) * 4,
        scratch_shapes=[
            pltpu.VMEM(act_grad.shape, F32),
            dma((2 * SLOTS,)), dma((3,)),
        ],
        compiler_params=pltpu.CompilerParams(vmem_limit_bytes=16 * 1024 * 1024),
        name="hand_over",
    )(coarse_out, fine_grad, coarse_grad, act_grad)


def solution(mesh):
    nb, ns = mesh.shape["blocks"], mesh.shape["sub"]
    split = P(("blocks", "sub"), None, None, None)
    return jax.shard_map(
        functools.partial(on_device, nb, ns),
        mesh=mesh,
        in_specs=(split, P(("blocks", "sub"), None), P(("blocks", "sub"), None), P(), P(), split),
        out_specs=(split, P(), P(), split),
        check_vma=False,
    )
```

```python
import functools

import jax
import jax.numpy as jnp
from jax import lax
from jax.experimental import pallas as pl
from jax.experimental.pallas import tpu as pltpu
from jax.sharding import PartitionSpec as P

BE = 16
C1 = 32
C2 = 64
SLOTS = 4
ROWS = BE * BE
MESH = pl.DeviceIdType.MESH
F32 = jnp.float32
BF16 = jnp.bfloat16


def iota(shape, dim):
    return lax.broadcasted_iota(jnp.int32, shape, dim)


def eye_matrix(size):
    return (iota((size, size), 0) == iota((size, size), 1)).astype(BF16)


def dot(a, b):
    return jnp.dot(a, b, preferred_element_type=F32)


def dot_t(a, b):
    return lax.dot_general(a, b, (((1,), (1,)), ((), ())), preferred_element_type=F32)


def shifted(cells, row, k):
    if k == 1:
        return cells
    sub = iota(cells.shape, 0)
    if k == 0:
        return jnp.where(sub == 0, row, pltpu.roll(cells, 1, 0))
    return jnp.where(sub == BE - 1, row, pltpu.roll(cells, BE - 1, 0))


def tiled_weight(row, width):
    per_tile = 128 // width
    groups = []
    sub = iota((8, 128), 0)
    lane = iota((8, 128), 1)
    for g in range(C1 // 8):
        first = g * 8 // per_tile
        picked = row[:, first * 128 : (first + 1) * 128]
        picked = jnp.broadcast_to(picked, (8, 128))
        for t in range(1, 8 // per_tile):
            tile = row[:, (first + t) * 128 : (first + t + 1) * 128]
            picked = jnp.where(sub // per_tile == t, tile, picked)
        groups.append(jnp.where(lane // width == sub % per_tile, picked, 0.0))
    tiled = jnp.concatenate(groups, axis=0)
    step = 64
    while step >= width:
        tiled = tiled + pltpu.roll(tiled, step, 1)
        step //= 2
    return tiled


def fold_taps(block, edge_low, edge_high, width):
    quarter = iota((width, 128), 1) // C1
    total = None
    for cls in range(4):
        part = None
        for z_out in (cls, cls + 4):
            rows = block[z_out * width : (z_out + 1) * width]
            tiles = [rows[:, :128], rows[:, 128:]]
            if z_out == 0:
                picked = jnp.where(quarter == 3, edge_low, tiles[0])
            elif z_out == 7:
                picked = jnp.where(quarter == 0, edge_high, tiles[1])
            elif z_out == 3:
                picked = jnp.where(quarter == 0, tiles[1], tiles[0])
            elif z_out == 4:
                picked = jnp.where(quarter == 3, tiles[0], tiles[1])
            else:
                picked = tiles[z_out // 4]
            part = picked if part is None else part + picked
        shift = (1 - cls) % 4 * C1
        if shift:
            part = pltpu.roll(part, shift, 1)
        total = part if total is None else total + part
    return jnp.where(quarter < 3, total, 0.0)


def body(
    nb, ns, nq, fine_rows, coarse_rows,
    coords, neigh, feat_hbm, fw_hbm, cw_hbm, cot_hbm,
    out_coarse, out_fine_grad, out_coarse_grad, out_act,
    feat, fw, cw, cot, hx, hc, hp, ps_ends, xp, ex, wf, wc, wce, wct, cp, ec, pg, up, acts, hid, gt, ct, ps, pool, pp, ep,
    folds, turned, sum_f, sum_c, red_f, red_c, got_f, got_c, mid_f, mid_c, all_f, all_c,
    halo_send, halo_recv, send_f, recv_f, send_c, recv_c, in_sem,
):
    loads = [
        pltpu.make_async_copy(src, dst, in_sem.at[i])
        for i, (src, dst) in enumerate(((fw_hbm, fw), (cw_hbm, cw), (cot_hbm, cot), (feat_hbm, feat)))
    ]
    for copy in loads:
        copy.start()

    i0 = lax.axis_index("blocks")
    i1 = lax.axis_index("sub")
    count = nb * ns
    me = i0 * ns + i1
    nxt = lax.rem(me + 1, count)
    prv = lax.rem(me + count - 1, count)
    prev_id = (prv // ns, lax.rem(prv, ns))
    next_id = (nxt // ns, lax.rem(nxt, ns))
    na = count // nq
    q = lax.rem(i0, nq)
    a = (i0 // nq) * ns + i1

    nz = nb // nq
    zs = [lax.rem(i0 // nq + k, nz) for k in range(nz)]
    ys = [lax.rem(i1 + k, ns) for k in range(ns)]
    blocks = [z * nq + q for z in zs]
    def way(k, size):
        return min(k, size - k)

    offsets = [(k, m) for k in range(nz) for m in range(ns) if k + m > 0]
    offsets.sort(key=lambda o: -way(o[0], nz) - way(o[1], ns))
    a_peers = [(zs[k] * ns + ys[m], (blocks[k], ys[m])) for k, m in offsets]
    nx = nq // 2
    xs = [lax.rem(q // 2 + k, nx) * 2 for k in range(nx)]
    cores = [lax.rem(q + k, 2) for k in range(2)]
    offsets = [(k, m) for k in range(nx) for m in range(2) if k + m > 0]
    offsets.sort(key=lambda o: -way(o[0], nx) - o[1])
    q_peers = [(i0 - q + xs[k] + cores[m], i1) for k, m in offsets]

    barrier = pltpu.get_barrier_semaphore()

    def greet(device):
        pl.semaphore_signal(barrier, inc=1, device_id=device, device_id_type=MESH)

    has_prev = me > 0
    has_next = me < count - 1
    pl.when(has_prev)(lambda: greet(prev_id))
    pl.when(has_next)(lambda: greet(next_id))
    for _, device in a_peers:
        greet(device)
    for device in q_peers:
        greet(device)

    def describe(src, dst, send, recv, device):
        return pltpu.make_async_remote_copy(
            src_ref=src, dst_ref=dst, send_sem=send, recv_sem=recv, device_id=device, device_id_type=MESH
        )

    def remote(src, dst, send, recv, device):
        describe(src, dst, send, recv, device).start()

    def swap(high, low, dst, k):
        up = describe(high, dst.at[0], halo_send.at[k], halo_recv.at[k], next_id)
        down = describe(low, dst.at[1], halo_send.at[k + 1], halo_recv.at[k + 1], prev_id)
        pl.when(has_next)(up.start)
        pl.when(has_prev)(down.start)

        def clear(side):
            dst[side] = jnp.zeros(dst.shape[1:], dst.dtype)

        def finish_swap():
            pl.when(has_prev)(up.wait_recv)
            pl.when(has_next)(down.wait_recv)
            pl.when(has_next)(up.wait_send)
            pl.when(has_prev)(down.wait_send)
            pl.when(jnp.logical_not(has_prev))(lambda: clear(0))
            pl.when(jnp.logical_not(has_next))(lambda: clear(1))

        return finish_swap

    loads[2].wait()
    loads[3].wait()
    pl.semaphore_wait(barrier, na + nq - 2 + has_prev.astype(jnp.int32) + has_next.astype(jnp.int32))
    end_swaps = [
        swap(feat.at[:, BE - 1], feat.at[:, 0], hx, 0),
        swap(cot.at[0, BE - 1], cot.at[0, 0], hc, 2),
    ]
    loads[0].wait()
    loads[1].wait()
    first = me * SLOTS
    quarter8 = iota((C1, 256), 1) // C1
    half8 = iota((C1, 512), 1) // C2
    half4 = iota((C1, 256), 1) // C2
    half2 = iota((C1, 128), 1) // C2
    zeros = jnp.zeros((2 * C1, 256), BF16)
    for dx in range(3):
        for dy in range(3):
            tap = dx * 3 + dy
            row_f = fw[dx, dy : dy + 1, :].astype(F32)
            tiles = []
            for dz in range(3):
                t = tiled_weight(row_f[:, dz * C1 * C1 : (dz + 1) * C1 * C1], C1)
                tiles.append(jnp.concatenate([t, t], axis=1))
            for z_in in range(8):
                line = jnp.where(quarter8 == z_in, tiles[1], 0.0)
                line = jnp.where(quarter8 == z_in + 1, tiles[0], line)
                line = jnp.where(quarter8 == z_in - 1, tiles[2], line)
                wf[tap * 256 + z_in * C1 : tap * 256 + (z_in + 1) * C1, :] = line.astype(BF16)
            base = 2304 + dx * 256
            high = base + (0, 64, 128)[dy]
            low = base + (96, 32, 224)[dy]
            wf[high : high + 32, :] = jnp.where(quarter8 == 7, tiles[2], 0.0).astype(BF16)
            wf[low : low + 32, :] = jnp.where(quarter8 == 0, tiles[0], 0.0).astype(BF16)
            if dy == 2:
                wf[base + 160 : base + 224, :] = zeros

            row_c = cw[dx, dy : dy + 1, :].astype(F32)
            narrow = [
                tiled_weight(row_c[:, dz * C1 * C2 : (dz + 1) * C1 * C2], C2) for dz in range(3)
            ]
            wide = [jnp.concatenate([t] * 4, axis=1) for t in narrow]
            for z_in in range(8):
                line = jnp.where(half8 == z_in, wide[1], 0.0)
                line = jnp.where(half8 == z_in + 1, wide[0], line)
                line = jnp.where(half8 == z_in - 1, wide[2], line)
                wc[tap, z_in * C1 : (z_in + 1) * C1, :] = line.astype(BF16)
            base = dx * 384 + dy * 128
            pair = [jnp.concatenate([t] * 2, axis=1) for t in narrow]
            wce[base : base + 32, :] = jnp.where(half4 == 1, pair[2], 0.0).astype(BF16)
            wce[base + 32 : base + 96, :] = zeros
            wce[base + 96 : base + 128, :] = jnp.where(half4 == 2, pair[0], 0.0).astype(BF16)
            base = (2 - dx) * 384 + (2 - dy) * 128
            wct[0:96, base : base + 128] = jnp.zeros((96, 128), BF16)
            wct[96:128, base : base + 128] = jnp.where(half2 == 0, narrow[0], 0.0).astype(BF16)
            wct[128:160, base : base + 128] = jnp.where(half2 == 1, narrow[2], 0.0).astype(BF16)
            wct[160:256, base : base + 128] = jnp.zeros((96, 128), BF16)

    eye = eye_matrix(256)

    flat_cot = cot[0].reshape(ROWS, BE * C2)
    for j in range(4):
        ct[j * 256 : (j + 1) * 256, :] = dot_t(eye, flat_cot[:, j * 256 : (j + 1) * 256]).astype(BF16)

    def put_cot(layer, cells):
        lane = iota((BE, 128), 1)
        zero = jnp.zeros((1, BE * C2), F32)
        for k in range(3):
            plane = shifted(cells, zero, k)
            cp[k, layer] = plane.astype(BF16)
            ec[layer, :, k * 128 : (k + 1) * 128] = jnp.where(
                lane < C2, plane[:, 512:640], plane[:, 384:512]
            ).astype(BF16)

    def cot_layer(x, _):
        put_cot(x + 1, cot[0, x].astype(F32))
        return 0

    for x in range(BE):
        cot_layer(x, 0)

    def put_cells(s, layer, cells, row_low, row_high, z_low, z_high):
        lane = iota((BE, 128), 1)
        zero = jnp.zeros((1, 128), F32)
        edges = ([], [])
        for k in range(3):
            plane = shifted(cells, (row_low, None, row_high)[k], k)
            xp[k, s, layer] = plane.astype(BF16)
            low = 0.0 if z_low is None else shifted(z_low, zero, k)
            high = 0.0 if z_high is None else shifted(z_high, zero, k)
            edges[0].append(jnp.where(lane < C1, plane[:, 256:384], low))
            edges[1].append(jnp.where(lane < C1, high, plane[:, 128:256]))
        for h in range(2):
            middle = pltpu.roll(edges[h][1], 64, 1)
            outer = (lane < C1) | (lane >= 3 * C1)
            ex[h, s, layer, :, 0:128] = jnp.where(outer, edges[h][0], middle).astype(BF16)
            ex[h, s, layer, :, 128:256] = edges[h][2].astype(BF16)

    def across(s, column):
        target = neigh[s, column]
        local = target - first
        return jnp.clip(local, 0, SLOTS - 1), local, (target >= 0).astype(F32)

    for s in range(SLOTS):
        ylow, _, ylow_on = across(s, 2)
        yhigh, _, yhigh_on = across(s, 3)
        zlow, _, zlow_on = across(s, 4)
        zhigh, _, zhigh_on = across(s, 5)

        def cell_layer(x, _):
            put_cells(
                s,
                x + 1,
                feat[s, x].astype(F32),
                feat[ylow, x].astype(F32)[BE - 1 : BE] * ylow_on,
                feat[yhigh, x].astype(F32)[0:1] * yhigh_on,
                feat[zlow, x, :, 384:512].astype(F32) * zlow_on,
                feat[zhigh, x, :, 0:128].astype(F32) * zhigh_on,
            )
            return 0

        for x in range(BE):
            cell_layer(x, 0)

    for finish_swap in end_swaps:
        finish_swap()

    put_cot(0, hc[0].astype(F32))
    put_cot(BE + 1, hc[1].astype(F32))
    for s in range(SLOTS):
        zero = jnp.zeros((1, BE * C1), F32)
        near, local, on = across(s, 0)
        inside = (local >= 0).astype(F32) * on
        outside = (local < 0).astype(F32) * on
        far = jnp.clip(local + SLOTS, 0, SLOTS - 1)
        plane = feat[near, BE - 1].astype(F32) * inside + hx[0, far].astype(F32) * outside
        put_cells(s, 0, plane, zero, zero, None, None)
        near, local, on = across(s, 1)
        inside = (local < SLOTS).astype(F32) * on
        outside = (local >= SLOTS).astype(F32) * on
        far = jnp.clip(local - SLOTS, 0, SLOTS - 1)
        plane = feat[near, 0].astype(F32) * inside + hx[1, far].astype(F32) * outside
        put_cells(s, BE + 1, plane, zero, zero, None, None)

    edge = jnp.concatenate([ec[k : k + BE].reshape(ROWS, 384) for k in range(3)], axis=1)
    from_edge = dot_t(edge, wct[...])
    for h in range(2):
        total = None
        for dx in range(3):
            for dy in range(3):
                window = cp[2 - dy, 2 - dx : 2 - dx + BE, :, h * 512 : (h + 1) * 512]
                term = dot_t(window.reshape(ROWS, 512), wc[dx * 3 + dy])
                total = term if total is None else total + term
        parts = [total[:, :128], total[:, 128:]]
        parts[1 - h] = parts[1 - h] + from_edge[:, h * 128 : (h + 1) * 128]
        for t in range(2):
            part = parts[t].reshape(2, 8, 2, 8, 128)
            for ox in range(2):
                for oy in range(2):
                    pg[ox * 4 + oy * 2 + h, :, :, t * 128 : (t + 1) * 128] = part[ox, :, oy]

    r = iota((256, 512), 0)
    l = iota((256, 512), 1)
    spread_z = ((l // 64 == r // 32) & (l % 32 == r % 32)).astype(BF16)
    r = iota((128, 64), 0)
    l = iota((128, 64), 1)
    spread_y = (r // 2 == l).astype(BF16)
    r = iota((64, 256), 0)
    l = iota((64, 256), 1)
    sum_xy = ((l // 32 == r // 8) & (l % 16 // 2 == r % 8)).astype(BF16)
    r = iota((256, 128), 0)
    l = iota((256, 128), 1)
    sum_z = ((r // 64 == l // 32) & (r % 32 == l % 32)).astype(F32)
    sum_z = (sum_z * 0.125).astype(BF16)

    grads = []
    for s in range(SLOTS):
        live = (coords[s, 0] >= 0).astype(F32)
        octant = lax.rem(coords[s, 0], 2) * 4 + coords[s, 1] * 2 + coords[s, 2]
        grads.append(pg[jnp.clip(octant, 0, 7)].reshape(64, 256) * (live * 0.125))
    grads = dot(jnp.concatenate(grads, axis=0).astype(BF16), spread_z).astype(BF16)
    for s in range(SLOTS):
        up[s] = dot(spread_y, grads[s * 64 : (s + 1) * 64]).reshape(8, BE, 512)

    def fine_act(s, _):
        for h in range(2):
            lanes = slice(h * 256, (h + 1) * 256)
            pieces = [
                xp[dy, s, dx : dx + BE, :, lanes].reshape(ROWS, 256)
                for dx in range(3)
                for dy in range(3)
            ]
            pieces += [ex[h, s, dx : dx + BE].reshape(ROWS, 256) for dx in range(3)]
            act = dot(jnp.concatenate(pieces, axis=1), wf[...])
            acts[s, :, :, lanes] = act.reshape(BE, BE, 256)
        return 0

    def fine_layer(i, _):
        s = i // BE
        x = lax.rem(i, BE)
        act = acts[s, x]
        sigma = 0.5 * jnp.tanh(0.5 * act) + 0.5
        gated = act * sigma
        hid[s, x] = (feat[s, x].astype(F32) + gated).astype(BF16)
        slope = sigma + gated * (1.0 - sigma)
        out_act[s, x] = (up[s, x // 2] * slope).astype(BF16)
        return 0

    for s in range(SLOTS + 1):
        if s < SLOTS:
            fine_act(s, 0)
        if s > 0:
            for x in range(BE):
                fine_layer((s - 1) * BE + x, 0)

    sums = jnp.concatenate([dot(sum_xy, hid[s].reshape(ROWS, 512)) for s in range(SLOTS)], axis=0)
    top = sums.astype(BF16)
    rest = (sums - top.astype(F32)).astype(BF16)
    for h in range(2):
        lanes = slice(h * 256, (h + 1) * 256)
        both = jnp.concatenate([top[:, lanes], rest[:, lanes]], axis=1)
        small = dot(both, jnp.concatenate([sum_z, sum_z], axis=0))
        ps[:, :, :, h * 128 : (h + 1) * 128] = small.reshape(SLOTS, 8, 8, 128)

    for t in range(8):
        slot = jnp.int32(0)
        on = jnp.int32(0)
        for s in range(SLOTS):
            octant = lax.rem(coords[s, 0], 2) * 4 + coords[s, 1] * 2 + coords[s, 2]
            here = ((coords[s, 0] >= 0) & (octant == t)).astype(jnp.int32)
            slot = slot + here * s
            on = on + here
        block = ps[jnp.clip(slot, 0, SLOTS - 1)] * on.astype(F32)
        ox, oy, oz = t // 4, t // 2 % 2, t % 2
        pool[ox * 8 : (ox + 1) * 8, oy * 8 : (oy + 1) * 8, oz * 256 : (oz + 1) * 256] = block
    ps_ends[0] = pool[0].astype(BF16)
    ps_ends[1] = pool[BE - 1].astype(BF16)
    end_pools = swap(ps_ends.at[1], ps_ends.at[0], hp, 4)

    def put_pool(layer, cells):
        lane = iota((BE, 128), 1)
        zero = jnp.zeros((1, BE * C1), F32)
        for k in range(3):
            plane = shifted(cells, zero, k)
            pp[k, layer] = plane.astype(BF16)
            ep[layer, :, k * 128 : (k + 1) * 128] = jnp.where(
                lane < C1, plane[:, 256:384], plane[:, 128:256]
            ).astype(BF16)

    def pool_layer(x, _):
        put_pool(x + 1, pool[x])
        return 0

    for x in range(BE):
        pool_layer(x, 0)

    eye = eye_matrix(256)
    for i in range(2 * SLOTS):
        lanes = slice(i % 2 * 256, i % 2 * 256 + 256)
        gt[i] = dot_t(eye, out_act[i // 2, :, :, lanes].reshape(ROWS, 256)).astype(BF16)
    eye = eye_matrix(128)

    def turn(sums, width):
        copies = 128 // width
        count = 3 * C1 // copies
        rows = [sums[tap * width : (tap + 1) * width, :] for tap in range(9) for _ in range(copies)]
        flipped = dot_t(eye, jnp.concatenate(rows, axis=0))
        for tap in range(9):
            turned[tap * 128 : (tap + 1) * 128, :] = flipped[:, tap * 128 : (tap + 1) * 128]
        lane = iota((count, 128), 1) // width
        lines = []
        for tap in range(9):
            base = tap * 128
            picked = turned[pl.ds(base, count, stride=copies), :]
            for t in range(1, copies):
                picked = jnp.where(lane == t, turned[pl.ds(base + t, count, stride=copies), :], picked)
            lines.append(picked)
        return lines

    def fine_taps(dx):
        left = jnp.concatenate([gt[i] for i in range(8)], axis=1)
        border = jnp.concatenate(
            [jnp.concatenate([gt[i, 0:32, :], gt[i, 224:256, :]], axis=0) for i in range(8)], axis=1
        )
        edges = jnp.concatenate(
            [ex[i % 2, i // 2, dx : dx + BE].reshape(ROWS, 256) for i in range(8)], axis=0
        )
        edge = dot(border, edges)
        edge = [edge[:, :128], pltpu.roll(edge[:, :128], 64, 1), edge[:, 128:]]
        for dy in range(3):
            right = jnp.concatenate(
                [
                    xp[dy, i // 2, dx : dx + BE, :, i % 2 * 256 : i % 2 * 256 + 256].reshape(ROWS, 256)
                    for i in range(8)
                ],
                axis=0,
            )
            folded = fold_taps(dot(left, right), edge[dy][:32], edge[dy][32:], C1)
            tap = dx * 3 + dy
            sum_f[tap * C1 : (tap + 1) * C1, :] = folded.astype(BF16)

    def coarse_taps(dx):
        left = jnp.concatenate([ct[0:512, :], ct[512:1024, :]], axis=1)
        edge = dot(ct[448:576, :], ep[dx : dx + BE].reshape(ROWS, 384))
        for dy in range(3):
            window = pp[dy, dx : dx + BE].reshape(ROWS, 512)
            right = jnp.concatenate([window[:, :256], window[:, 256:]], axis=0)
            lanes = slice(dy * 128, (dy + 1) * 128)
            folded = fold_taps(dot(left, right), edge[64:, lanes], edge[:64, lanes], C2)
            tap = dx * 3 + dy
            sum_c[tap * C2 : (tap + 1) * C2, :] = folded.astype(BF16)

    def all_of(ref, send, recv):
        return pltpu.make_async_remote_copy(
            src_ref=ref, dst_ref=ref, send_sem=send, recv_sem=recv, device_id=next_id, device_id_type=MESH
        )

    def shard(i, rows):
        return pl.ds(pl.multiple_of(i * rows, rows), rows)

    def spread(red, got, rows, send, recv):
        for j, (other, device) in enumerate(a_peers):
            remote(red.at[shard(other, rows)], got.at[j], send.at[0], recv.at[0], device)
        return all_of(got, send.at[0], recv.at[0])

    def exchange(copies, red, got, mid, rows, send, recv):
        copies.wait_recv()
        total = red[shard(a, rows), :].astype(F32)
        for j in range(na - 1):
            total = total + got[j].astype(F32)
        mid[q] = total.astype(BF16)
        for device in q_peers:
            remote(mid.at[q], mid.at[q], send.at[1], recv.at[1], device)
        return all_of(mid.at[0 : nq - 1], send.at[1], recv.at[1])

    def gather(copies, mid, full, rows, send, recv):
        copies.wait_recv()
        total = mid[0].astype(F32)
        for j in range(1, nq):
            total = total + mid[j].astype(F32)
        part = shard(a, rows)
        full[part, :] = total.astype(BF16)
        for _, device in a_peers:
            remote(full.at[part], full.at[part], send.at[2], recv.at[2], device)
        return all_of(full.at[0 : (na - 1) * rows], send.at[2], recv.at[2])

    def finish(copies, full, out, count):
        copies.wait_recv()
        folds[: 9 * count, :] = full[: 9 * count, :].astype(F32)
        for dx in range(3):
            for j in range(count):
                out[dx, :, j * 128 : (j + 1) * 128] = folds[pl.ds(dx * 3 * count + j, 3, stride=count), :]

    fine_taps(0)
    fine_taps(1)
    fine_taps(2)
    rows = turn(sum_f, C1) + [jnp.zeros((na * fine_rows - 216, 128), F32)]
    red_f[...] = jnp.concatenate(rows, axis=0).astype(BF16)
    f1 = spread(red_f, got_f, fine_rows, send_f, recv_f)
    end_pools()
    put_pool(0, hp[0].astype(F32))
    put_pool(BE + 1, hp[1].astype(F32))
    for dx in range(3):
        coarse_taps(dx)
    for tap, rows in enumerate(turn(sum_c, C2)):
        red_c[tap * 48 : (tap + 1) * 48, :] = rows.astype(BF16)
    if na * coarse_rows > 432:
        red_c[432:, :] = jnp.zeros((na * coarse_rows - 432, 128), BF16)
    c1 = spread(red_c, got_c, coarse_rows, send_c, recv_c)
    f2 = exchange(f1, red_f, got_f, mid_f, fine_rows, send_f, recv_f)
    edge = jnp.concatenate([ep[k : k + BE].reshape(ROWS, 384) for k in range(3)], axis=1)
    from_edge = dot(edge, wce[...])
    for h in range(2):
        pieces = [
            pp[dy, dx : dx + BE, :, h * 256 : (h + 1) * 256].reshape(ROWS, 256)
            for dx in range(3)
            for dy in range(3)
        ]
        total = dot(jnp.concatenate(pieces, axis=1), wc[...].reshape(9 * 256, 512))
        parts = [total[:, t * 128 : (t + 1) * 128] for t in range(4)]
        parts[3 if h == 0 else 0] += from_edge[:, h * 128 : (h + 1) * 128]
        for t in range(4):
            base = h * 512 + t * 128
            out_coarse[0, :, :, base : base + 128] = parts[t].astype(BF16).reshape(BE, BE, 128)
    c2 = exchange(c1, red_c, got_c, mid_c, coarse_rows, send_c, recv_c)
    f3 = gather(f2, mid_f, all_f, fine_rows, send_f, recv_f)
    c3 = gather(c2, mid_c, all_c, coarse_rows, send_c, recv_c)
    finish(f3, all_f, out_fine_grad, 24)
    finish(c3, all_c, out_coarse_grad, 48)
    for copy in (f1, f2, f3, c1, c2, c3):
        copy.wait_send()


def hand_over(
    scale, coarse, fine_grad, coarse_grad, act, out_coarse, out_fine_grad, out_coarse_grad, out_cell,
    wide, out_sem, other_sem,
):
    half = BE // 2
    cuts = [(s, slice(h * half, (h + 1) * half)) for s in range(SLOTS) for h in range(2)]
    outs = [pltpu.make_async_copy(wide.at[c], out_cell.at[c], out_sem.at[i]) for i, c in enumerate(cuts)]
    pairs = ((coarse, out_coarse), (fine_grad, out_fine_grad), (coarse_grad, out_coarse_grad))
    others = [pltpu.make_async_copy(b, c, other_sem.at[i]) for i, (b, c) in enumerate(pairs)]
    for i, cut in enumerate(cuts):
        wide[cut] = act[cut].astype(F32) * scale
        outs[i].start()
        if i == 0:
            for copy in others:
                copy.start()
    for copy in outs + others:
        copy.wait()


def on_device(nb, ns, features, coords, neighbours, fine_weight, coarse_weight, cotangent):
    nq = 8 if nb % 16 == 0 else min(nb, 2)
    na = nb * ns // nq
    fine_rows = -(-216 // (na * 16)) * 16
    coarse_rows = -(-432 // (na * 16)) * 16
    vmem = pl.BlockSpec(memory_space=pltpu.VMEM)
    smem = pl.BlockSpec(memory_space=pltpu.SMEM)
    hbm = pl.BlockSpec(memory_space=pl.ANY)
    dma = pltpu.SemaphoreType.DMA
    coarse_out, fine_grad, coarse_grad, act_grad = pl.pallas_call(
        functools.partial(body, nb, ns, nq, fine_rows, coarse_rows),
        out_shape=(
            pltpu.VMEM((1, BE, BE, BE * C2), BF16),
            pltpu.VMEM((3, 3, 3 * C1 * C1), F32),
            pltpu.VMEM((3, 3, 3 * C1 * C2), F32),
            pltpu.VMEM((SLOTS, BE, BE, BE * C1), BF16),
        ),
        in_specs=[smem, smem, hbm, hbm, hbm, hbm],
        out_specs=(vmem, vmem, vmem, vmem),
        scratch_shapes=[
            pltpu.VMEM((SLOTS, BE, BE, BE * C1), BF16),
            pltpu.VMEM((3, 3, 3 * C1 * C1), BF16),
            pltpu.VMEM((3, 3, 3 * C1 * C2), BF16),
            pltpu.VMEM((1, BE, BE, BE * C2), BF16),
            pltpu.VMEM((2, SLOTS, BE, BE * C1), BF16),
            pltpu.VMEM((2, BE, BE * C2), BF16),
            pltpu.VMEM((2, BE, BE * C1), BF16),
            pltpu.VMEM((2, BE, BE * C1), BF16),
            pltpu.VMEM((3, SLOTS, BE + 2, BE, BE * C1), BF16),
            pltpu.VMEM((2, SLOTS, BE + 2, BE, 256), BF16),
            pltpu.VMEM((12 * 256, 256), BF16),
            pltpu.VMEM((9, 256, 512), BF16),
            pltpu.VMEM((9 * 128, 256), BF16),
            pltpu.VMEM((256, 9 * 128), BF16),
            pltpu.VMEM((3, BE + 2, BE, BE * C2), BF16),
            pltpu.VMEM((BE + 2, BE, 384), BF16),
            pltpu.VMEM((8, 8, 8, 256), F32),
            pltpu.VMEM((SLOTS, 8, BE, 512), F32),
            pltpu.VMEM((SLOTS, BE, BE, 512), F32),
            pltpu.VMEM((SLOTS, BE, BE, 512), BF16),
            pltpu.VMEM((2 * SLOTS, 256, 256), BF16),
            pltpu.VMEM((BE * C2, ROWS), BF16),
            pltpu.VMEM((SLOTS, 8, 8, 256), F32),
            pltpu.VMEM((BE, BE, BE * C1), F32),
            pltpu.VMEM((3, BE + 2, BE, BE * C1), BF16),
            pltpu.VMEM((BE + 2, BE, 384), BF16),
            pltpu.VMEM((432, 128), F32),
            pltpu.VMEM((9 * 128, 128), F32),
            pltpu.VMEM((9 * C1, 128), BF16),
            pltpu.VMEM((9 * C2, 128), BF16),
            pltpu.VMEM((na * fine_rows, 128), BF16),
            pltpu.VMEM((na * coarse_rows, 128), BF16),
            pltpu.VMEM((na - 1, fine_rows, 128), BF16),
            pltpu.VMEM((na - 1, coarse_rows, 128), BF16),
            pltpu.VMEM((nq, fine_rows, 128), BF16),
            pltpu.VMEM((nq, coarse_rows, 128), BF16),
            pltpu.VMEM((na * fine_rows, 128), BF16),
            pltpu.VMEM((na * coarse_rows, 128), BF16),
            dma((6,)), dma((6,)),
            dma((3,)), dma((3,)), dma((3,)), dma((3,)), dma((4,)),
        ],
        compiler_params=pltpu.CompilerParams(
            collective_id=0, has_side_effects=True, vmem_limit_bytes=58 * 1024 * 1024
        ),
        name="unet_level",
    )(coords, neighbours, features, fine_weight, coarse_weight, cotangent)
    scale = float(nb * ns * BE**3) ** 0.5
    return pl.pallas_call(
        functools.partial(hand_over, scale),
        out_shape=(
            jax.ShapeDtypeStruct(coarse_out.shape, BF16),
            jax.ShapeDtypeStruct(fine_grad.shape, F32),
            jax.ShapeDtypeStruct(coarse_grad.shape, F32),
            jax.ShapeDtypeStruct(act_grad.shape, F32),
        ),
        in_specs=[vmem] * 4,
        out_specs=(hbm,) * 4,
        scratch_shapes=[
            pltpu.VMEM(act_grad.shape, F32),
            dma((2 * SLOTS,)), dma((3,)),
        ],
        compiler_params=pltpu.CompilerParams(vmem_limit_bytes=16 * 1024 * 1024),
        name="hand_over",
    )(coarse_out, fine_grad, coarse_grad, act_grad)


def solution(mesh):
    nb, ns = mesh.shape["blocks"], mesh.shape["sub"]
    split = P(("blocks", "sub"), None, None, None)
    return jax.shard_map(
        functools.partial(on_device, nb, ns),
        mesh=mesh,
        in_specs=(split, P(("blocks", "sub"), None), P(("blocks", "sub"), None), P(), P(), split),
        out_specs=(split, P(), P(), split),
        check_vma=False,
    )
```

```python
import functools

import jax
import jax.numpy as jnp
from jax import lax
from jax.experimental import pallas as pl
from jax.experimental.pallas import tpu as pltpu
from jax.sharding import PartitionSpec as P

BE = 16
C1 = 32
C2 = 64
SLOTS = 4
ROWS = BE * BE
MESH = pl.DeviceIdType.MESH
F32 = jnp.float32
BF16 = jnp.bfloat16


def iota(shape, dim):
    return lax.broadcasted_iota(jnp.int32, shape, dim)


def eye_matrix(size):
    return (iota((size, size), 0) == iota((size, size), 1)).astype(BF16)


def dot(a, b):
    return jnp.dot(a, b, preferred_element_type=F32)


def dot_t(a, b):
    return lax.dot_general(a, b, (((1,), (1,)), ((), ())), preferred_element_type=F32)


def shifted(cells, row, k):
    if k == 1:
        return cells
    sub = iota(cells.shape, 0)
    if k == 0:
        return jnp.where(sub == 0, row, pltpu.roll(cells, 1, 0))
    return jnp.where(sub == BE - 1, row, pltpu.roll(cells, BE - 1, 0))


def tiled_weight(row, width):
    per_tile = 128 // width
    groups = []
    sub = iota((8, 128), 0)
    lane = iota((8, 128), 1)
    for g in range(C1 // 8):
        first = g * 8 // per_tile
        picked = row[:, first * 128 : (first + 1) * 128]
        picked = jnp.broadcast_to(picked, (8, 128))
        for t in range(1, 8 // per_tile):
            tile = row[:, (first + t) * 128 : (first + t + 1) * 128]
            picked = jnp.where(sub // per_tile == t, tile, picked)
        groups.append(jnp.where(lane // width == sub % per_tile, picked, 0.0))
    tiled = jnp.concatenate(groups, axis=0)
    step = 64
    while step >= width:
        tiled = tiled + pltpu.roll(tiled, step, 1)
        step //= 2
    return tiled


def fold_taps(block, edge_low, edge_high, width):
    quarter = iota((width, 128), 1) // C1
    total = None
    for cls in range(4):
        part = None
        for z_out in (cls, cls + 4):
            rows = block[z_out * width : (z_out + 1) * width]
            tiles = [rows[:, :128], rows[:, 128:]]
            if z_out == 0:
                picked = jnp.where(quarter == 3, edge_low, tiles[0])
            elif z_out == 7:
                picked = jnp.where(quarter == 0, edge_high, tiles[1])
            elif z_out == 3:
                picked = jnp.where(quarter == 0, tiles[1], tiles[0])
            elif z_out == 4:
                picked = jnp.where(quarter == 3, tiles[0], tiles[1])
            else:
                picked = tiles[z_out // 4]
            part = picked if part is None else part + picked
        shift = (1 - cls) % 4 * C1
        if shift:
            part = pltpu.roll(part, shift, 1)
        total = part if total is None else total + part
    return jnp.where(quarter < 3, total, 0.0)


def body(
    nb, ns, nq, fine_rows, coarse_rows,
    coords, neigh, feat_hbm, fw_hbm, cw_hbm, cot_hbm,
    out_coarse, out_fine_grad, out_coarse_grad, out_act,
    feat, fw, cw, cot, hx, hc, hp, ps_ends, xp, ex, wf, wc, wce, wct, cp, ec, pg, up, acts, hid, gt, ct, ps, pool, pp, ep,
    folds, turned, sum_f, sum_c, red_f, red_c, got_f, got_c, mid_f, mid_c, all_f, all_c,
    halo_send, halo_recv, send_f, recv_f, send_c, recv_c, in_sem,
):
    loads = [
        pltpu.make_async_copy(src, dst, in_sem.at[i])
        for i, (src, dst) in enumerate(((fw_hbm, fw), (cw_hbm, cw), (cot_hbm, cot), (feat_hbm, feat)))
    ]
    for copy in loads:
        copy.start()

    i0 = lax.axis_index("blocks")
    i1 = lax.axis_index("sub")
    count = nb * ns
    me = i0 * ns + i1
    nxt = lax.rem(me + 1, count)
    prv = lax.rem(me + count - 1, count)
    prev_id = (prv // ns, lax.rem(prv, ns))
    next_id = (nxt // ns, lax.rem(nxt, ns))
    na = count // nq
    q = lax.rem(i0, nq)
    a = (i0 // nq) * ns + i1

    nz = nb // nq
    zs = [lax.rem(i0 // nq + k, nz) for k in range(nz)]
    ys = [lax.rem(i1 + k, ns) for k in range(ns)]
    blocks = [z * nq + q for z in zs]
    def way(k, size):
        return min(k, size - k)

    offsets = [(k, m) for k in range(nz) for m in range(ns) if k + m > 0]
    offsets.sort(key=lambda o: -way(o[0], nz) - way(o[1], ns))
    a_peers = [(zs[k] * ns + ys[m], (blocks[k], ys[m])) for k, m in offsets]
    nx = nq // 2
    xs = [lax.rem(q // 2 + k, nx) * 2 for k in range(nx)]
    cores = [lax.rem(q + k, 2) for k in range(2)]
    offsets = [(k, m) for k in range(nx) for m in range(2) if k + m > 0]
    offsets.sort(key=lambda o: -way(o[0], nx) - o[1])
    q_peers = [(i0 - q + xs[k] + cores[m], i1) for k, m in offsets]

    barrier = pltpu.get_barrier_semaphore()

    def greet(device):
        pl.semaphore_signal(barrier, inc=1, device_id=device, device_id_type=MESH)

    has_prev = me > 0
    has_next = me < count - 1
    pl.when(has_prev)(lambda: greet(prev_id))
    pl.when(has_next)(lambda: greet(next_id))
    for _, device in a_peers:
        greet(device)
    for device in q_peers:
        greet(device)

    def describe(src, dst, send, recv, device):
        return pltpu.make_async_remote_copy(
            src_ref=src, dst_ref=dst, send_sem=send, recv_sem=recv, device_id=device, device_id_type=MESH
        )

    def remote(src, dst, send, recv, device):
        describe(src, dst, send, recv, device).start()

    def swap(high, low, dst, k):
        up = describe(high, dst.at[0], halo_send.at[k], halo_recv.at[k], next_id)
        down = describe(low, dst.at[1], halo_send.at[k + 1], halo_recv.at[k + 1], prev_id)
        pl.when(has_next)(up.start)
        pl.when(has_prev)(down.start)

        def clear(side):
            dst[side] = jnp.zeros(dst.shape[1:], dst.dtype)

        def finish_swap():
            pl.when(has_prev)(up.wait_recv)
            pl.when(has_next)(down.wait_recv)
            pl.when(has_next)(up.wait_send)
            pl.when(has_prev)(down.wait_send)
            pl.when(jnp.logical_not(has_prev))(lambda: clear(0))
            pl.when(jnp.logical_not(has_next))(lambda: clear(1))

        return finish_swap

    loads[2].wait()
    loads[3].wait()
    pl.semaphore_wait(barrier, na + nq - 2 + has_prev.astype(jnp.int32) + has_next.astype(jnp.int32))
    end_swaps = [
        swap(feat.at[:, BE - 1], feat.at[:, 0], hx, 0),
        swap(cot.at[0, BE - 1], cot.at[0, 0], hc, 2),
    ]
    loads[0].wait()
    loads[1].wait()
    first = me * SLOTS
    quarter8 = iota((C1, 256), 1) // C1
    half8 = iota((C1, 512), 1) // C2
    half4 = iota((C1, 256), 1) // C2
    half2 = iota((C1, 128), 1) // C2
    zeros = jnp.zeros((2 * C1, 256), BF16)
    for dx in range(3):
        for dy in range(3):
            tap = dx * 3 + dy
            row_f = fw[dx, dy : dy + 1, :].astype(F32)
            tiles = []
            for dz in range(3):
                t = tiled_weight(row_f[:, dz * C1 * C1 : (dz + 1) * C1 * C1], C1)
                tiles.append(jnp.concatenate([t, t], axis=1))
            for z_in in range(8):
                line = jnp.where(quarter8 == z_in, tiles[1], 0.0)
                line = jnp.where(quarter8 == z_in + 1, tiles[0], line)
                line = jnp.where(quarter8 == z_in - 1, tiles[2], line)
                wf[tap * 256 + z_in * C1 : tap * 256 + (z_in + 1) * C1, :] = line.astype(BF16)
            base = 2304 + dx * 256
            high = base + (0, 64, 128)[dy]
            low = base + (96, 32, 224)[dy]
            wf[high : high + 32, :] = jnp.where(quarter8 == 7, tiles[2], 0.0).astype(BF16)
            wf[low : low + 32, :] = jnp.where(quarter8 == 0, tiles[0], 0.0).astype(BF16)
            if dy == 2:
                wf[base + 160 : base + 224, :] = zeros

            row_c = cw[dx, dy : dy + 1, :].astype(F32)
            narrow = [
                tiled_weight(row_c[:, dz * C1 * C2 : (dz + 1) * C1 * C2], C2) for dz in range(3)
            ]
            wide = [jnp.concatenate([t] * 4, axis=1) for t in narrow]
            for z_in in range(8):
                line = jnp.where(half8 == z_in, wide[1], 0.0)
                line = jnp.where(half8 == z_in + 1, wide[0], line)
                line = jnp.where(half8 == z_in - 1, wide[2], line)
                wc[tap, z_in * C1 : (z_in + 1) * C1, :] = line.astype(BF16)
            base = dx * 384 + dy * 128
            pair = [jnp.concatenate([t] * 2, axis=1) for t in narrow]
            wce[base : base + 32, :] = jnp.where(half4 == 1, pair[2], 0.0).astype(BF16)
            wce[base + 32 : base + 96, :] = zeros
            wce[base + 96 : base + 128, :] = jnp.where(half4 == 2, pair[0], 0.0).astype(BF16)
            base = (2 - dx) * 384 + (2 - dy) * 128
            wct[0:96, base : base + 128] = jnp.zeros((96, 128), BF16)
            wct[96:128, base : base + 128] = jnp.where(half2 == 0, narrow[0], 0.0).astype(BF16)
            wct[128:160, base : base + 128] = jnp.where(half2 == 1, narrow[2], 0.0).astype(BF16)
            wct[160:256, base : base + 128] = jnp.zeros((96, 128), BF16)

    eye = eye_matrix(256)

    flat_cot = cot[0].reshape(ROWS, BE * C2)
    for j in range(4):
        ct[j * 256 : (j + 1) * 256, :] = dot_t(eye, flat_cot[:, j * 256 : (j + 1) * 256]).astype(BF16)

    def put_cot(layer, cells):
        lane = iota((BE, 128), 1)
        zero = jnp.zeros((1, BE * C2), F32)
        for k in range(3):
            plane = shifted(cells, zero, k)
            cp[k, layer] = plane.astype(BF16)
            ec[layer, :, k * 128 : (k + 1) * 128] = jnp.where(
                lane < C2, plane[:, 512:640], plane[:, 384:512]
            ).astype(BF16)

    def cot_layer(x, _):
        put_cot(x + 1, cot[0, x].astype(F32))
        return 0

    for x in range(BE):
        cot_layer(x, 0)

    def put_cells(s, layer, cells, row_low, row_high, z_low, z_high):
        lane = iota((BE, 128), 1)
        zero = jnp.zeros((1, 128), F32)
        edges = ([], [])
        for k in range(3):
            plane = shifted(cells, (row_low, None, row_high)[k], k)
            xp[k, s, layer] = plane.astype(BF16)
            low = 0.0 if z_low is None else shifted(z_low, zero, k)
            high = 0.0 if z_high is None else shifted(z_high, zero, k)
            edges[0].append(jnp.where(lane < C1, plane[:, 256:384], low))
            edges[1].append(jnp.where(lane < C1, high, plane[:, 128:256]))
        for h in range(2):
            middle = pltpu.roll(edges[h][1], 64, 1)
            outer = (lane < C1) | (lane >= 3 * C1)
            ex[h, s, layer, :, 0:128] = jnp.where(outer, edges[h][0], middle).astype(BF16)
            ex[h, s, layer, :, 128:256] = edges[h][2].astype(BF16)

    def across(s, column):
        target = neigh[s, column]
        local = target - first
        return jnp.clip(local, 0, SLOTS - 1), local, (target >= 0).astype(F32)

    for s in range(SLOTS):
        ylow, _, ylow_on = across(s, 2)
        yhigh, _, yhigh_on = across(s, 3)
        zlow, _, zlow_on = across(s, 4)
        zhigh, _, zhigh_on = across(s, 5)

        def cell_layer(x, _):
            put_cells(
                s,
                x + 1,
                feat[s, x].astype(F32),
                feat[ylow, x].astype(F32)[BE - 1 : BE] * ylow_on,
                feat[yhigh, x].astype(F32)[0:1] * yhigh_on,
                feat[zlow, x, :, 384:512].astype(F32) * zlow_on,
                feat[zhigh, x, :, 0:128].astype(F32) * zhigh_on,
            )
            return 0

        for x in range(BE):
            cell_layer(x, 0)

    for finish_swap in end_swaps:
        finish_swap()

    put_cot(0, hc[0].astype(F32))
    put_cot(BE + 1, hc[1].astype(F32))
    for s in range(SLOTS):
        zero = jnp.zeros((1, BE * C1), F32)
        near, local, on = across(s, 0)
        inside = (local >= 0).astype(F32) * on
        outside = (local < 0).astype(F32) * on
        far = jnp.clip(local + SLOTS, 0, SLOTS - 1)
        plane = feat[near, BE - 1].astype(F32) * inside + hx[0, far].astype(F32) * outside
        put_cells(s, 0, plane, zero, zero, None, None)
        near, local, on = across(s, 1)
        inside = (local < SLOTS).astype(F32) * on
        outside = (local >= SLOTS).astype(F32) * on
        far = jnp.clip(local - SLOTS, 0, SLOTS - 1)
        plane = feat[near, 0].astype(F32) * inside + hx[1, far].astype(F32) * outside
        put_cells(s, BE + 1, plane, zero, zero, None, None)

    edge = jnp.concatenate([ec[k : k + BE].reshape(ROWS, 384) for k in range(3)], axis=1)
    from_edge = dot_t(edge, wct[...])
    for h in range(2):
        total = None
        for dx in range(3):
            for dy in range(3):
                window = cp[2 - dy, 2 - dx : 2 - dx + BE, :, h * 512 : (h + 1) * 512]
                term = dot_t(window.reshape(ROWS, 512), wc[dx * 3 + dy])
                total = term if total is None else total + term
        parts = [total[:, :128], total[:, 128:]]
        parts[1 - h] = parts[1 - h] + from_edge[:, h * 128 : (h + 1) * 128]
        for t in range(2):
            part = parts[t].reshape(2, 8, 2, 8, 128)
            for ox in range(2):
                for oy in range(2):
                    pg[ox * 4 + oy * 2 + h, :, :, t * 128 : (t + 1) * 128] = part[ox, :, oy]

    r = iota((256, 512), 0)
    l = iota((256, 512), 1)
    spread_z = ((l // 64 == r // 32) & (l % 32 == r % 32)).astype(BF16)
    r = iota((128, 64), 0)
    l = iota((128, 64), 1)
    spread_y = (r // 2 == l).astype(BF16)
    r = iota((64, 256), 0)
    l = iota((64, 256), 1)
    sum_xy = ((l // 32 == r // 8) & (l % 16 // 2 == r % 8)).astype(BF16)
    r = iota((256, 128), 0)
    l = iota((256, 128), 1)
    sum_z = ((r // 64 == l // 32) & (r % 32 == l % 32)).astype(F32)
    sum_z = (sum_z * 0.125).astype(BF16)

    grads = []
    for s in range(SLOTS):
        live = (coords[s, 0] >= 0).astype(F32)
        octant = lax.rem(coords[s, 0], 2) * 4 + coords[s, 1] * 2 + coords[s, 2]
        grads.append(pg[jnp.clip(octant, 0, 7)].reshape(64, 256) * (live * 0.125))
    grads = dot(jnp.concatenate(grads, axis=0).astype(BF16), spread_z).astype(BF16)
    for s in range(SLOTS):
        up[s] = dot(spread_y, grads[s * 64 : (s + 1) * 64]).reshape(8, BE, 512)

    def fine_act(s, _):
        for h in range(2):
            lanes = slice(h * 256, (h + 1) * 256)
            pieces = [
                xp[dy, s, dx : dx + BE, :, lanes].reshape(ROWS, 256)
                for dx in range(3)
                for dy in range(3)
            ]
            pieces += [ex[h, s, dx : dx + BE].reshape(ROWS, 256) for dx in range(3)]
            act = dot(jnp.concatenate(pieces, axis=1), wf[...])
            acts[s, :, :, lanes] = act.reshape(BE, BE, 256)
        return 0

    def fine_layer(i, _):
        s = i // BE
        x = lax.rem(i, BE)
        act = acts[s, x]
        sigma = 0.5 * jnp.tanh(0.5 * act) + 0.5
        gated = act * sigma
        hid[s, x] = (feat[s, x].astype(F32) + gated).astype(BF16)
        slope = sigma + gated * (1.0 - sigma)
        out_act[s, x] = (up[s, x // 2] * slope).astype(BF16)
        return 0

    for s in range(SLOTS + 1):
        if s < SLOTS:
            fine_act(s, 0)
        if s > 0:
            for x in range(BE):
                fine_layer((s - 1) * BE + x, 0)

    sums = jnp.concatenate([dot(sum_xy, hid[s].reshape(ROWS, 512)) for s in range(SLOTS)], axis=0)
    top = sums.astype(BF16)
    rest = (sums - top.astype(F32)).astype(BF16)
    for h in range(2):
        lanes = slice(h * 256, (h + 1) * 256)
        both = jnp.concatenate([top[:, lanes], rest[:, lanes]], axis=1)
        small = dot(both, jnp.concatenate([sum_z, sum_z], axis=0))
        ps[:, :, :, h * 128 : (h + 1) * 128] = small.reshape(SLOTS, 8, 8, 128)

    for t in range(8):
        slot = jnp.int32(0)
        on = jnp.int32(0)
        for s in range(SLOTS):
            octant = lax.rem(coords[s, 0], 2) * 4 + coords[s, 1] * 2 + coords[s, 2]
            here = ((coords[s, 0] >= 0) & (octant == t)).astype(jnp.int32)
            slot = slot + here * s
            on = on + here
        block = ps[jnp.clip(slot, 0, SLOTS - 1)] * on.astype(F32)
        ox, oy, oz = t // 4, t // 2 % 2, t % 2
        pool[ox * 8 : (ox + 1) * 8, oy * 8 : (oy + 1) * 8, oz * 256 : (oz + 1) * 256] = block
    ps_ends[0] = pool[0].astype(BF16)
    ps_ends[1] = pool[BE - 1].astype(BF16)
    end_pools = swap(ps_ends.at[1], ps_ends.at[0], hp, 4)

    def put_pool(layer, cells):
        lane = iota((BE, 128), 1)
        zero = jnp.zeros((1, BE * C1), F32)
        for k in range(3):
            plane = shifted(cells, zero, k)
            pp[k, layer] = plane.astype(BF16)
            ep[layer, :, k * 128 : (k + 1) * 128] = jnp.where(
                lane < C1, plane[:, 256:384], plane[:, 128:256]
            ).astype(BF16)

    def pool_layer(x, _):
        put_pool(x + 1, pool[x])
        return 0

    for x in range(BE):
        pool_layer(x, 0)

    eye = eye_matrix(256)
    for i in range(2 * SLOTS):
        lanes = slice(i % 2 * 256, i % 2 * 256 + 256)
        gt[i] = dot_t(eye, out_act[i // 2, :, :, lanes].reshape(ROWS, 256)).astype(BF16)
    eye = eye_matrix(128)

    def turn(sums, width):
        copies = 128 // width
        count = 3 * C1 // copies
        rows = [sums[tap * width : (tap + 1) * width, :] for tap in range(9) for _ in range(copies)]
        flipped = dot_t(eye, jnp.concatenate(rows, axis=0))
        for tap in range(9):
            turned[tap * 128 : (tap + 1) * 128, :] = flipped[:, tap * 128 : (tap + 1) * 128]
        lane = iota((count, 128), 1) // width
        lines = []
        for tap in range(9):
            base = tap * 128
            picked = turned[pl.ds(base, count, stride=copies), :]
            for t in range(1, copies):
                picked = jnp.where(lane == t, turned[pl.ds(base + t, count, stride=copies), :], picked)
            lines.append(picked)
        return lines

    def fine_taps(dx):
        left = jnp.concatenate([gt[i] for i in range(8)], axis=1)
        border = jnp.concatenate(
            [jnp.concatenate([gt[i, 0:32, :], gt[i, 224:256, :]], axis=0) for i in range(8)], axis=1
        )
        edges = jnp.concatenate(
            [ex[i % 2, i // 2, dx : dx + BE].reshape(ROWS, 256) for i in range(8)], axis=0
        )
        edge = dot(border, edges)
        edge = [edge[:, :128], pltpu.roll(edge[:, :128], 64, 1), edge[:, 128:]]
        for dy in range(3):
            right = jnp.concatenate(
                [
                    xp[dy, i // 2, dx : dx + BE, :, i % 2 * 256 : i % 2 * 256 + 256].reshape(ROWS, 256)
                    for i in range(8)
                ],
                axis=0,
            )
            folded = fold_taps(dot(left, right), edge[dy][:32], edge[dy][32:], C1)
            tap = dx * 3 + dy
            sum_f[tap * C1 : (tap + 1) * C1, :] = folded.astype(BF16)

    def coarse_taps(dx):
        left = jnp.concatenate([ct[0:512, :], ct[512:1024, :]], axis=1)
        edge = dot(ct[448:576, :], ep[dx : dx + BE].reshape(ROWS, 384))
        for dy in range(3):
            window = pp[dy, dx : dx + BE].reshape(ROWS, 512)
            right = jnp.concatenate([window[:, :256], window[:, 256:]], axis=0)
            lanes = slice(dy * 128, (dy + 1) * 128)
            folded = fold_taps(dot(left, right), edge[64:, lanes], edge[:64, lanes], C2)
            tap = dx * 3 + dy
            sum_c[tap * C2 : (tap + 1) * C2, :] = folded.astype(BF16)

    def all_of(ref, send, recv):
        return pltpu.make_async_remote_copy(
            src_ref=ref, dst_ref=ref, send_sem=send, recv_sem=recv, device_id=next_id, device_id_type=MESH
        )

    def shard(i, rows):
        return pl.ds(pl.multiple_of(i * rows, rows), rows)

    def spread(red, got, rows, send, recv):
        for j, (other, device) in enumerate(a_peers):
            remote(red.at[shard(other, rows)], got.at[j], send.at[0], recv.at[0], device)
        return all_of(got, send.at[0], recv.at[0])

    def exchange(copies, red, got, mid, rows, send, recv):
        copies.wait_recv()
        total = red[shard(a, rows), :].astype(F32)
        for j in range(na - 1):
            total = total + got[j].astype(F32)
        mid[q] = total.astype(BF16)
        for device in q_peers:
            remote(mid.at[q], mid.at[q], send.at[1], recv.at[1], device)
        return all_of(mid.at[0 : nq - 1], send.at[1], recv.at[1])

    def gather(copies, mid, full, rows, send, recv):
        copies.wait_recv()
        total = mid[0].astype(F32)
        for j in range(1, nq):
            total = total + mid[j].astype(F32)
        part = shard(a, rows)
        full[part, :] = total.astype(BF16)
        for _, device in a_peers:
            remote(full.at[part], full.at[part], send.at[2], recv.at[2], device)
        return all_of(full.at[0 : (na - 1) * rows], send.at[2], recv.at[2])

    def finish(copies, full, out, count):
        copies.wait_recv()
        folds[: 9 * count, :] = full[: 9 * count, :].astype(F32)
        for dx in range(3):
            for j in range(count):
                out[dx, :, j * 128 : (j + 1) * 128] = folds[pl.ds(dx * 3 * count + j, 3, stride=count), :]

    fine_taps(0)
    fine_taps(1)
    fine_taps(2)
    rows = turn(sum_f, C1) + [jnp.zeros((na * fine_rows - 216, 128), F32)]
    red_f[...] = jnp.concatenate(rows, axis=0).astype(BF16)
    end_pools()
    put_pool(0, hp[0].astype(F32))
    put_pool(BE + 1, hp[1].astype(F32))
    f1 = spread(red_f, got_f, fine_rows, send_f, recv_f)
    for dx in range(3):
        coarse_taps(dx)
    for tap, rows in enumerate(turn(sum_c, C2)):
        red_c[tap * 48 : (tap + 1) * 48, :] = rows.astype(BF16)
    if na * coarse_rows > 432:
        red_c[432:, :] = jnp.zeros((na * coarse_rows - 432, 128), BF16)
    c1 = spread(red_c, got_c, coarse_rows, send_c, recv_c)
    f2 = exchange(f1, red_f, got_f, mid_f, fine_rows, send_f, recv_f)
    edge = jnp.concatenate([ep[k : k + BE].reshape(ROWS, 384) for k in range(3)], axis=1)
    from_edge = dot(edge, wce[...])
    for h in range(2):
        pieces = [
            pp[dy, dx : dx + BE, :, h * 256 : (h + 1) * 256].reshape(ROWS, 256)
            for dx in range(3)
            for dy in range(3)
        ]
        total = dot(jnp.concatenate(pieces, axis=1), wc[...].reshape(9 * 256, 512))
        parts = [total[:, t * 128 : (t + 1) * 128] for t in range(4)]
        parts[3 if h == 0 else 0] += from_edge[:, h * 128 : (h + 1) * 128]
        for t in range(4):
            base = h * 512 + t * 128
            out_coarse[0, :, :, base : base + 128] = parts[t].astype(BF16).reshape(BE, BE, 128)
    c2 = exchange(c1, red_c, got_c, mid_c, coarse_rows, send_c, recv_c)
    f3 = gather(f2, mid_f, all_f, fine_rows, send_f, recv_f)
    c3 = gather(c2, mid_c, all_c, coarse_rows, send_c, recv_c)
    finish(f3, all_f, out_fine_grad, 24)
    finish(c3, all_c, out_coarse_grad, 48)
    for copy in (f1, f2, f3, c1, c2, c3):
        copy.wait_send()


def hand_over(
    scale, coarse, fine_grad, coarse_grad, act, out_coarse, out_fine_grad, out_coarse_grad, out_cell,
    wide, out_sem, other_sem,
):
    half = BE // 2
    cuts = [(s, slice(h * half, (h + 1) * half)) for s in range(SLOTS) for h in range(2)]
    outs = [pltpu.make_async_copy(wide.at[c], out_cell.at[c], out_sem.at[i]) for i, c in enumerate(cuts)]
    pairs = ((coarse, out_coarse), (fine_grad, out_fine_grad), (coarse_grad, out_coarse_grad))
    others = [pltpu.make_async_copy(b, c, other_sem.at[i]) for i, (b, c) in enumerate(pairs)]
    for i, cut in enumerate(cuts):
        wide[cut] = act[cut].astype(F32) * scale
        outs[i].start()
        if i == 0:
            for copy in others:
                copy.start()
    for copy in outs + others:
        copy.wait()


def on_device(nb, ns, features, coords, neighbours, fine_weight, coarse_weight, cotangent):
    nq = 8 if nb % 16 == 0 else min(nb, 2)
    na = nb * ns // nq
    fine_rows = -(-216 // (na * 16)) * 16
    coarse_rows = -(-432 // (na * 16)) * 16
    vmem = pl.BlockSpec(memory_space=pltpu.VMEM)
    smem = pl.BlockSpec(memory_space=pltpu.SMEM)
    hbm = pl.BlockSpec(memory_space=pl.ANY)
    dma = pltpu.SemaphoreType.DMA
    coarse_out, fine_grad, coarse_grad, act_grad = pl.pallas_call(
        functools.partial(body, nb, ns, nq, fine_rows, coarse_rows),
        out_shape=(
            pltpu.VMEM((1, BE, BE, BE * C2), BF16),
            pltpu.VMEM((3, 3, 3 * C1 * C1), F32),
            pltpu.VMEM((3, 3, 3 * C1 * C2), F32),
            pltpu.VMEM((SLOTS, BE, BE, BE * C1), BF16),
        ),
        in_specs=[smem, smem, hbm, hbm, hbm, hbm],
        out_specs=(vmem, vmem, vmem, vmem),
        scratch_shapes=[
            pltpu.VMEM((SLOTS, BE, BE, BE * C1), BF16),
            pltpu.VMEM((3, 3, 3 * C1 * C1), BF16),
            pltpu.VMEM((3, 3, 3 * C1 * C2), BF16),
            pltpu.VMEM((1, BE, BE, BE * C2), BF16),
            pltpu.VMEM((2, SLOTS, BE, BE * C1), BF16),
            pltpu.VMEM((2, BE, BE * C2), BF16),
            pltpu.VMEM((2, BE, BE * C1), BF16),
            pltpu.VMEM((2, BE, BE * C1), BF16),
            pltpu.VMEM((3, SLOTS, BE + 2, BE, BE * C1), BF16),
            pltpu.VMEM((2, SLOTS, BE + 2, BE, 256), BF16),
            pltpu.VMEM((12 * 256, 256), BF16),
            pltpu.VMEM((9, 256, 512), BF16),
            pltpu.VMEM((9 * 128, 256), BF16),
            pltpu.VMEM((256, 9 * 128), BF16),
            pltpu.VMEM((3, BE + 2, BE, BE * C2), BF16),
            pltpu.VMEM((BE + 2, BE, 384), BF16),
            pltpu.VMEM((8, 8, 8, 256), F32),
            pltpu.VMEM((SLOTS, 8, BE, 512), F32),
            pltpu.VMEM((SLOTS, BE, BE, 512), F32),
            pltpu.VMEM((SLOTS, BE, BE, 512), BF16),
            pltpu.VMEM((2 * SLOTS, 256, 256), BF16),
            pltpu.VMEM((BE * C2, ROWS), BF16),
            pltpu.VMEM((SLOTS, 8, 8, 256), F32),
            pltpu.VMEM((BE, BE, BE * C1), F32),
            pltpu.VMEM((3, BE + 2, BE, BE * C1), BF16),
            pltpu.VMEM((BE + 2, BE, 384), BF16),
            pltpu.VMEM((432, 128), F32),
            pltpu.VMEM((9 * 128, 128), F32),
            pltpu.VMEM((9 * C1, 128), BF16),
            pltpu.VMEM((9 * C2, 128), BF16),
            pltpu.VMEM((na * fine_rows, 128), BF16),
            pltpu.VMEM((na * coarse_rows, 128), BF16),
            pltpu.VMEM((na - 1, fine_rows, 128), BF16),
            pltpu.VMEM((na - 1, coarse_rows, 128), BF16),
            pltpu.VMEM((nq, fine_rows, 128), BF16),
            pltpu.VMEM((nq, coarse_rows, 128), BF16),
            pltpu.VMEM((na * fine_rows, 128), BF16),
            pltpu.VMEM((na * coarse_rows, 128), BF16),
            dma((6,)), dma((6,)),
            dma((3,)), dma((3,)), dma((3,)), dma((3,)), dma((4,)),
        ],
        compiler_params=pltpu.CompilerParams(
            collective_id=0, has_side_effects=True, vmem_limit_bytes=58 * 1024 * 1024
        ),
        name="unet_level",
    )(coords, neighbours, features, fine_weight, coarse_weight, cotangent)
    scale = float(nb * ns * BE**3) ** 0.5
    return pl.pallas_call(
        functools.partial(hand_over, scale),
        out_shape=(
            jax.ShapeDtypeStruct(coarse_out.shape, BF16),
            jax.ShapeDtypeStruct(fine_grad.shape, F32),
            jax.ShapeDtypeStruct(coarse_grad.shape, F32),
            jax.ShapeDtypeStruct(act_grad.shape, F32),
        ),
        in_specs=[vmem] * 4,
        out_specs=(hbm,) * 4,
        scratch_shapes=[
            pltpu.VMEM(act_grad.shape, F32),
            dma((2 * SLOTS,)), dma((3,)),
        ],
        compiler_params=pltpu.CompilerParams(vmem_limit_bytes=16 * 1024 * 1024),
        name="hand_over",
    )(coarse_out, fine_grad, coarse_grad, act_grad)


def solution(mesh):
    nb, ns = mesh.shape["blocks"], mesh.shape["sub"]
    split = P(("blocks", "sub"), None, None, None)
    return jax.shard_map(
        functools.partial(on_device, nb, ns),
        mesh=mesh,
        in_specs=(split, P(("blocks", "sub"), None), P(("blocks", "sub"), None), P(), P(), split),
        out_specs=(split, P(), P(), split),
        check_vma=False,
    )
```
